32 devices in a mesh: half: 2 (over core), wide: 8 (over z, x), narrow: 2 (over y).
Axes of the slice: x: 2, y: 2, z: 4, core: 2. Of those that a mesh axis runs over, the one named last changes fastest.
Arguments:
- stream: bfloat16 [2, 16, 1024, 512], P('half', ('wide', 'narrow')), may hold values from -6 to 6
- cotangent: bfloat16 [16, 1024, 512], P(('wide', 'narrow')), may hold values from -6 to 6
- lengths: int32 [2, 16], P(None, ('wide', 'narrow')), may hold values from 256 to 1024, as said below
- owners: int32 [2, 56], P('half'), may hold values from 0 to 7, as said below
- master: float32 [2, 112, 128, 512], P('half', 'wide', 'narrow'), as said below
- moment_one: float32 [2, 112, 128, 512], P('half', 'wide', 'narrow'), may hold values from -384 to 384
- moment_two: float32 [2, 112, 128, 512], P('half', 'wide', 'narrow'), may hold values from 4096 to 16384
- vec_master: float32 [15, 512], replicated
- vec_one: float32 [15, 512], replicated, may hold values from -384 to 384
- vec_two: float32 [15, 512], replicated, may hold values from 4096 to 16384
Outputs:
- out_stream: bfloat16 [2, 16, 1024, 512], P('half', ('wide', 'narrow'))
- grad_stream: float32 [2, 16, 1024, 512], P('half', ('wide', 'narrow'))
- new_moment_one: float32 [2, 112, 128, 512], P('half', 'wide', 'narrow')
- new_moment_two: float32 [2, 112, 128, 512], P('half', 'wide', 'narrow')
- new_master: float32 [2, 112, 128, 512], P('half', 'wide', 'narrow')
- new_copy: bfloat16 [2, 112, 128, 512], P('half', 'wide', 'narrow')
- new_vec_one: float32 [15, 512], replicated
- new_vec_two: float32 [15, 512], replicated
- new_vec_master: float32 [15, 512], replicated
The draws below stay inside these ranges and needn't reach their ends.
Inputs may be any that keep to these rules, and one draw needn't show every extreme that they name: `lengths`: positions at or past a document's length are padding. In each row some document has exactly 1024. `owners`: no index holds more than 14 pieces of a row; in each row one index holds exactly 14. `master`: slots that no piece maps to hold values that reach only their own update.
All inputs are finite; a program needn't handle non-finite values.
Results may differ from the reference program's by a relative error of at most 0.025.
The reference program's roundings to bfloat16 on the way count: a program that leaves them out, or rounds other values in their place, can miss the bound.
Values may be sent and summed in bfloat16 or wider, within the bound.
No kernel may reach another device: no remote copies, remote signals or barrier semaphores. Data moves between devices by JAX's collectives and lax.ppermute only.
A program may use at most 384 MiB of HBM per device.

```python
import math
import jax
import jax.numpy as jnp
from jax import lax

D = 512
FF = 2048
HEADS = 8
LEN = 1024
PIECE = 128
STEP = 5
ROWS = 16
PIECES = 56
CAP = 14
SLOTS = 112
N_WIDE = 8


def owner_table(key):
    tables = []
    for which_half in range(2):
        subkey = jax.random.fold_in(key, 101 + which_half)
        first_key, second_key, third_key = jax.random.split(subkey, 3)
        crowded = jax.random.randint(first_key, (), 0, SLOTS // CAP)
        shuffled = jax.random.permutation(second_key, SLOTS).astype(jnp.int32)
        slot_ids = jnp.arange(SLOTS).astype(jnp.int32)
        ranking = shuffled + SLOTS * (slot_ids // CAP == crowded).astype(jnp.int32)
        chosen = jnp.argsort(ranking)[:PIECES - CAP].astype(jnp.int32)
        picked = jnp.concatenate([crowded * CAP + jnp.arange(CAP).astype(jnp.int32), chosen])
        picked = jax.random.permutation(third_key, picked)
        tables.append(picked // CAP)
    return jnp.stack(tables).astype(jnp.int32)


def draw_owners(key, part):
    return owner_table(key)


def draw_master(key, part):
    owners = owner_table(key)
    key = jax.random.fold_in(key, 5)
    counter = jnp.arange(PIECES).astype(jnp.int32)
    same = owners[:, :, None] == owners[:, None, :]
    earlier = counter[None, None, :] < counter[None, :, None]
    ranks = jnp.sum((same & earlier).astype(jnp.int32), 2)
    slot_of = owners * CAP + ranks
    hit = slot_of[:, None, :] == jnp.arange(SLOTS).astype(jnp.int32)[None, :, None]
    pieces = jnp.sum(hit.astype(jnp.int32) * counter[None, None, :], 2)
    used = jnp.any(hit, 2)
    rows = pieces[:, :, None] * PIECE + jnp.arange(PIECE).astype(jnp.int32)[None, None, :]
    region = jnp.minimum(rows // D, 5)
    table = jnp.array([[1.4, 1.4, 1.0, 4.0, 1.4, 1.0], [1.4, 1.4, 1.0, 4.0, 1.4, 4.0]], jnp.float32)
    onehot = (region[..., None] == jnp.arange(6)).astype(jnp.float32)
    factor = jnp.sum(onehot * table[:, None, None, :], -1)
    factor = jnp.where(rows < 6 * D, factor, jnp.where(rows < 6 * D + FF, 1.0, 1.7 * math.sqrt(D / FF)))
    factor = jnp.where(used[:, :, None], factor, 1.0) / math.sqrt(D)
    noise = jax.random.normal(key, (2, SLOTS, PIECE, D), jnp.float32)
    return noise * factor[..., None]


def draw_lengths(key, part):
    key = jax.random.fold_in(key, 3)
    first_key, second_key = jax.random.split(key)
    base = jax.random.randint(first_key, (2, ROWS), LEN // 4, LEN + 1)
    longest = jax.random.randint(second_key, (2,), 0, ROWS)
    hit = jnp.arange(ROWS)[None, :] == longest[:, None]
    return jnp.where(hit, LEN, base).astype(jnp.int32)


def draw_vec_master(key, part):
    key = jax.random.fold_in(key, 9)
    first_key, second_key, third_key = jax.random.split(key, 3)
    row_kind = jnp.arange(15)[:, None] % 3
    weighs = jnp.exp(jax.random.uniform(first_key, (15, D), jnp.float32, 0.0, math.log(2.0)))
    gains = jax.random.uniform(second_key, (15, D), jnp.float32, 0.6, 1.4)
    shifts = 0.3 * jax.random.normal(third_key, (15, D), jnp.float32)
    return jnp.where(row_kind == 0, weighs, jnp.where(row_kind == 1, gains, shifts))


def block_scale(key, shape, cuts, low, largest):
    loudness = 1.0
    for position, blocks in cuts:
        draws = jax.random.uniform(jax.random.fold_in(jax.random.fold_in(key, 6), position), (blocks,), jnp.float32, low / len(cuts), largest / len(cuts))
        loudness = loudness * jnp.repeat(jnp.exp(draws), shape[position] // blocks).reshape((-1,) + (1,) * (len(shape) - 1 - position))
    return loudness


def centred(stream_key, extent, scale, most, cuts=(), held_as=jnp.bfloat16):
    level = block_scale(stream_key, extent, cuts, -0.22, 0.18) if cuts else 1.0
    values = jax.random.normal(stream_key, extent, jnp.float32) * scale * level
    return jnp.minimum(jnp.maximum(values, -most), most).astype(held_as)


def setup_inputs(seed: int = 0) -> dict:
    key_of = jax.random.split(jax.random.key(seed), 11)
    return {
        "stream": centred(key_of[0], (2, ROWS, LEN, D), 1.0, 6.0, ((0, 2), (1, 16))),
        "cotangent": centred(key_of[1], (ROWS, LEN, D), 1.0, 6.0, ((0, 16),)),
        "lengths": draw_lengths(jax.random.fold_in(key_of[10], 71), 0),
        "owners": draw_owners(jax.random.fold_in(key_of[10], 71), 0),
        "master": draw_master(jax.random.fold_in(key_of[10], 71), 0),
        "moment_one": centred(key_of[5], (2, SLOTS, PIECE, D), (0.5 * (ROWS * LEN) ** 0.5), 384.0, ((0, 2), (1, 8), (2, 2)), jnp.float32),
        "moment_two": jnp.clip(jnp.exp(math.log(16384.0) - 1.3862944 * jax.random.uniform(key_of[6], (2, SLOTS, PIECE, D), jnp.float32) ** block_scale(key_of[6], (2, SLOTS, PIECE, D), ((0, 2), (1, 8), (2, 2)), -0.2, 0.2)), 4096.0, 16384.0),
        "vec_master": draw_vec_master(jax.random.fold_in(key_of[10], 71), 0),
        "vec_one": centred(key_of[8], (15, D), (0.5 * (ROWS * LEN) ** 0.5), 384.0, (), jnp.float32),
        "vec_two": jnp.clip(jnp.exp(jax.random.uniform(key_of[9], (15, D), jnp.float32, math.log(4096.0), math.log(16384.0))), 4096.0, 16384.0),
    }


eps_norm = 1e-05
beta_one = 0.5
beta_two = 0.5
rate_matrix = 0.05
rate_vector = 0.3
decay_matrix = 0.01
eps_adam = 1e-08
highest = lax.Precision.HIGHEST

@jax.custom_vjp
def low(v):
    return lax.optimization_barrier(v.astype(jnp.bfloat16)).astype(jnp.float32)

@jax.custom_vjp
def low_back(v):
    return v

def low_keep(v):
    return (low(v), None)

def low_pass(kept, grad):
    return (grad,)

def back_keep(v):
    return (v, None)

def back_low(kept, grad):
    return (low(grad),)
low.defvjp(low_keep, low_pass)
low_back.defvjp(back_keep, back_low)

def matmul(left, right):
    return jnp.dot(left, right, precision=highest)

def layer_norm(resid, gain, shift):
    center = resid - lax.optimization_barrier(jnp.mean(resid, -1, keepdims=True))
    spread = lax.optimization_barrier(jnp.mean(center * center, -1, keepdims=True))
    return center * lax.rsqrt(spread + eps_norm) * gain + shift

def resid_norm(inner, weigh, branch, gain, shift):
    return layer_norm(inner * weigh + branch, gain, shift)

def smooth(pre_act):
    return jax.nn.gelu(pre_act, approximate=False)

def project(inputs, weight):
    return low(low_back(matmul(inputs, weight)))

def attend(queries, key_rows, value_rows, limit, causal):
    length = queries.shape[0]
    key_count = key_rows.shape[0]
    query_heads = queries.reshape(length, HEADS, -1)
    key_heads = key_rows.reshape(key_count, HEADS, -1)
    value_heads = value_rows.reshape(key_count, HEADS, -1)
    raw_scores = jnp.einsum('qhe,khe->hqk', query_heads, key_heads, precision=highest) / math.sqrt(query_heads.shape[-1])
    columns = jnp.arange(key_count)
    allowed = columns[None, :] < limit
    if causal:
        allowed = allowed & (columns[None, :] <= jnp.arange(length)[:, None])
    scores = low_back(jnp.where(allowed[None], raw_scores, -1e+30))
    weights = low(jax.nn.softmax(scores, axis=-1))
    context = jnp.einsum('hqk,khe->qhe', weights, value_heads, precision=highest).reshape(length, -1)
    return low(low_back(context))

def split_rows(weight):
    model_width = weight.shape[1]
    hidden = (weight.shape[0] - 6 * model_width) // 2
    parts = [weight[number * model_width:(number + 1) * model_width] for number in range(6)]
    parts.append(weight[6 * model_width:6 * model_width + hidden])
    parts.append(weight[6 * model_width + hidden:])
    return parts

def feed_forward(inner, vector, first, up_rows, down_rows):
    pre_act = low_back(matmul(low(inner), up_rows.T))
    branch = low_back(matmul(low(smooth(pre_act)), down_rows))
    return resid_norm(inner, vector[first], branch, vector[first + 1], vector[first + 2])

def pair(source, target, cotan, source_len, target_len, enc_weight, dec_weight, vector):
    enc_parts = split_rows(enc_weight)
    dec_parts = split_rows(dec_weight)
    context = attend(project(source, enc_parts[0]), project(source, enc_parts[1]), project(source, enc_parts[2]), source_len, False)
    inner = resid_norm(source, vector[0], low_back(matmul(context, enc_parts[3])), vector[1], vector[2])
    memory = low(feed_forward(inner, vector, 3, enc_parts[6], enc_parts[7]))
    mem_keys = project(memory, enc_parts[4])
    mem_values = project(memory, enc_parts[5])
    self_ctx = attend(project(target, dec_parts[0]), project(target, dec_parts[1]), project(target, dec_parts[2]), target_len, True)
    inner_one = resid_norm(target, vector[6], low_back(matmul(self_ctx, dec_parts[3])), vector[7], vector[8])
    cross_query = project(low(inner_one), dec_parts[4])
    cross_ctx = attend(cross_query, mem_keys, mem_values, source_len, False)
    inner_two = resid_norm(inner_one, vector[9], low_back(matmul(cross_ctx, dec_parts[5])), vector[10], vector[11])
    output = feed_forward(inner_two, vector, 12, dec_parts[6], dec_parts[7])
    valid = (jnp.arange(output.shape[0]) < target_len).astype(jnp.float32)
    loss = jnp.sum(output * cotan * valid[:, None])
    return (loss, (memory, output))

def slot_pieces(owner_row, capacity, slot_count):
    count = owner_row.shape[0]
    counter = jnp.arange(count).astype(jnp.int32)
    same = owner_row[:, None] == owner_row[None, :]
    earlier = counter[None, :] < counter[:, None]
    ranks = lax.optimization_barrier(jnp.sum((same & earlier).astype(jnp.int32), 1)).astype(jnp.int32)
    slot_of = (owner_row * capacity + ranks).astype(jnp.int32)
    hit = slot_of[None, :] == jnp.arange(slot_count).astype(jnp.int32)[:, None]
    piece = lax.optimization_barrier(jnp.sum(hit.astype(jnp.int32) * counter[None, :], 1)).astype(jnp.int32)
    used = jnp.any(hit, 1)
    return (slot_of, piece, used)

def adam(weight, gradient, first, second, step_rate, decay_rate):
    first_new = beta_one * first + (1.0 - beta_one) * gradient
    second_new = beta_two * second + (1.0 - beta_two) * gradient * gradient
    first_hat = first_new / (1.0 - beta_one ** STEP)
    second_hat = second_new / (1.0 - beta_two ** STEP)
    weight_new = weight - step_rate * (first_hat / (jnp.sqrt(second_hat) + eps_adam) + decay_rate * weight)
    return (weight_new, first_new, second_new)

def reference(stream, cotangent, lengths, owners, master, moment_one, moment_two, vec_master, vec_one, vec_two):
    slot_count = master.shape[1]
    capacity = slot_count // N_WIDE
    piece_rows = master.shape[2]
    model_width = master.shape[3]
    weights = []
    tables = []
    for group in range(2):
        slot_of, piece, used = slot_pieces(owners[group], capacity, slot_count)
        rounded = master[group].astype(jnp.bfloat16).astype(jnp.float32)
        weights.append(rounded[slot_of].reshape(-1, model_width))
        tables.append((piece, used))
    sources = stream[0].astype(jnp.float32)
    targets = stream[1].astype(jnp.float32)
    cotan = cotangent.astype(jnp.float32)

    def forward(sources, targets, enc_weight, dec_weight, vector):

        def scan_step(running, member):
            loss, outs = jax.checkpoint(pair)(member[0], member[1], member[2], member[3], member[4], enc_weight, dec_weight, vector)
            return (running + loss, outs)
        running, outs = lax.scan(scan_step, jnp.zeros((), jnp.float32), (sources, targets, cotan, lengths[0], lengths[1]))
        return (running, outs)
    running, backward, outs = jax.vjp(forward, sources, targets, weights[0], weights[1], vec_master, has_aux=True)
    grad_src, grad_tgt, grad_enc, grad_dec, grad_vec = backward(jnp.ones((), jnp.float32))
    news = []
    for group, gradient in enumerate((grad_enc, grad_dec)):
        piece, used = tables[group]
        pieces = gradient.reshape(-1, piece_rows, model_width)
        slot_grad = pieces[piece] * used.astype(jnp.float32)[:, None, None]
        news.append(adam(master[group], slot_grad, moment_one[group], moment_two[group], rate_matrix, decay_matrix))
    vec_new, vec_first, vec_second = adam(vec_master, grad_vec, vec_one, vec_two, rate_vector, 0.0)
    new_master = jnp.stack([news[0][0], news[1][0]])
    out_stream = jnp.stack([outs[0], outs[1]]).astype(jnp.bfloat16)
    return (out_stream, jnp.stack([grad_src, grad_tgt]), jnp.stack([news[0][1], news[1][1]]), jnp.stack([news[0][2], news[1][2]]), new_master, new_master.astype(jnp.bfloat16), vec_first, vec_second, vec_new)
```

```python
import math
from functools import partial

import jax
import jax.numpy as jnp
from jax import lax
from jax.experimental import pallas as pl
from jax.experimental.pallas import tpu as pltpu
from jax.sharding import PartitionSpec as P

HEADS = 8
STEP = 5
QB = 256
RB = 256
NEG = -1e30

eps_norm = 1e-05
beta_one = 0.5
beta_two = 0.5
rate_matrix = 0.05
rate_vector = 0.3
decay_matrix = 0.01
eps_adam = 1e-08
bfloat = jnp.bfloat16
single = jnp.float32
VM = pl.BlockSpec(memory_space=pltpu.VMEM)
SM = pl.BlockSpec(memory_space=pltpu.SMEM)
HB = pl.BlockSpec(memory_space=pl.ANY)


def mm(left, right):
    return jnp.dot(left, right, preferred_element_type=single)


def mm_tn(left, right):
    return lax.dot_general(left, right, (((0,), (0,)), ((), ())), preferred_element_type=single)


def mm_nt(left, right):
    return lax.dot_general(left, right, (((1,), (1,)), ((), ())), preferred_element_type=single)


def block_of(index, size):
    return pl.ds(pl.multiple_of(index * size, size), size)


def normed(resid):
    center = resid - jnp.mean(resid, -1, keepdims=True)
    spread = jnp.mean(center * center, -1, keepdims=True)
    rstd = lax.rsqrt(spread + eps_norm)
    return center * rstd, rstd


def norm_back(resid, grad, gain):
    hat, rstd = normed(resid)
    grad_hat = grad * gain
    grad_resid = rstd * (
        grad_hat
        - jnp.mean(grad_hat, -1, keepdims=True)
        - hat * jnp.mean(grad_hat * hat, -1, keepdims=True)
    )
    return grad_resid, jnp.sum(grad * hat, 0, keepdims=True), jnp.sum(grad, 0, keepdims=True)


def gelu_parts(pre_act):
    half = 0.5 * (1.0 + lax.erf(pre_act * math.sqrt(0.5)))
    slope = half + pre_act * (jnp.exp(-0.5 * pre_act * pre_act) * (1.0 / math.sqrt(2.0 * math.pi)))
    return pre_act * half, slope


def pair_keys(tile, first_extra, ones):
    rows = tile.shape[0]
    lane = lax.broadcasted_iota(jnp.int32, (rows, 128), 1)
    wide_tile = tile.astype(single)
    out = []
    for head in range(2):
        at = lane - (64 - 64 * head)
        extra = jnp.where(at == 0, first_extra, jnp.where((at > 0) & (at < ones), 1.0, 0.0))
        mine = (lane < 64) if head == 0 else (lane >= 64)
        out.append(jnp.where(mine, wide_tile, extra).astype(bfloat))
    return out


def pair_queries(tile, head, extra_rows):
    mine = tile[64 * head : 64 * head + 64]
    row = lax.broadcasted_iota(jnp.int32, mine.shape, 0)
    extra = jnp.zeros(mine.shape, single)
    for number, value in enumerate(extra_rows):
        extra = jnp.where(row == number, value, extra)
    extra = extra.astype(bfloat)
    return jnp.concatenate([mine, extra] if head == 0 else [extra, mine], 0)


def split_three(value):
    high = value.astype(bfloat).astype(single)
    rest = value - high
    middle = rest.astype(bfloat).astype(single)
    return [high, middle, rest - middle]


def key_bias(limit, rows):
    row = lax.broadcasted_iota(jnp.int32, (rows, 128), 0)
    return jnp.where(row < limit, 0.0, NEG)


def score_parts(scores, diagonal):
    if not diagonal:
        return [scores]
    size = scores.shape[1]
    cut = scores.shape[0] - size
    row = lax.broadcasted_iota(jnp.int32, (size, size), 0)
    column = lax.broadcasted_iota(jnp.int32, (size, size), 1)
    last = jnp.where(row <= column, scores[cut:], NEG)
    return [scores[:cut], last] if cut else [last]


def over_blocks(causal, length, body):
    @pl.when(causal == 0)
    def _():
        def step(index, unused):
            body(index, length, False)
            return 0

        lax.fori_loop(0, length // QB, step, 0)

    @pl.when(causal != 0)
    def _():
        for index in range(length // QB):
            body(index, (index + 1) * QB, True)


def attend(limit, causal, key_ref, query_t, value_t, ctx_t, lse_ref, key_two):
    length, width = key_ref.shape
    bias = key_bias(limit, length)

    def pair(number, unused):
        columns = block_of(number, 128)
        for head, tile in enumerate(pair_keys(key_ref[:, columns], bias, 1)):
            key_two[head] = tile

        def body(index, extent, diagonal):
            at = block_of(index, QB)
            tile = query_t[columns, at]
            for head in range(2):
                mine = pl.ds(pl.multiple_of(number * 128 + 64 * head, 64), 64)
                scores = mm(key_two[head, :extent], pair_queries(tile, head, [1.0]))
                parts = score_parts(scores, diagonal)
                top = jnp.max(parts[0], 0, keepdims=True)
                for part in parts[1:]:
                    top = jnp.maximum(top, jnp.max(part, 0, keepdims=True))
                parts = [jnp.exp(part - top) for part in parts]
                total = sum(jnp.sum(part, 0, keepdims=True) for part in parts)
                weights = jnp.concatenate([part.astype(bfloat) for part in parts], 0)
                context = mm(value_t[mine, :extent], weights)
                ctx_t[mine, at] = (context * (1.0 / total)).astype(bfloat)
                lse_ref[pl.ds(number * 2 + head, 1), at] = top + jnp.log(total)

        over_blocks(causal, length, body)
        return 0

    lax.fori_loop(0, width // 128, pair, 0)


def attend_back(
    limit, causal, query_ref, key_ref, value_ref, query_t, key_t, grad_ctx, grad_ctx_t, lse_ref, dot_ref,
    grad_key, grad_value, grad_query_t, key_two, value_two,
):
    length, width = key_ref.shape
    bias = key_bias(limit, length)
    grad_key[...] = jnp.zeros(grad_key.shape, single)
    grad_value[...] = jnp.zeros(grad_value.shape, single)

    def pair(number, unused):
        columns = block_of(number, 128)
        for head, tile in enumerate(pair_keys(key_ref[:, columns], bias, 4)):
            key_two[head] = tile
        for head, tile in enumerate(pair_keys(value_ref[:, columns], 1.0, 3)):
            value_two[head] = tile

        def body(index, extent, diagonal):
            at = block_of(index, QB)
            query_tile = query_t[columns, at]
            ctx_tile = grad_ctx_t[columns, at]
            all_weights, all_grads = [], []
            for head in range(2):
                mine = pl.ds(pl.multiple_of(number * 128 + 64 * head, 64), 64)
                row = pl.ds(number * 2 + head, 1)
                minus_lse = split_three(-lse_ref[row, at])
                scores = mm(
                    key_two[head, :extent], pair_queries(query_tile, head, [1.0] + minus_lse)
                )
                weights = [jnp.exp(part) for part in score_parts(scores, diagonal)]
                weights = jnp.concatenate(weights, 0)
                minus_dot = split_three(-dot_ref[row, at])
                grad_weights = mm(value_two[head, :extent], pair_queries(ctx_tile, head, minus_dot))
                grads = (weights * grad_weights).astype(bfloat)
                all_weights.append(weights.astype(bfloat))
                all_grads.append(grads)
                grad_query = mm(key_t[mine, :extent], grads)
                grad_query_t[mine, at] = (grad_query * 0.125).astype(bfloat)
            lane = lax.broadcasted_iota(jnp.int32, (QB, 128), 1)

            def both(tile):
                tile = tile.astype(single)
                return jnp.concatenate(
                    [
                        jnp.where(lane < 64, tile, 0.0).astype(bfloat),
                        jnp.where(lane < 64, 0.0, tile).astype(bfloat),
                    ],
                    0,
                )

            grad_value[:extent, columns] += mm(
                jnp.concatenate(all_weights, 1), both(grad_ctx[at, columns])
            )
            grad_key[:extent, columns] += mm(
                jnp.concatenate(all_grads, 1), both(query_ref[at, columns])
            )

        over_blocks(causal, length, body)
        return 0

    lax.fori_loop(0, width // 128, pair, 0)


def by_rows(length, body, init=0):
    def step(index, carry):
        return body(block_of(index, RB), carry)

    return lax.fori_loop(0, length // RB, step, init)


class Emitter:
    def __init__(self, table, target, stage, semaphores):
        self.table, self.target, self.stage, self.semaphores = table, target, stage, semaphores
        self.copies = []

    def chunk(self, number, first_piece, value):
        stage, half_rows = self.stage, self.target.shape[1]
        stage[number] = value.astype(bfloat)
        count = stage.shape[1] // half_rows
        per_piece = 128 // half_rows
        for part in range(count):
            copy = pltpu.make_async_copy(
                stage.at[number, pl.ds(part * half_rows, half_rows)],
                self.target.at[self.table[first_piece * per_piece + part]],
                self.semaphores.at[number * count + part],
            )
            copy.start()
            self.copies.append(copy)

    def wait(self):
        for copy in self.copies:
            copy.wait()


def zero_rows(width):
    return (jnp.zeros((1, width), single),) * 3


def put_rows(ref, rows):
    for number, row in enumerate(rows):
        ref[number : number + 1] = row


def project_norm(length, ctx_t, weight, inner_ref, vec, resid_ref, out_ref):
    def body(rows, carry):
        branch = mm(ctx_t[:, rows].T, weight[...])
        resid = inner_ref[rows].astype(single) * vec[0:1] + branch
        resid_ref[rows] = resid
        out_ref[rows] = normed(resid)[0] * vec[1:2] + vec[2:3]
        return carry

    by_rows(length, body)


def self_forward_kernel(
    scal, x, weight, vec, query, key, value, ctx_t, lse, resid, out, query_t, value_t, key_two
):
    length, width = x.shape

    def body(rows, carry):
        tile = x[rows]
        for number, ref in enumerate((query, key, value)):
            ref[rows] = mm(tile, weight[width * number : width * (number + 1)]).astype(bfloat)
        query_t[:, rows] = (query[rows] * bfloat(0.125)).T
        value_t[:, rows] = value[rows].T
        return carry

    by_rows(length, body)
    attend(scal[0], scal[1], key, query_t, value_t, ctx_t, lse, key_two)
    project_norm(length, ctx_t, weight.at[3 * width :], x, vec, resid, out)


def encoder_ff_kernel(
    scal, inner, up, down, cross, vec, activ, slope, resid, memory, sendout
):
    length, width = inner.shape

    @pl.when(scal[2] != 0)
    def _():
        def body(rows, carry):
            tile = inner[rows]
            act, grad = gelu_parts(mm_nt(tile.astype(bfloat), up[...]))
            act = act.astype(bfloat)
            activ[rows] = act
            slope[rows] = grad.astype(bfloat)
            total = tile * vec[0:1] + mm(act, down[...])
            resid[rows] = total
            mem = (normed(total)[0] * vec[1:2] + vec[2:3]).astype(bfloat)
            memory[rows] = mem
            sendout[0, rows] = mm(mem, cross[:width]).astype(bfloat)
            sendout[1, rows] = mm(mem, cross[width:]).astype(bfloat)
            return carry

        by_rows(length, body)


def cross_forward_kernel(
    scal, inner, keys, cross, vec, query, ctx_t, lse, resid, out, query_t, value_t, key_two
):
    length, width = inner.shape

    @pl.when(scal[2] == 0)
    def _():
        def body(rows, carry):
            query[rows] = mm(inner[rows].astype(bfloat), cross[:width]).astype(bfloat)
            query_t[:, rows] = (query[rows] * bfloat(0.125)).T
            value_t[:, rows] = keys[1, rows].T
            return carry

        by_rows(length, body)
        attend(scal[0], scal[1], keys.at[0], query_t, value_t, ctx_t, lse, key_two)
        project_norm(length, ctx_t, cross.at[width:], inner, vec, resid, out)


def ff_back(length, emit, grad_branch, activ, slope, inner_low, up, down, grad_inner):
    def body(rows, carry):
        grad = mm_nt(grad_branch[rows], down[...]) * slope[rows].astype(single)
        grad = grad.astype(bfloat)
        slope[rows] = grad
        grad_inner[rows] += mm(grad, up[...])
        return carry

    by_rows(length, body)
    for number in range(activ.shape[1] // 512):
        columns = slice(number * 512, (number + 1) * 512)
        emit.chunk(2 * number, 24 + 4 * number, mm_tn(slope[:, columns], inner_low[...]))
        emit.chunk(2 * number + 1, 40 + 4 * number, mm_tn(activ[:, columns], grad_branch[...]))


def decoder_ff_kernel(
    scal, table, inner, up, down, vec, cotan, out, grad_inner, grad_vec, target,
    activ, slope, inner_low, grad_branch, stage, semaphores,
):
    length, width = inner.shape

    @pl.when(scal[2] == 0)
    def _():
        def body(rows, carry):
            tile = inner[rows]
            low = tile.astype(bfloat)
            inner_low[rows] = low
            act, grad = gelu_parts(mm_nt(low, up[...]))
            act = act.astype(bfloat)
            activ[rows] = act
            slope[rows] = grad.astype(bfloat)
            total = tile * vec[0:1] + mm(act, down[...])
            out[rows] = (normed(total)[0] * vec[1:2] + vec[2:3]).astype(bfloat)
            row = lax.broadcasted_iota(jnp.int32, tile.shape, 0) + rows.start
            grad_out = jnp.where(row < scal[3], cotan[rows].astype(single), 0.0)
            grad_resid, grad_gain, grad_shift = norm_back(total, grad_out, vec[1:2])
            grad_branch[rows] = grad_resid.astype(bfloat)
            grad_inner[rows] = grad_resid * vec[0:1]
            weigh = jnp.sum(grad_resid * tile, 0, keepdims=True)
            return (carry[0] + weigh, carry[1] + grad_gain, carry[2] + grad_shift)

        put_rows(grad_vec, by_rows(length, body, zero_rows(width)))
        emit = Emitter(table, target, stage, semaphores)
        ff_back(length, emit, grad_branch, activ, slope, inner_low, up, down, grad_inner)
        emit.wait()


def branch_back(length, resid, grad_out, inner, vec, grad_branch, grad_inner, grad_vec):
    width = resid.shape[1]

    def body(rows, carry):
        grad_resid, grad_gain, grad_shift = norm_back(resid[rows], grad_out[rows], vec[1:2])
        grad_branch[rows] = grad_resid.astype(bfloat)
        grad_inner[rows] = grad_resid * vec[0:1]
        weigh = jnp.sum(grad_resid * inner[rows].astype(single), 0, keepdims=True)
        return (carry[0] + weigh, carry[1] + grad_gain, carry[2] + grad_shift)

    put_rows(grad_vec, by_rows(length, body, zero_rows(width)))


def ctx_back(length, grad_branch, weight, ctx_t, grad_ctx, grad_ctx_t, dot_ref):
    def body(rows, carry):
        grad_ctx[rows] = mm_nt(grad_branch[rows], weight[...]).astype(bfloat)
        grad_ctx_t[:, rows] = grad_ctx[rows].T
        for head in range(HEADS):
            mine = slice(64 * head, 64 * head + 64)
            product = grad_ctx_t[mine, rows].astype(single) * ctx_t[mine, rows].astype(single)
            dot_ref[head : head + 1, rows] = jnp.sum(product, 0, keepdims=True)
        return carry

    by_rows(length, body)


def cross_back_kernel(
    scal, table, inner, resid, query, keys, ctx_t, lse, cross, vec, grad_out, held,
    sendback, grad_inner, grad_vec, target,
    grad_branch, grad_ctx, grad_ctx_t, dot_ref, query_t, key_t, grad_key, grad_value, grad_query_t,
    key_two, value_two, stage, semaphores,
):
    length, width = inner.shape

    @pl.when(scal[2] == 0)
    def _():
        emit = Emitter(table, target, stage, semaphores)
        branch_back(length, resid, grad_out, inner, vec, grad_branch, grad_inner, grad_vec)
        emit.chunk(1, 20, mm(ctx_t[...], grad_branch[...]))
        ctx_back(length, grad_branch, cross.at[width:], ctx_t, grad_ctx, grad_ctx_t, dot_ref)

        def body(rows, carry):
            query_t[:, rows] = (query[rows] * bfloat(0.125)).T
            key_t[:, rows] = keys[0, rows].T
            return carry

        by_rows(length, body)
        attend_back(
            scal[0], scal[1], query, keys.at[0], keys.at[1], query_t, key_t, grad_ctx, grad_ctx_t, lse, dot_ref,
            grad_key, grad_value, grad_query_t, key_two, value_two,
        )

        def last(rows, carry):
            sendback[0, rows] = (grad_key[rows] * 0.125).astype(bfloat)
            sendback[1, rows] = grad_value[rows].astype(bfloat)
            grad_query = grad_query_t[:, rows].T
            grad_inner[rows] += mm_nt(grad_query, cross[:width])
            grad_ctx[rows] = grad_query
            return carry

        by_rows(length, last)
        emit.chunk(0, 16, mm_tn(inner[...].astype(bfloat), grad_ctx[...]))
        emit.wait()


def encoder_back_kernel(
    scal, table, received, memory, cross, inner, resid, activ, slope, up, down, vec, held,
    grad_inner, grad_vec, target,
    grad_mem, inner_low, grad_branch, stage, semaphores,
):
    length, width = inner.shape

    @pl.when(scal[2] != 0)
    def _():
        emit = Emitter(table, target, stage, semaphores)

        def body(rows, carry):
            grad_mem[rows] = mm_nt(received[0, rows], cross[:width]) + mm_nt(
                received[1, rows], cross[width:]
            )
            inner_low[rows] = inner[rows].astype(bfloat)
            return carry

        by_rows(length, body)
        branch_back(length, resid, grad_mem, inner, vec, grad_branch, grad_inner, grad_vec)
        ff_back(length, emit, grad_branch, activ, slope, inner_low, up, down, grad_inner)
        emit.chunk(8, 16, mm_tn(memory[...], received[0]))
        emit.chunk(9, 20, mm_tn(memory[...], received[1]))
        emit.wait()


def self_back_kernel(
    scal, table, x, weight, vec, resid, query, key, value, ctx_t, lse, grad_out, held,
    grad_x, grad_vec, target,
    grad_branch, grad_ctx, grad_ctx_t, dot_ref, query_t, key_t, grad_key, grad_value, grad_query_t,
    key_two, value_two, stage, semaphores,
):
    length, width = x.shape
    emit = Emitter(table, target, stage, semaphores)
    branch_back(length, resid, grad_out, x, vec, grad_branch, grad_x, grad_vec)
    emit.chunk(3, 12, mm(ctx_t[...], grad_branch[...]))
    ctx_back(length, grad_branch, weight.at[3 * width :], ctx_t, grad_ctx, grad_ctx_t, dot_ref)

    def body(rows, carry):
        query_t[:, rows] = (query[rows] * bfloat(0.125)).T
        key_t[:, rows] = key[rows].T
        return carry

    by_rows(length, body)
    attend_back(
        scal[0], scal[1], query, key, value, query_t, key_t, grad_ctx, grad_ctx_t, lse, dot_ref,
        grad_key, grad_value, grad_query_t, key_two, value_two,
    )

    def last(rows, carry):
        parts = (
            grad_query_t[:, rows].T,
            (grad_key[rows] * 0.125).astype(bfloat),
            grad_value[rows].astype(bfloat),
        )
        total = grad_x[rows]
        for number, part in enumerate(parts):
            total += mm_nt(part, weight[width * number : width * (number + 1)])
        grad_x[rows] = total
        grad_branch[rows] = parts[0]
        grad_ctx[rows] = parts[1]
        return carry

    by_rows(length, last)
    emit.chunk(0, 0, mm_tn(x[...], grad_branch[...]))
    emit.chunk(1, 4, mm_tn(x[...], grad_ctx[...]))
    emit.chunk(2, 8, mm_tn(x[...], grad_value[...].astype(bfloat)))
    emit.wait()


def call(kernel, ins, outs, scratch, name, aliases=None):
    specs = [spec for spec, unused in ins]
    return pl.pallas_call(
        kernel,
        in_specs=specs,
        out_specs=[spec for spec, unused in outs],
        out_shape=[shape for unused, shape in outs],
        scratch_shapes=scratch,
        input_output_aliases=aliases or {},
        compiler_params=pltpu.CompilerParams(vmem_limit_bytes=58 << 20),
        name=name,
    )(*[value for unused, value in ins])


def shaped(*shape, dtype=single):
    return jax.ShapeDtypeStruct(shape, dtype)


def low(*shape):
    return jax.ShapeDtypeStruct(shape, bfloat)


def low_vm(*shape):
    return pltpu.VMEM(shape, bfloat)


def full_vm(*shape):
    return pltpu.VMEM(shape, single)


def adam(weight, gradient, first, second, step_rate, decay_rate):
    first_new = beta_one * first + (1.0 - beta_one) * gradient
    second_new = beta_two * second + (1.0 - beta_two) * gradient * gradient
    first_hat = first_new / (1.0 - beta_one**STEP)
    second_hat = second_new / (1.0 - beta_two**STEP)
    weight_new = weight - step_rate * (
        first_hat / (jnp.sqrt(second_hat) + eps_adam) + decay_rate * weight
    )
    return (weight_new, first_new, second_new)


def on_device(
    stream, cotangent, lengths, owners, master, moment_one, moment_two, vec_master, vec_one, vec_two
):
    narrow_size = lax.axis_size("narrow")
    wide_size = lax.axis_size("wide")
    owner_row = owners[0]
    capacity = master.shape[1]
    half_rows = master.shape[2]
    width = master.shape[3]
    count = owner_row.shape[0]
    counter = jnp.arange(count)
    same = owner_row[:, None] == owner_row[None, :]
    earlier = counter[None, :] < counter[:, None]
    ranks = jnp.sum((same & earlier).astype(jnp.int32), 1)
    places = (
        owner_row[:, None] * narrow_size + jnp.arange(narrow_size)[None, :]
    ) * capacity + ranks[:, None]
    gathered = lax.all_gather(master[0].astype(bfloat), ("wide", "narrow"), axis=0, tiled=True)
    hidden = (count * half_rows * narrow_size - 6 * width) // 2
    piece_rows = half_rows * narrow_size

    def weight_rows(first, rows):
        order = places[first // piece_rows : (first + rows) // piece_rows].reshape(-1)
        return jnp.take(gathered, order, axis=0).reshape(-1, width)

    is_source = lax.axis_index("half") == 0
    x = stream[0, 0]
    length = x.shape[0]
    source_len, target_len = lengths[0, 0], lengths[1, 0]
    own_len = jnp.where(is_source, source_len, target_len)
    flag = is_source.astype(jnp.int32)
    own_scal = jnp.stack([own_len, 1 - flag, flag, target_len]).astype(jnp.int32)
    cross_scal = jnp.stack([source_len, jnp.int32(0), flag, target_len]).astype(jnp.int32)
    table = places.reshape(-1).astype(jnp.int32)
    self_vec = jnp.where(is_source, vec_master[0:3], vec_master[6:9])
    self_w = (VM, weight_rows(0, 4 * width))
    up_w = (VM, weight_rows(6 * width, hidden))
    down_w = (VM, weight_rows(6 * width + hidden, hidden))
    cross_w = (VM, weight_rows(4 * width, 2 * width))
    slots = shaped(capacity * wide_size * narrow_size, half_rows, width, dtype=bfloat)
    stage_of = lambda chunks: [
        low_vm(chunks, 512, width),
        pltpu.SemaphoreType.DMA((chunks * 512 // half_rows,)),
    ]
    two = low_vm(2, length, 128)

    query, key, value, ctx_t, lse, resid, inner = call(
        self_forward_kernel,
        [(SM, own_scal), (VM, x), self_w, (VM, self_vec)],
        [(VM, low(length, width))] * 3
        + [(VM, low(width, length)), (VM, shaped(HEADS, length))]
        + [(VM, shaped(length, width))] * 2,
        [low_vm(width, length), low_vm(width, length), two],
        "self_forward",
    )
    activ, slope, ff_resid, memory, sendout = call(
        encoder_ff_kernel,
        [(SM, own_scal), (VM, inner), up_w, down_w, cross_w, (VM, vec_master[3:6])],
        [
            (VM, low(length, hidden)),
            (VM, low(length, hidden)),
            (VM, shaped(length, width)),
            (VM, low(length, width)),
            (VM, low(2, length, width)),
        ],
        [],
        "encoder_ff",
    )
    keys = lax.ppermute(sendout, "half", [(0, 1)])
    cross_query, cross_ctx_t, cross_lse, cross_resid, inner_two = call(
        cross_forward_kernel,
        [(SM, cross_scal), (VM, inner), (VM, keys), cross_w, (VM, vec_master[9:12])],
        [
            (VM, low(length, width)),
            (VM, low(width, length)),
            (VM, shaped(HEADS, length)),
            (VM, shaped(length, width)),
            (VM, shaped(length, width)),
        ],
        [low_vm(width, length), low_vm(width, length), two],
        "cross_forward",
    )
    output, grad_two, ff_vec, target = call(
        decoder_ff_kernel,
        [
            (SM, own_scal),
            (SM, table),
            (VM, inner_two),
            up_w,
            down_w,
            (VM, vec_master[12:15]),
            (VM, cotangent[0]),
        ],
        [
            (VM, low(length, width)),
            (VM, shaped(length, width)),
            (VM, shaped(3, width)),
            (HB, slots),
        ],
        [low_vm(length, hidden), low_vm(length, hidden), low_vm(length, width), low_vm(length, width)]
        + stage_of(8),
        "decoder_ff",
    )
    attn_scratch = (
        [low_vm(length, width), low_vm(length, width), low_vm(width, length), full_vm(HEADS, length)]
        + [low_vm(width, length), low_vm(width, length)]
        + [full_vm(length, width), full_vm(length, width), low_vm(width, length), two, two]
    )
    sendback, grad_one, cross_vec, target = call(
        cross_back_kernel,
        [
            (SM, cross_scal),
            (SM, table),
            (VM, inner),
            (VM, cross_resid),
            (VM, cross_query),
            (VM, keys),
            (VM, cross_ctx_t),
            (VM, cross_lse),
            cross_w,
            (VM, vec_master[9:12]),
            (VM, grad_two),
            (HB, target),
        ],
        [
            (VM, low(2, length, width)),
            (VM, shaped(length, width)),
            (VM, shaped(3, width)),
            (HB, slots),
        ],
        attn_scratch + stage_of(2),
        "cross_back",
        {11: 3},
    )
    returned = lax.ppermute(sendback, "half", [(1, 0)])
    grad_inner, memory_vec, target = call(
        encoder_back_kernel,
        [
            (SM, own_scal),
            (SM, table),
            (VM, returned),
            (VM, memory),
            cross_w,
            (VM, inner),
            (VM, ff_resid),
            (VM, activ),
            (VM, slope),
            up_w,
            down_w,
            (VM, vec_master[3:6]),
            (HB, target),
        ],
        [(VM, shaped(length, width)), (VM, shaped(3, width)), (HB, slots)],
        [full_vm(length, width), low_vm(length, width), low_vm(length, width)] + stage_of(10),
        "encoder_back",
        {12: 2},
    )
    grad_x, own_vec, target = call(
        self_back_kernel,
        [
            (SM, own_scal),
            (SM, table),
            (VM, x),
            self_w,
            (VM, self_vec),
            (VM, resid),
            (VM, query),
            (VM, key),
            (VM, value),
            (VM, ctx_t),
            (VM, lse),
            (VM, jnp.where(is_source, grad_inner, grad_one)),
            (HB, target),
        ],
        [(VM, shaped(length, width)), (VM, shaped(3, width)), (HB, slots)],
        attn_scratch + stage_of(4),
        "self_back",
        {12: 2},
    )
    zeros = jnp.zeros((3, width), single)
    vec_grads = jnp.where(
        is_source,
        jnp.concatenate([own_vec, memory_vec, zeros, zeros, zeros], 0),
        jnp.concatenate([zeros, zeros, own_vec, cross_vec, ff_vec], 0),
    )
    mine = lax.psum_scatter(target, ("wide", "narrow"), scatter_dimension=0, tiled=True)
    used = jnp.sum((owner_row == lax.axis_index("wide")).astype(jnp.int32))
    mine = jnp.where(
        (jnp.arange(capacity) < used)[:, None, None], mine.astype(single), 0.0
    )
    vec_total = lax.psum(vec_grads, ("half", "wide", "narrow"))
    new_weight, new_first, new_second = adam(
        master[0], mine, moment_one[0], moment_two[0], rate_matrix, decay_matrix
    )
    vec_weight, vec_first, vec_second = adam(
        vec_master, vec_total, vec_one, vec_two, rate_vector, 0.0
    )
    return (
        jnp.where(is_source, memory, output)[None, None],
        grad_x[None, None],
        new_first[None],
        new_second[None],
        new_weight[None],
        new_weight.astype(bfloat)[None],
        vec_first,
        vec_second,
        vec_weight,
    )


def solution(mesh):
    in_specs = (
        P("half", ("wide", "narrow"), None, None),
        P(("wide", "narrow"), None, None),
        P(None, ("wide", "narrow")),
        P("half", None),
        P("half", "wide", "narrow", None),
        P("half", "wide", "narrow", None),
        P("half", "wide", "narrow", None),
        P(),
        P(),
        P(),
    )
    out_specs = (
        P("half", ("wide", "narrow"), None, None),
        P("half", ("wide", "narrow"), None, None),
        P("half", "wide", "narrow", None),
        P("half", "wide", "narrow", None),
        P("half", "wide", "narrow", None),
        P("half", "wide", "narrow", None),
        P(),
        P(),
        P(),
    )
    return jax.shard_map(
        on_device, mesh=mesh, in_specs=in_specs, out_specs=out_specs, check_vma=False
    )
```

```python
import math
from functools import partial

import jax
import jax.numpy as jnp
from jax import lax
from jax.experimental import pallas as pl
from jax.experimental.pallas import tpu as pltpu
from jax.sharding import PartitionSpec as P

HEADS = 8
STEP = 5
QB = 256
RB = 256
NEG = -1e30

eps_norm = 1e-05
beta_one = 0.5
beta_two = 0.5
rate_matrix = 0.05
rate_vector = 0.3
decay_matrix = 0.01
eps_adam = 1e-08
bfloat = jnp.bfloat16
single = jnp.float32
VM = pl.BlockSpec(memory_space=pltpu.VMEM)
SM = pl.BlockSpec(memory_space=pltpu.SMEM)
HB = pl.BlockSpec(memory_space=pl.ANY)


def mm(left, right):
    return jnp.dot(left, right, preferred_element_type=single)


def mm_tn(left, right):
    return lax.dot_general(left, right, (((0,), (0,)), ((), ())), preferred_element_type=single)


def mm_nt(left, right):
    return lax.dot_general(left, right, (((1,), (1,)), ((), ())), preferred_element_type=single)


def block_of(index, size):
    return pl.ds(pl.multiple_of(index * size, size), size)


def normed(resid):
    center = resid - jnp.mean(resid, -1, keepdims=True)
    spread = jnp.mean(center * center, -1, keepdims=True)
    rstd = lax.rsqrt(spread + eps_norm)
    return center * rstd, rstd


def norm_back(resid, grad, gain):
    hat, rstd = normed(resid)
    grad_hat = grad * gain
    grad_resid = rstd * (
        grad_hat
        - jnp.mean(grad_hat, -1, keepdims=True)
        - hat * jnp.mean(grad_hat * hat, -1, keepdims=True)
    )
    return grad_resid, jnp.sum(grad * hat, 0, keepdims=True), jnp.sum(grad, 0, keepdims=True)


def gelu_parts(pre_act):
    half = 0.5 * (1.0 + lax.erf(pre_act * math.sqrt(0.5)))
    slope = half + pre_act * (jnp.exp(-0.5 * pre_act * pre_act) * (1.0 / math.sqrt(2.0 * math.pi)))
    return pre_act * half, slope


def pair_keys(tile, first_extra, ones):
    rows = tile.shape[0]
    lane = lax.broadcasted_iota(jnp.int32, (rows, 128), 1)
    wide_tile = tile.astype(single)
    out = []
    for head in range(2):
        at = lane - (64 - 64 * head)
        extra = jnp.where(at == 0, first_extra, jnp.where((at > 0) & (at < ones), 1.0, 0.0))
        mine = (lane < 64) if head == 0 else (lane >= 64)
        out.append(jnp.where(mine, wide_tile, extra).astype(bfloat))
    return out


def pair_queries(tile, head, extra_rows):
    mine = tile[64 * head : 64 * head + 64]
    row = lax.broadcasted_iota(jnp.int32, mine.shape, 0)
    extra = jnp.zeros(mine.shape, single)
    for number, value in enumerate(extra_rows):
        extra = jnp.where(row == number, value, extra)
    extra = extra.astype(bfloat)
    return jnp.concatenate([mine, extra] if head == 0 else [extra, mine], 0)


def split_three(value):
    high = value.astype(bfloat).astype(single)
    rest = value - high
    middle = rest.astype(bfloat).astype(single)
    return [high, middle, rest - middle]


def key_bias(limit, rows):
    row = lax.broadcasted_iota(jnp.int32, (rows, 128), 0)
    return jnp.where(row < limit, 0.0, NEG)


def score_parts(scores, diagonal):
    if not diagonal:
        return [scores]
    size = scores.shape[1]
    cut = scores.shape[0] - size
    row = lax.broadcasted_iota(jnp.int32, (size, size), 0)
    column = lax.broadcasted_iota(jnp.int32, (size, size), 1)
    last = jnp.where(row <= column, scores[cut:], NEG)
    return [scores[:cut], last] if cut else [last]


def over_blocks(causal, rows, length, body):
    def every():
        def step(index, unused):
            body(index, length, False)
            return 0

        lax.fori_loop(0, rows // QB, step, 0)

    if causal is None:
        every()
        return
    pl.when(causal == 0)(every)

    @pl.when(causal != 0)
    def _():
        for index in range(length // QB):
            body(index, (index + 1) * QB, True)


def attend(limit, causal, key_ref, query_t, value_t, ctx_t, lse_ref, key_two):
    length, width = key_ref.shape
    bias = key_bias(limit, length)

    def pair(number, unused):
        columns = block_of(number, 128)
        for head, tile in enumerate(pair_keys(key_ref[:, columns], bias, 1)):
            key_two[head] = tile

        def body(index, extent, diagonal):
            at = block_of(index, QB)
            tile = query_t[columns, at]
            for head in range(2):
                mine = pl.ds(pl.multiple_of(number * 128 + 64 * head, 64), 64)
                scores = mm(key_two[head, :extent], pair_queries(tile, head, [1.0]))
                parts = score_parts(scores, diagonal)
                top = jnp.max(parts[0], 0, keepdims=True)
                for part in parts[1:]:
                    top = jnp.maximum(top, jnp.max(part, 0, keepdims=True))
                parts = [jnp.exp(part - top) for part in parts]
                total = sum(jnp.sum(part, 0, keepdims=True) for part in parts)
                weights = jnp.concatenate([part.astype(bfloat) for part in parts], 0)
                context = mm(value_t[mine, :extent], weights)
                ctx_t[mine, at] = (context * (1.0 / total)).astype(bfloat)
                lse_ref[pl.ds(number * 2 + head, 1), at] = top + jnp.log(total)

        over_blocks(causal, query_t.shape[1], length, body)
        return 0

    lax.fori_loop(0, width // 128, pair, 0)


def attend_back(
    limit, causal, query_ref, key_ref, value_ref, query_t, key_t, grad_ctx, grad_ctx_t, lse_ref, dot_ref,
    grad_key, grad_value, grad_query_t, key_two, value_two,
):
    length, width = key_ref.shape
    bias = key_bias(limit, length)
    grad_key[...] = jnp.zeros(grad_key.shape, single)
    grad_value[...] = jnp.zeros(grad_value.shape, single)

    def pair(number, unused):
        columns = block_of(number, 128)
        for head, tile in enumerate(pair_keys(key_ref[:, columns], bias, 4)):
            key_two[head] = tile
        for head, tile in enumerate(pair_keys(value_ref[:, columns], 1.0, 3)):
            value_two[head] = tile

        def body(index, extent, diagonal):
            at = block_of(index, QB)
            query_tile = query_t[columns, at]
            ctx_tile = grad_ctx_t[columns, at]
            all_weights, all_grads = [], []
            for head in range(2):
                mine = pl.ds(pl.multiple_of(number * 128 + 64 * head, 64), 64)
                row = pl.ds(number * 2 + head, 1)
                minus_lse = split_three(-lse_ref[row, at])
                scores = mm(
                    key_two[head, :extent], pair_queries(query_tile, head, [1.0] + minus_lse)
                )
                weights = [jnp.exp(part) for part in score_parts(scores, diagonal)]
                weights = jnp.concatenate(weights, 0)
                minus_dot = split_three(-dot_ref[row, at])
                grad_weights = mm(value_two[head, :extent], pair_queries(ctx_tile, head, minus_dot))
                grads = (weights * grad_weights).astype(bfloat)
                all_weights.append(weights.astype(bfloat))
                all_grads.append(grads)
                grad_query = mm(key_t[mine, :extent], grads)
                grad_query_t[mine, at] = (grad_query * 0.125).astype(bfloat)
            lane = lax.broadcasted_iota(jnp.int32, (QB, 128), 1)

            def both(tile):
                tile = tile.astype(single)
                return jnp.concatenate(
                    [
                        jnp.where(lane < 64, tile, 0.0).astype(bfloat),
                        jnp.where(lane < 64, 0.0, tile).astype(bfloat),
                    ],
                    0,
                )

            grad_value[:extent, columns] += mm(
                jnp.concatenate(all_weights, 1), both(grad_ctx[at, columns])
            )
            grad_key[:extent, columns] += mm(
                jnp.concatenate(all_grads, 1), both(query_ref[at, columns])
            )

        over_blocks(causal, query_t.shape[1], length, body)
        return 0

    lax.fori_loop(0, width // 128, pair, 0)


def by_rows(length, body, init=0):
    def step(index, carry):
        return body(block_of(index, RB), carry)

    return lax.fori_loop(0, length // RB, step, init)


class Emitter:
    def __init__(self, table, target, stage, semaphores):
        self.table, self.target, self.stage, self.semaphores = table, target, stage, semaphores
        self.copies = []

    def chunk(self, number, first_piece, value):
        stage, half_rows = self.stage, self.target.shape[1]
        stage[number] = value.astype(bfloat)
        count = stage.shape[1] // half_rows
        per_piece = 128 // half_rows
        for part in range(count):
            copy = pltpu.make_async_copy(
                stage.at[number, pl.ds(part * half_rows, half_rows)],
                self.target.at[self.table[first_piece * per_piece + part]],
                self.semaphores.at[number * count + part],
            )
            copy.start()
            self.copies.append(copy)

    def wait(self):
        for copy in self.copies:
            copy.wait()


class Moves:
    def __init__(self, role):
        self.role = role
        self.loads = []
        self.stores = []
        self.waited = set()

    def load(self, dest, ways, semaphores):
        def begin(way):
            for number, (source, first, at, rows) in enumerate(way):
                if rows is not None:
                    source = source.at[pl.ds(first, rows)]
                    target = dest.at[pl.ds(at, rows)]
                else:
                    target = dest
                pltpu.make_async_copy(source, target, semaphores.at[number]).start()

        def finish(way):
            for number, (source, first, at, rows) in enumerate(way):
                if rows is not None:
                    source = source.at[pl.ds(first, rows)]
                    target = dest.at[pl.ds(at, rows)]
                else:
                    target = dest
                pltpu.make_async_copy(source, target, semaphores.at[number]).wait()

        def split(act):
            if len(ways) == 1:
                act(ways[0])
                return
            pl.when(self.role != 0)(lambda: act(ways[0]))
            pl.when(self.role == 0)(lambda: act(ways[1]))

        split(begin)
        self.loads.append((dest, lambda: split(finish)))

    def need(self, *refs):
        for number, (dest, finish) in enumerate(self.loads):
            if number not in self.waited and any(dest is ref for ref in refs):
                self.waited.add(number)
                finish()

    def rest(self):
        self.need(*[dest for dest, unused in self.loads])

    def place(self, source, target, semaphore):
        self.stores.append([source, target, semaphore, None])

    def put(self, *refs):
        for entry in self.stores:
            if entry[3] is None and any(entry[0] is ref for ref in refs):
                entry[3] = pltpu.make_async_copy(entry[0], entry[1], entry[2])
                entry[3].start()

    def finish(self):
        self.rest()
        self.put(*[entry[0] for entry in self.stores])
        for entry in self.stores:
            entry[3].wait()


def part(value, first, rows):
    return ("load", [[(value, first, 0, rows)]])


def whole(value):
    return ("load", [[(value, 0, 0, None)]])


def either(source_way, target_way):
    return ("load", [source_way, target_way])


def call(body, name, scal, active, ins, outs, scratch, aliases=()):
    args, specs, scratch_all, plan = [scal], [SM], [], []
    counts = {"load": 0, "store": 0}

    def arg(value, spec):
        args.append(value)
        specs.append(spec)
        return len(args) - 1

    held = []
    for kind, value in ins:
        if kind == "load":
            ways = [[(arg(v, HB), first, at, rows) for v, first, at, rows in way] for way in value]
            v, first, at, rows = value[0][0]
            total = max(a + r for _, _, a, r in value[0]) if rows is not None else None
            shape = v.shape if rows is None else (total,) + v.shape[1:]
            held.append(("load", ways, shape, v.dtype, max(len(w) for w in ways)))
        else:
            held.append((kind, arg(value, SM if kind == "smem" else HB)))
    vmem, sems = [], []
    for entry in held:
        if entry[0] == "load":
            vmem.append(pltpu.VMEM(entry[2], entry[3]))
            sems.append(pltpu.SemaphoreType.DMA((entry[4],)))
    for kind, shape in outs:
        if kind == "store":
            vmem.append(pltpu.VMEM(shape.shape, shape.dtype))
            sems.append(pltpu.SemaphoreType.DMA((1,)))
    count_in, count_out = len(args), len(outs)

    def kernel(*refs):
        inputs, outputs = refs[:count_in], refs[count_in : count_in + count_out]
        rest = refs[count_in + count_out :]
        buffers, semaphores = list(rest[: len(vmem)]), list(rest[len(vmem) : len(vmem) + len(sems)])
        extra = rest[len(vmem) + len(sems) :]
        scal_ref = inputs[0]

        def run():
            moves = Moves(scal_ref[2])
            given = []
            for entry in held:
                if entry[0] == "load":
                    dest, semaphore = buffers.pop(0), semaphores.pop(0)
                    ways = [[(inputs[i], f, a, r) for i, f, a, r in way] for way in entry[1]]
                    moves.load(dest, ways, semaphore)
                    given.append(dest)
                else:
                    given.append(inputs[entry[1]])
            for (kind, unused), output in zip(outs, outputs):
                if kind == "store":
                    source, semaphore = buffers.pop(0), semaphores.pop(0)
                    moves.place(source, output, semaphore.at[0])
                    given.append(source)
                else:
                    given.append(output)
            body(moves, scal_ref, *given, *extra)
            moves.finish()

        if active is None:
            run()
        else:
            pl.when(scal_ref[2] == active)(run)

    pairs = {}
    for position, output in aliases:
        pairs[held[position][1]] = output
    return pl.pallas_call(
        kernel,
        in_specs=specs,
        out_specs=[HB] * count_out,
        out_shape=[shape for unused, shape in outs],
        scratch_shapes=vmem + sems + list(scratch),
        input_output_aliases=pairs,
        compiler_params=pltpu.CompilerParams(vmem_limit_bytes=58 << 20),
        name=name,
    )(*args)


def zero_rows(width):
    return (jnp.zeros((1, width), single),) * 3


def put_rows(ref, rows):
    for number, row in enumerate(rows):
        ref[number : number + 1] = row


def project_norm(length, ctx_t, weight, inner_ref, vec, resid_ref, out_ref):
    def body(rows, carry):
        branch = mm(ctx_t[:, rows].T, weight[...])
        resid = inner_ref[rows].astype(single) * vec[0:1] + branch
        resid_ref[rows] = resid
        out_ref[rows] = normed(resid)[0] * vec[1:2] + vec[2:3]
        return carry

    by_rows(length, body)


def self_forward_body(
    io, scal, x, weight, out_weight, vec, query, key, value, ctx_t, lse, resid, out,
    query_t, value_t, key_two,
):
    length, width = x.shape
    io.need(x, weight)

    def body(rows, carry):
        tile = x[rows]
        for number, ref in enumerate((query, key, value)):
            ref[rows] = mm(tile, weight[width * number : width * (number + 1)]).astype(bfloat)
        query_t[:, rows] = (query[rows] * bfloat(0.125)).T
        value_t[:, rows] = value[rows].T
        return carry

    by_rows(length, body)
    io.put(query, key, value)
    attend(scal[0], scal[1], key, query_t, value_t, ctx_t, lse, key_two)
    io.put(ctx_t, lse)
    io.rest()
    project_norm(length, ctx_t, out_weight, x, vec, resid, out)


def encoder_ff_body(
    io, scal, inner, up, down, cross, vec, activ, slope, resid, memory, sendout
):
    length, width = inner.shape
    io.rest()

    def body(rows, carry):
        tile = inner[rows]
        act, grad = gelu_parts(mm_nt(tile.astype(bfloat), up[...]))
        act = act.astype(bfloat)
        activ[rows] = act
        slope[rows] = grad.astype(bfloat)
        total = tile * vec[0:1] + mm(act, down[...])
        resid[rows] = total
        mem = (normed(total)[0] * vec[1:2] + vec[2:3]).astype(bfloat)
        memory[rows] = mem
        sendout[0, rows] = mm(mem, cross[:width]).astype(bfloat)
        sendout[1, rows] = mm(mem, cross[width:]).astype(bfloat)
        return carry

    by_rows(length, body)


def cross_forward_body(
    io, scal, inner, keys, cross, vec, query, ctx_t, lse, resid, out, query_t, value_t, key_two
):
    rows_here, width = inner.shape
    io.need(inner, cross, keys)

    def body(rows, carry):
        query[rows] = mm(inner[rows].astype(bfloat), cross[:width]).astype(bfloat)
        query_t[:, rows] = (query[rows] * bfloat(0.125)).T
        return carry

    def turn(rows, carry):
        value_t[:, rows] = keys[1, rows].T
        return carry

    by_rows(rows_here, body)
    by_rows(keys.shape[1], turn)
    attend(scal[4], None, keys.at[0], query_t, value_t, ctx_t, lse, key_two)
    io.put(query, ctx_t, lse)
    io.rest()
    project_norm(rows_here, ctx_t, cross.at[width:], inner, vec, resid, out)


def ff_back(length, emit, grad_branch, activ, slope, inner_low, up, down, grad_inner):
    def body(rows, carry):
        grad = mm_nt(grad_branch[rows], down[...]) * slope[rows].astype(single)
        grad = grad.astype(bfloat)
        slope[rows] = grad
        grad_inner[rows] += mm(grad, up[...])
        return carry

    by_rows(length, body)
    for number in range(activ.shape[1] // 512):
        columns = slice(number * 512, (number + 1) * 512)
        emit(0, number, mm_tn(slope[:, columns], inner_low[...]))
        emit(1, number, mm_tn(activ[:, columns], grad_branch[...]))


def decoder_ff_body(
    io, scal, inner, up, down, vec, cotan, out, grad_inner, grad_vec, grads,
    activ, slope, inner_low, grad_branch,
):
    length, width = inner.shape
    io.rest()

    def body(rows, carry):
        tile = inner[rows]
        low_tile = tile.astype(bfloat)
        inner_low[rows] = low_tile
        act, grad = gelu_parts(mm_nt(low_tile, up[...]))
        act = act.astype(bfloat)
        activ[rows] = act
        slope[rows] = grad.astype(bfloat)
        total = tile * vec[0:1] + mm(act, down[...])
        out[rows] = (normed(total)[0] * vec[1:2] + vec[2:3]).astype(bfloat)
        row = lax.broadcasted_iota(jnp.int32, tile.shape, 0) + rows.start
        grad_out = jnp.where(row < scal[3], cotan[rows].astype(single), 0.0)
        grad_resid, grad_gain, grad_shift = norm_back(total, grad_out, vec[1:2])
        grad_branch[rows] = grad_resid.astype(bfloat)
        grad_inner[rows] = grad_resid * vec[0:1]
        weigh = jnp.sum(grad_resid * tile, 0, keepdims=True)
        return (carry[0] + weigh, carry[1] + grad_gain, carry[2] + grad_shift)

    put_rows(grad_vec, by_rows(length, body, zero_rows(width)))
    io.put(out, grad_vec)
    hidden = up.shape[0]

    def emit(which, number, value):
        grads[which * hidden + number * 512 : which * hidden + (number + 1) * 512] = value.astype(bfloat)

    ff_back(length, emit, grad_branch, activ, slope, inner_low, up, down, grad_inner)


def branch_back(length, resid, grad_out, inner, vec, grad_branch, grad_inner, grad_vec):
    width = resid.shape[1]

    def body(rows, carry):
        grad_resid, grad_gain, grad_shift = norm_back(resid[rows], grad_out[rows], vec[1:2])
        grad_branch[rows] = grad_resid.astype(bfloat)
        grad_inner[rows] = grad_resid * vec[0:1]
        weigh = jnp.sum(grad_resid * inner[rows].astype(single), 0, keepdims=True)
        return (carry[0] + weigh, carry[1] + grad_gain, carry[2] + grad_shift)

    put_rows(grad_vec, by_rows(length, body, zero_rows(width)))


def ctx_back(length, grad_branch, weight, ctx_t, grad_ctx, grad_ctx_t, dot_ref):
    def body(rows, carry):
        grad_ctx[rows] = mm_nt(grad_branch[rows], weight[...]).astype(bfloat)
        grad_ctx_t[:, rows] = grad_ctx[rows].T
        for head in range(HEADS):
            mine = slice(64 * head, 64 * head + 64)
            product = grad_ctx_t[mine, rows].astype(single) * ctx_t[mine, rows].astype(single)
            dot_ref[head : head + 1, rows] = jnp.sum(product, 0, keepdims=True)
        return carry

    by_rows(length, body)


def cross_back_body(
    io, scal, inner, resid, query, keys, ctx_t, lse, cross, vec, grad_out,
    sendback, grad_inner, grad_vec, grads,
    grad_branch, grad_ctx, grad_ctx_t, dot_ref, query_t, key_t, grad_key, grad_value, grad_query_t,
    key_two, value_two,
):
    rows_here, width = inner.shape
    io.need(inner, resid, vec, grad_out)
    branch_back(rows_here, resid, grad_out, inner, vec, grad_branch, grad_inner, grad_vec)
    io.rest()
    io.put(grad_vec)
    grads[width:] = mm(ctx_t[...], grad_branch[...]).astype(bfloat)
    ctx_back(rows_here, grad_branch, cross.at[width:], ctx_t, grad_ctx, grad_ctx_t, dot_ref)

    def body(rows, carry):
        query_t[:, rows] = (query[rows] * bfloat(0.125)).T
        return carry

    def turn(rows, carry):
        key_t[:, rows] = keys[0, rows].T
        return carry

    by_rows(rows_here, body)
    by_rows(keys.shape[1], turn)
    attend_back(
        scal[4], None, query, keys.at[0], keys.at[1], query_t, key_t, grad_ctx, grad_ctx_t, lse, dot_ref,
        grad_key, grad_value, grad_query_t, key_two, value_two,
    )

    def send(rows, carry):
        sendback[0, rows] = (grad_key[rows] * 0.125).astype(bfloat)
        sendback[1, rows] = grad_value[rows].astype(bfloat)
        return carry

    by_rows(keys.shape[1], send)
    io.put(sendback)

    def last(rows, carry):
        grad_query = grad_query_t[:, rows].T
        grad_inner[rows] += mm_nt(grad_query, cross[:width])
        grad_ctx[rows] = grad_query
        return carry

    by_rows(rows_here, last)
    io.put(grad_inner)
    grads[:width] = mm_tn(inner[...].astype(bfloat), grad_ctx[...]).astype(bfloat)


def encoder_back_body(
    io, scal, table, own, received, memory, cross, inner, resid, activ, slope, up, down, vec,
    grad_inner, grad_vec, target,
    grad_mem, inner_low, grad_branch, stage, semaphores,
):
    length, width = inner.shape
    emit = Emitter(table, target, stage, semaphores)
    io.need(own, received, cross, inner)

    def body(rows, carry):
        for number in range(2):
            total = own[number, rows].astype(single) + received[number, rows].astype(single)
            own[number, rows] = total.astype(bfloat)
        grad_mem[rows] = mm_nt(own[0, rows], cross[:width]) + mm_nt(own[1, rows], cross[width:])
        inner_low[rows] = inner[rows].astype(bfloat)
        return carry

    by_rows(length, body)
    io.rest()
    branch_back(length, resid, grad_mem, inner, vec, grad_branch, grad_inner, grad_vec)
    io.put(grad_vec)

    def each(which, number, value):
        emit.chunk(2 * number + which, 24 + 16 * which + 4 * number, value)

    ff_back(length, each, grad_branch, activ, slope, inner_low, up, down, grad_inner)
    io.put(grad_inner)
    emit.chunk(8, 16, mm_tn(memory[...], own[0]))
    emit.chunk(9, 20, mm_tn(memory[...], own[1]))
    emit.wait()


def self_back_body(
    io, scal, table, x, weight, out_weight, vec, resid, query, key, value, ctx_t, lse, grad_out, held,
    grad_x, grad_vec, target,
    grad_branch, grad_ctx, grad_ctx_t, dot_ref, query_t, key_t, grad_key, grad_value, grad_query_t,
    key_two, value_two, stage, semaphores,
):
    length, width = x.shape
    emit = Emitter(table, target, stage, semaphores)
    io.need(resid, grad_out, x, vec)
    branch_back(length, resid, grad_out, x, vec, grad_branch, grad_x, grad_vec)
    io.put(grad_vec)
    io.need(ctx_t, out_weight)
    emit.chunk(3, 12, mm(ctx_t[...], grad_branch[...]))
    ctx_back(length, grad_branch, out_weight, ctx_t, grad_ctx, grad_ctx_t, dot_ref)
    io.rest()

    def body(rows, carry):
        query_t[:, rows] = (query[rows] * bfloat(0.125)).T
        key_t[:, rows] = key[rows].T
        return carry

    by_rows(length, body)
    attend_back(
        scal[0], scal[1], query, key, value, query_t, key_t, grad_ctx, grad_ctx_t, lse, dot_ref,
        grad_key, grad_value, grad_query_t, key_two, value_two,
    )

    def last(rows, carry):
        parts = (
            grad_query_t[:, rows].T,
            (grad_key[rows] * 0.125).astype(bfloat),
            grad_value[rows].astype(bfloat),
        )
        total = grad_x[rows]
        for number, low_grad in enumerate(parts):
            total += mm_nt(low_grad, weight[width * number : width * (number + 1)])
        grad_x[rows] = total
        grad_branch[rows], grad_ctx[rows], value[rows] = parts
        return carry

    by_rows(length, last)
    io.put(grad_x)
    for number, ref in enumerate((grad_branch, grad_ctx, value)):
        emit.chunk(number, 4 * number, mm_tn(x[...], ref[...]))
    emit.wait()


def merge_body(io, scal, table, ff_own, ff_other, cross_own, cross_other, held, target, stage, semaphores):
    emit = Emitter(table, target, stage, semaphores)
    io.rest()
    chunk = stage.shape[1]
    for first, own, other in ((16, cross_own, cross_other), (24, ff_own, ff_other)):
        for number in range(own.shape[0] // chunk):
            rows = slice(number * chunk, (number + 1) * chunk)
            total = own[rows].astype(single) + other[rows].astype(single)
            emit.chunk((first - 16) // 4 + number, first + 4 * number, total)
    emit.wait()


def place_kernel(where, scal, table, *refs):
    sources = refs[: len(where)]
    first_out, rest_out, pieces, semaphores, out_semaphores = refs[len(where) :]
    cut = first_out.shape[0]

    def each(act):
        base = 0
        for source, ranges in zip(sources, where):
            for start, stop, distance, other, first in ranges:

                def step(slot, unused):
                    piece = table[distance, first + slot - start]
                    at = piece * 2 + (scal[0] if other == 0 else 1 - scal[0])

                    @pl.when(piece >= 0)
                    def _():
                        semaphore = semaphores.at[base + slot]
                        act(pltpu.make_async_copy(source.at[slot], pieces.at[at], semaphore))

                    return 0

                lax.fori_loop(start, stop, step, 0)
            base += source.shape[0]

    each(lambda copy: copy.start())
    each(lambda copy: copy.wait())
    outs = [
        pltpu.make_async_copy(pieces.at[pl.ds(0, cut)], first_out, out_semaphores.at[0]),
        pltpu.make_async_copy(pieces.at[pl.ds(cut, rest_out.shape[0])], rest_out, out_semaphores.at[1]),
    ]
    for copy in outs:
        copy.start()
    for copy in outs:
        copy.wait()


RING = (0, 2, 4, 6, 7, 5, 3, 1)
LEAD = 8


def round_ring(value, step):
    count = len(RING)
    return lax.ppermute(value, "wide", [(RING[i], RING[(i + step) % count]) for i in range(count)])


def swapped(value):
    return lax.ppermute(value, "narrow", [(0, 1), (1, 0)])


def step_of(up, down, across):
    return lax.optimization_barrier((round_ring(up, 1), round_ring(down, -1), swapped(across)))


def join(*values):
    return jnp.concatenate(values, 0)


def ring_gather(own):
    every, lead, half = own.shape[0], LEAD, LEAD // 2
    late = every - lead
    found = [([(0, every, 0, 0, 0)], own)]

    def ahead(value, far, near):
        ranges = [(0, lead, far, 0, 0)]
        if near is not None:
            ranges += [(lead, lead + late, near, 0, lead), (lead + late, lead + 2 * late, near, 1, lead)]
        found.append((ranges, value))

    up, down, across = step_of(own[:lead], own[:lead], own[lead:])
    found.append(([(0, late, 0, 1, lead)], across))
    ahead(up, 7, None)
    ahead(down, 1, None)
    pair = join(own[lead:], across)
    up, down, across = step_of(join(up, pair), join(down, pair), join(up, down, own[:half]))
    found.append(
        ([(0, lead, 7, 1, 0), (lead, 2 * lead, 1, 1, 0), (2 * lead, 2 * lead + half, 0, 1, 0)], across)
    )
    ahead(up, 6, 7)
    ahead(down, 2, 1)
    up, down, across = step_of(up, down, join(up[:lead], down[:lead], own[half:lead]))
    found.append(
        ([(0, lead, 6, 1, 0), (lead, 2 * lead, 2, 1, 0), (2 * lead, 2 * lead + half, 0, 1, half)], across)
    )
    ahead(up, 5, 6)
    ahead(down, 3, 2)
    up, down, across = step_of(join(up[:half], up[lead:]), down[half:], join(up[:lead], down[:lead]))
    found.append(([(0, lead, 5, 1, 0), (lead, 2 * lead, 3, 1, 0)], across))
    for value, first, near in ((up, 0, 5), (down, half, 3)):
        ranges = [(0, half, 4, 0, first), (half, half + late, near, 0, lead)]
        found.append((ranges + [(half + late, half + 2 * late, near, 1, lead)], value))
    up, down, across = step_of(
        up[half : half + late], down[half + late :], join(up[:half], down[:half])
    )
    found.append(([(0, late, 4, 0, lead)], up))
    found.append(([(0, late, 4, 1, lead)], down))
    found.append(([(0, lead, 4, 1, 0)], across))
    return found


def added(*values):
    return sum(value.astype(single) for value in values).astype(bfloat)


def ring_scatter(grads):
    lead, half = LEAD, LEAD // 2
    late = grads.shape[2] - lead

    def both(distance):
        return grads[distance, :, lead:].reshape((-1,) + grads.shape[3:])

    def mine(distance, start=0, stop=lead):
        return grads[distance, 0, start:stop]

    def other(distance, start=0, stop=lead):
        return grads[distance, 1, start:stop]

    up, down, across = step_of(grads[4, 0, lead:], grads[4, 1, lead:], other(4))
    first = added(mine(4), across)
    up = join(first[:half], added(up, grads[3, 0, lead:]), grads[3, 1, lead:])
    down = join(first[half:], grads[5, 0, lead:], added(down, grads[5, 1, lead:]))
    up, down, across = step_of(up, down, join(other(3), other(5)))
    up = join(
        added(mine(3, 0, half), across[:half], up[:half]),
        added(mine(3, half), across[half:lead]),
        added(up[half:], both(2)),
    )
    down = join(
        added(mine(5, 0, half), across[lead : lead + half]),
        added(mine(5, half), across[lead + half :], down[:half]),
        added(down[half:], both(6)),
    )
    up, down, across = step_of(up, down, join(other(2), other(6), other(0, 0, half)))
    nearest = [across[2 * lead :]]
    up = join(added(mine(2), across[:lead], up[:lead]), added(up[lead:], both(1)))
    down = join(added(mine(6), across[lead : 2 * lead], down[:lead]), added(down[lead:], both(7)))
    up, down, across = step_of(up, down, join(other(1), other(7), other(0, half)))
    nearest.append(across[2 * lead :])
    total = sum(value.astype(single) for value in (both(0), up[lead:], down[lead:]))
    up, down, across = step_of(
        added(mine(1), across[:lead], up[:lead]),
        added(mine(7), across[lead : 2 * lead], down[:lead]),
        total[late:].astype(bfloat),
    )
    first = sum(value.astype(single) for value in (mine(0), join(*nearest), up, down))
    return join(first, total[:late] + across.astype(single))


def shaped(*shape, dtype=single):
    return jax.ShapeDtypeStruct(shape, dtype)


def low(*shape):
    return jax.ShapeDtypeStruct(shape, bfloat)


def low_vm(*shape):
    return pltpu.VMEM(shape, bfloat)


def full_vm(*shape):
    return pltpu.VMEM(shape, single)


def sum_over(value, axis):
    size = lax.axis_size(axis)
    bit = 1
    while bit < size:
        value = value + lax.ppermute(value, axis, [(i, i ^ bit) for i in range(size)])
        bit *= 2
    return value


def adam(weight, gradient, first, second, step_rate, decay_rate):
    first_new = beta_one * first + (1.0 - beta_one) * gradient
    second_new = beta_two * second + (1.0 - beta_two) * gradient * gradient
    first_hat = first_new / (1.0 - beta_one**STEP)
    second_hat = second_new / (1.0 - beta_two**STEP)
    weight_new = weight - step_rate * (
        first_hat / (jnp.sqrt(second_hat) + eps_adam) + decay_rate * weight
    )
    return (weight_new, first_new, second_new)


def on_device(
    stream, cotangent, lengths, owners, master, moment_one, moment_two, vec_master, vec_one, vec_two
):
    narrow_size = lax.axis_size("narrow")
    wide_size = lax.axis_size("wide")
    owner_row = owners[0]
    capacity = master.shape[1]
    half_rows = master.shape[2]
    width = master.shape[3]
    count = owner_row.shape[0]
    counter = jnp.arange(count)
    same = owner_row[:, None] == owner_row[None, :]
    earlier = counter[None, :] < counter[:, None]
    ranks = jnp.sum((same & earlier).astype(jnp.int32), 1)
    places = (
        owner_row[:, None] * narrow_size + jnp.arange(narrow_size)[None, :]
    ) * capacity + ranks[:, None]
    on_ring = wide_size == len(RING) and narrow_size == 2 and capacity > LEAD
    wide_at, narrow_at = lax.axis_index("wide"), lax.axis_index("narrow")
    self_rows, rest_rows = 4 * width, count * half_rows * narrow_size - 4 * width
    own = master[0].astype(bfloat)
    if on_ring:
        turned = [RING.index(i) for i in range(wide_size)]
        position = jnp.array(turned)[wide_at]
        owner_ring = jnp.array(turned)[owner_row]
        distance = (owner_ring - position) % wide_size
        halves = jnp.arange(narrow_size)[None, :] ^ narrow_at
        table = ((distance[:, None] * 2 + halves) * capacity + ranks[:, None]).reshape(-1)
        slot_of = distance * capacity + ranks
        hit = slot_of[None, :] == jnp.arange(wide_size * capacity)[:, None]
        pieces = jnp.sum(hit.astype(jnp.int32) * (counter + 1)[None, :], 1) - 1
        found = ring_gather(own)
        slots_found = sum(value.shape[0] for unused, value in found)
        weight, rest = pl.pallas_call(
            partial(place_kernel, [where for where, unused in found]),
            in_specs=[SM, SM] + [HB] * len(found),
            out_specs=[HB, HB],
            out_shape=[
                low(self_rows // half_rows, half_rows, width),
                low(rest_rows // half_rows, half_rows, width),
            ],
            scratch_shapes=[
                low_vm(count * narrow_size, half_rows, width),
                pltpu.SemaphoreType.DMA((slots_found,)),
                pltpu.SemaphoreType.DMA((2,)),
            ],
            compiler_params=pltpu.CompilerParams(vmem_limit_bytes=58 << 20),
            name="place_weights",
        )(
            narrow_at.astype(jnp.int32)[None],
            pieces.reshape(wide_size, capacity).astype(jnp.int32),
            *[value for unused, value in found],
        )
        weight, rest = weight.reshape(-1, width), rest.reshape(-1, width)
    else:
        places = (
            owner_row[:, None] * narrow_size + jnp.arange(narrow_size)[None, :]
        ) * capacity + ranks[:, None]
        table = places.reshape(-1)
        gathered = lax.all_gather(own, ("wide", "narrow"), axis=0, tiled=True)
        weight = jnp.take(gathered, table, axis=0).reshape(-1, width)
        weight, rest = weight[:self_rows], weight[self_rows:]
    table = table.astype(jnp.int32)
    hidden = (rest_rows - 2 * width) // 2
    is_source = lax.axis_index("half") == 0
    x = stream[0, 0]
    length = x.shape[0]
    some = length // 2
    source_len, target_len = lengths[0, 0], lengths[1, 0]
    flag = is_source.astype(jnp.int32)
    scal = jnp.stack(
        [
            jnp.where(is_source, source_len, target_len),
            1 - flag,
            flag,
            jnp.where(is_source, target_len - some, target_len),
            source_len,
        ]
    ).astype(jnp.int32)
    self_vec = whole(jnp.where(is_source, vec_master[0:3], vec_master[6:9]))
    cross_vec, ff_vec = whole(vec_master[9:12]), whole(vec_master[12:15])
    memory_vec = whole(vec_master[3:6])
    cross_w = part(rest, 0, 2 * width)
    up_w = part(rest, 2 * width, hidden)
    down_w = part(rest, 2 * width + hidden, hidden)
    slots = low(capacity * wide_size * narrow_size, half_rows, width)

    def stage_of(chunks):
        return [
            low_vm(chunks, 512, width),
            pltpu.SemaphoreType.DMA((chunks * 512 // half_rows,)),
        ]

    def store(*shape, dtype=single):
        return ("store", shaped(*shape, dtype=dtype))

    low_out = partial(store, dtype=bfloat)
    two = low_vm(2, length, 128)
    down_half, up_half = [(1, 0)], [(0, 1)]

    rest_other = lax.ppermute(rest, "half", down_half)
    query, key, value, ctx_t, lse, resid, inner = call(
        self_forward_body,
        "self_forward",
        scal,
        None,
        [whole(x), part(weight, 0, 3 * width), part(weight, 3 * width, width), self_vec],
        [low_out(length, width)] * 3
        + [low_out(width, length), store(HEADS, length)]
        + [store(length, width)] * 2,
        [low_vm(width, length), low_vm(width, length), two],
    )
    inner_other = lax.ppermute(inner[some:], "half", down_half)
    activ, slope, ff_resid, memory, sendout = call(
        encoder_ff_body,
        "encoder_ff",
        scal,
        1,
        [whole(inner), up_w, down_w, cross_w, memory_vec],
        [low_out(length, hidden)] * 2
        + [store(length, width), low_out(length, width), low_out(2, length, width)],
        [],
    )
    sendout_other = lax.ppermute(sendout, "half", up_half)

    def shared(first, rows):
        return either([(rest_other, first, 0, rows)], [(rest, first, 0, rows)])

    mid_inner = either([(inner_other, 0, 0, some)], [(inner, 0, 0, some)])
    keys = either([(sendout, 0, 0, None)], [(sendout_other, 0, 0, None)])
    cross_query, cross_ctx_t, cross_lse, cross_resid, inner_two = call(
        cross_forward_body,
        "cross_forward",
        scal,
        None,
        [mid_inner, keys, shared(0, 2 * width), cross_vec],
        [low_out(some, width), low_out(width, some), store(HEADS, some)] + [store(some, width)] * 2,
        [low_vm(width, some), low_vm(width, length), two],
    )
    cotan = cotangent[0]
    output, grad_two, grad_ff_vec, grad_ff = call(
        decoder_ff_body,
        "decoder_ff",
        scal,
        None,
        [
            whole(inner_two),
            shared(2 * width, hidden),
            shared(2 * width + hidden, hidden),
            ff_vec,
            either([(cotan, some, 0, some)], [(cotan, 0, 0, some)]),
        ],
        [low_out(some, width), store(some, width), store(3, width), low_out(2 * hidden, width)],
        [low_vm(some, hidden), low_vm(some, hidden), low_vm(some, width), low_vm(some, width)],
    )
    output_other = lax.ppermute(output, "half", up_half)
    grad_ff_other = lax.ppermute(grad_ff, "half", up_half)

    def attn_scratch(rows):
        return (
            [low_vm(rows, width), low_vm(rows, width), low_vm(width, rows), full_vm(HEADS, rows)]
            + [low_vm(width, rows), low_vm(width, length)]
            + [full_vm(length, width), full_vm(length, width), low_vm(width, rows), two, two]
        )

    sendback, grad_one, grad_cross_vec, grad_cross = call(
        cross_back_body,
        "cross_back",
        scal,
        None,
        [
            mid_inner,
            whole(cross_resid),
            whole(cross_query),
            keys,
            whole(cross_ctx_t),
            whole(cross_lse),
            shared(0, 2 * width),
            cross_vec,
            whole(grad_two),
        ],
        [
            low_out(2, length, width),
            store(some, width),
            store(3, width),
            low_out(2 * width, width),
        ],
        attn_scratch(some),
    )
    sendback_other = lax.ppermute(sendback, "half", down_half)
    grad_one_other = lax.ppermute(grad_one, "half", up_half)
    grad_cross_other = lax.ppermute(grad_cross, "half", up_half)
    grad_inner, grad_memory_vec, target = call(
        encoder_back_body,
        "encoder_back",
        scal,
        1,
        [
            ("smem", table),
            whole(sendback),
            whole(sendback_other),
            whole(memory),
            cross_w,
            whole(inner),
            whole(ff_resid),
            whole(activ),
            whole(slope),
            up_w,
            down_w,
            memory_vec,
        ],
        [store(length, width), store(3, width), ("hbm", slots)],
        [full_vm(length, width), low_vm(length, width), low_vm(length, width)] + stage_of(10),
    )
    grad_x, grad_self_vec, target = call(
        self_back_body,
        "self_back",
        scal,
        None,
        [
            ("smem", table),
            whole(x),
            part(weight, 0, 3 * width),
            part(weight, 3 * width, width),
            self_vec,
            whole(resid),
            whole(query),
            whole(key),
            whole(value),
            whole(ctx_t),
            whole(lse),
            either(
                [(grad_inner, 0, 0, length)],
                [(grad_one, 0, 0, some), (grad_one_other, 0, some, some)],
            ),
            ("hbm", target),
        ],
        [store(length, width), store(3, width), ("hbm", slots)],
        attn_scratch(length) + stage_of(4),
        [(12, 2)],
    )
    (target,) = call(
        merge_body,
        "merge",
        scal,
        0,
        [
            ("smem", table),
            whole(grad_ff),
            whole(grad_ff_other),
            whole(grad_cross),
            whole(grad_cross_other),
            ("hbm", target),
        ],
        [("hbm", slots)],
        stage_of(10),
        [(5, 0)],
    )
    vec_grads = jnp.concatenate(
        [
            jnp.where(is_source, grad_self_vec, 0.0),
            jnp.where(is_source, grad_memory_vec, 0.0),
            jnp.where(is_source, 0.0, grad_self_vec),
            grad_cross_vec,
            grad_ff_vec,
        ],
        0,
    )
    for axis in ("narrow", "wide"):
        vec_grads = sum_over(vec_grads, axis)
    if on_ring:
        mine = ring_scatter(target.reshape(wide_size, 2, capacity, half_rows, width))
    else:
        mine = lax.psum_scatter(target, ("wide", "narrow"), scatter_dimension=0, tiled=True)
    mine, vec_grads = lax.optimization_barrier((mine, vec_grads))
    vec_grads = sum_over(vec_grads, "half")
    used = jnp.sum((owner_row == wide_at).astype(jnp.int32))
    mine = jnp.where((jnp.arange(capacity) < used)[:, None, None], mine.astype(single), 0.0)
    new_weight, new_first, new_second = adam(
        master[0], mine, moment_one[0], moment_two[0], rate_matrix, decay_matrix
    )
    vec_weight, vec_first, vec_second = adam(
        vec_master, vec_grads, vec_one, vec_two, rate_vector, 0.0
    )
    output = jnp.concatenate([output, output_other], 0)
    return (
        jnp.where(is_source, memory, output)[None, None],
        grad_x[None, None],
        new_first[None],
        new_second[None],
        new_weight[None],
        new_weight.astype(bfloat)[None],
        vec_first,
        vec_second,
        vec_weight,
    )


def solution(mesh):
    in_specs = (
        P("half", ("wide", "narrow"), None, None),
        P(("wide", "narrow"), None, None),
        P(None, ("wide", "narrow")),
        P("half", None),
        P("half", "wide", "narrow", None),
        P("half", "wide", "narrow", None),
        P("half", "wide", "narrow", None),
        P(),
        P(),
        P(),
    )
    out_specs = (
        P("half", ("wide", "narrow"), None, None),
        P("half", ("wide", "narrow"), None, None),
        P("half", "wide", "narrow", None),
        P("half", "wide", "narrow", None),
        P("half", "wide", "narrow", None),
        P("half", "wide", "narrow", None),
        P(),
        P(),
        P(),
    )
    return jax.shard_map(
        on_device, mesh=mesh, in_specs=in_specs, out_specs=out_specs, check_vma=False
    )
```

```python
import math
from functools import partial

import jax
import jax.numpy as jnp
from jax import lax
from jax.experimental import pallas as pl
from jax.experimental.pallas import tpu as pltpu
from jax.sharding import PartitionSpec as P

HEADS = 8
STEP = 5
CAUSAL = 512
RB = 512
NEG = -1e30

eps_norm = 1e-05
beta_one = 0.5
beta_two = 0.5
rate_matrix = 0.05
rate_vector = 0.3
decay_matrix = 0.01
eps_adam = 1e-08
bfloat = jnp.bfloat16
single = jnp.float32
VM = pl.BlockSpec(memory_space=pltpu.VMEM)
SM = pl.BlockSpec(memory_space=pltpu.SMEM)
HB = pl.BlockSpec(memory_space=pl.ANY)


def mm(left, right):
    return jnp.dot(left, right, preferred_element_type=single)


def mm_tn(left, right):
    return lax.dot_general(left, right, (((0,), (0,)), ((), ())), preferred_element_type=single)


def mm_nt(left, right):
    return lax.dot_general(left, right, (((1,), (1,)), ((), ())), preferred_element_type=single)


def block_of(index, size):
    return pl.ds(pl.multiple_of(index * size, size), size)


def normed(resid):
    center = resid - jnp.mean(resid, -1, keepdims=True)
    spread = jnp.mean(center * center, -1, keepdims=True)
    rstd = lax.rsqrt(spread + eps_norm)
    return center * rstd, rstd


def norm_back(resid, grad, gain):
    hat, rstd = normed(resid)
    grad_hat = grad * gain
    grad_resid = rstd * (
        grad_hat
        - jnp.mean(grad_hat, -1, keepdims=True)
        - hat * jnp.mean(grad_hat * hat, -1, keepdims=True)
    )
    return grad_resid, jnp.sum(grad * hat, 0, keepdims=True), jnp.sum(grad, 0, keepdims=True)


def gelu_parts(pre_act):
    half = 0.5 * (1.0 + lax.erf(pre_act * math.sqrt(0.5)))
    slope = half + pre_act * (jnp.exp(-0.5 * pre_act * pre_act) * (1.0 / math.sqrt(2.0 * math.pi)))
    return pre_act * half, slope


def pair_keys(tile, first_extra, ones):
    rows = tile.shape[0]
    lane = lax.broadcasted_iota(jnp.int32, (rows, 128), 1)
    wide_tile = tile.astype(single)
    out = []
    for head in range(2):
        at = lane - (64 - 64 * head)
        extra = jnp.where(at == 0, first_extra, jnp.where((at > 0) & (at < ones), 1.0, 0.0))
        mine = (lane < 64) if head == 0 else (lane >= 64)
        out.append(jnp.where(mine, wide_tile, extra).astype(bfloat))
    return out


def pair_queries(tile, head, extra_rows):
    mine = tile[64 * head : 64 * head + 64]
    row = lax.broadcasted_iota(jnp.int32, mine.shape, 0)
    extra = jnp.zeros(mine.shape, single)
    for number, value in enumerate(extra_rows):
        extra = jnp.where(row == number, value, extra)
    extra = extra.astype(bfloat)
    return jnp.concatenate([mine, extra] if head == 0 else [extra, mine], 0)


def split_three(value):
    high = value.astype(bfloat).astype(single)
    rest = value - high
    middle = rest.astype(bfloat).astype(single)
    return [high, middle, rest - middle]


def key_bias(limit, rows):
    row = lax.broadcasted_iota(jnp.int32, (rows, 128), 0)
    return jnp.where(row < limit, 0.0, NEG)


def score_parts(scores, diagonal):
    if not diagonal:
        return [scores]
    size = scores.shape[1]
    cut = scores.shape[0] - size
    row = lax.broadcasted_iota(jnp.int32, (size, size), 0)
    column = lax.broadcasted_iota(jnp.int32, (size, size), 1)
    last = jnp.where(row <= column, scores[cut:], NEG)
    return [scores[:cut], last] if cut else [last]


def over_blocks(causal, rows, length, body):
    def every():
        body(0, rows, length, False)

    if causal is None:
        every()
        return
    pl.when(causal == 0)(every)

    @pl.when(causal != 0)
    def _():
        for first in range(0, rows, CAUSAL):
            body(first, CAUSAL, first + CAUSAL, True)


def head_rows(group, heads, head):
    return pl.ds(pl.multiple_of((group * heads + head) * 64, 64), 64)


def attend(limit, causal, key_ref, query_t, value_t, ctx_t, lse_ref, key_tiles):
    length, width = key_ref.shape
    heads = key_tiles.shape[0]
    bias = key_bias(limit, length)

    def group_of(group, unused):
        for number in range(heads // 2):
            columns = block_of(group * (heads // 2) + number, 128)
            for head, tile in enumerate(pair_keys(key_ref[:, columns], bias, 1)):
                key_tiles[2 * number + head] = tile

        def body(first, queries, extent, diagonal):
            at = slice(first, first + queries)

            def scores_of(head):
                columns = block_of(group * (heads // 2) + head // 2, 128)
                tile = pair_queries(query_t[columns, at], head % 2, [1.0])
                return mm(key_tiles[head, :extent], tile)

            following = scores_of(0)
            for head in range(heads):
                parts = score_parts(following, diagonal)
                if head + 1 < heads:
                    following = scores_of(head + 1)
                top = jnp.max(parts[0], 0, keepdims=True)
                for more in parts[1:]:
                    top = jnp.maximum(top, jnp.max(more, 0, keepdims=True))
                parts = [jnp.exp(more - top) for more in parts]
                total = sum(jnp.sum(more, 0, keepdims=True) for more in parts)
                weights = jnp.concatenate([more.astype(bfloat) for more in parts], 0)
                mine = head_rows(group, heads, head)
                context = mm(value_t[mine, :extent], weights)
                ctx_t[mine, at] = (context * (1.0 / total)).astype(bfloat)
                lse_ref[pl.ds(group * heads + head, 1), at] = top + jnp.log(total)

        over_blocks(causal, query_t.shape[1], length, body)
        return 0

    lax.fori_loop(0, HEADS // heads, group_of, 0)


def attend_back(
    limit, causal, query_ref, key_ref, value_ref, query_t, key_t, grad_ctx, grad_ctx_t, lse_ref, dot_ref,
    grad_key, grad_value, grad_query_t, key_two, value_two,
):
    length, width = key_ref.shape
    bias = key_bias(limit, length)

    def pair(number, unused):
        columns = block_of(number, 128)
        for head, tile in enumerate(pair_keys(key_ref[:, columns], bias, 4)):
            key_two[head] = tile
        for head, tile in enumerate(pair_keys(value_ref[:, columns], 1.0, 3)):
            value_two[head] = tile

        def body(first, queries, extent, diagonal):
            at = slice(first, first + queries)

            def products_of(head):
                row = pl.ds(number * 2 + head, 1)
                constants = [1.0] + split_three(-lse_ref[row, at])
                scores = mm(
                    key_two[head, :extent], pair_queries(query_t[columns, at], head, constants)
                )
                constants = split_three(-dot_ref[row, at])
                grad_weights = mm(
                    value_two[head, :extent], pair_queries(grad_ctx_t[columns, at], head, constants)
                )
                return scores, grad_weights

            lane = lax.broadcasted_iota(jnp.int32, (queries, 128), 1)

            def both(tile):
                tile = tile.astype(single)
                return jnp.concatenate(
                    [
                        jnp.where(lane < 64, tile, 0.0).astype(bfloat),
                        jnp.where(lane < 64, 0.0, tile).astype(bfloat),
                    ],
                    0,
                )

            all_weights, all_grads = [], []
            following = products_of(0)
            for head in range(2):
                scores, grad_weights = following
                if head == 0:
                    following = products_of(1)
                weights = [jnp.exp(more) for more in score_parts(scores, diagonal)]
                weights = jnp.concatenate(weights, 0)
                grads = (weights * grad_weights).astype(bfloat)
                all_weights.append(weights.astype(bfloat))
                all_grads.append(grads)
                mine = head_rows(number, 2, head)
                grad_query = mm(key_t[mine, :extent], grads)
                grad_query_t[mine, at] = (grad_query * 0.125).astype(bfloat)
            for out, parts, other in (
                (grad_value, all_weights, grad_ctx),
                (grad_key, all_grads, query_ref),
            ):
                total = mm(jnp.concatenate(parts, 1), both(other[at, columns]))
                if first:
                    total = jnp.concatenate([out[:first, columns] + total[:first], total[first:]], 0)
                out[:extent, columns] = total

        over_blocks(causal, query_t.shape[1], length, body)
        return 0

    lax.fori_loop(0, width // 128, pair, 0)


def by_rows(length, body, init=0):
    def step(index, carry):
        return body(block_of(index, RB), carry)

    return lax.fori_loop(0, length // RB, step, init)


class Emitter:
    def __init__(self, table, target, stage, semaphores):
        self.table, self.target, self.stage, self.semaphores = table, target, stage, semaphores
        self.copies = []

    def chunk(self, number, first_piece, value):
        stage, half_rows = self.stage, self.target.shape[1]
        stage[number] = value.astype(bfloat)
        count = stage.shape[1] // half_rows
        per_piece = 128 // half_rows
        for part in range(count):
            copy = pltpu.make_async_copy(
                stage.at[number, pl.ds(part * half_rows, half_rows)],
                self.target.at[self.table[first_piece * per_piece + part]],
                self.semaphores.at[number * count + part],
            )
            copy.start()
            self.copies.append(copy)

    def wait(self):
        for copy in self.copies:
            copy.wait()


class Moves:
    def __init__(self, role):
        self.role = role
        self.loads = []
        self.stores = []
        self.waited = set()

    def load(self, dest, ways, semaphores):
        def begin(way):
            for number, (source, first, at, rows) in enumerate(way):
                if rows is not None:
                    source = source.at[pl.ds(first, rows)]
                    target = dest.at[pl.ds(at, rows)]
                else:
                    target = dest
                pltpu.make_async_copy(source, target, semaphores.at[number]).start()

        def finish(way):
            for number, (source, first, at, rows) in enumerate(way):
                if rows is not None:
                    source = source.at[pl.ds(first, rows)]
                    target = dest.at[pl.ds(at, rows)]
                else:
                    target = dest
                pltpu.make_async_copy(source, target, semaphores.at[number]).wait()

        def split(act):
            if len(ways) == 1:
                act(ways[0])
                return
            pl.when(self.role != 0)(lambda: act(ways[0]))
            pl.when(self.role == 0)(lambda: act(ways[1]))

        split(begin)
        self.loads.append((dest, lambda: split(finish)))

    def need(self, *refs):
        for number, (dest, finish) in enumerate(self.loads):
            if number not in self.waited and any(dest is ref for ref in refs):
                self.waited.add(number)
                finish()

    def rest(self):
        self.need(*[dest for dest, unused in self.loads])

    def place(self, source, target, semaphore):
        self.stores.append([source, target, semaphore, None])

    def put(self, *refs):
        for entry in self.stores:
            if entry[3] is None and any(entry[0] is ref for ref in refs):
                entry[3] = pltpu.make_async_copy(entry[0], entry[1], entry[2])
                entry[3].start()

    def finish(self):
        self.rest()
        self.put(*[entry[0] for entry in self.stores])
        for entry in self.stores:
            entry[3].wait()


def part(value, first, rows):
    return ("load", [[(value, first, 0, rows)]])


def whole(value):
    return ("load", [[(value, 0, 0, None)]])


def either(source_way, target_way):
    return ("load", [source_way, target_way])


def call(body, name, scal, active, ins, outs, scratch, aliases=(), limit=58):
    args, specs, scratch_all, plan = [scal], [SM], [], []
    counts = {"load": 0, "store": 0}

    def arg(value, spec):
        args.append(value)
        specs.append(spec)
        return len(args) - 1

    held = []
    for kind, value in ins:
        if kind == "load":
            ways = [[(arg(v, HB), first, at, rows) for v, first, at, rows in way] for way in value]
            v, first, at, rows = value[0][0]
            total = max(a + r for _, _, a, r in value[0]) if rows is not None else None
            shape = v.shape if rows is None else (total,) + v.shape[1:]
            held.append(("load", ways, shape, v.dtype, max(len(w) for w in ways)))
        else:
            held.append((kind, arg(value, SM if kind == "smem" else HB)))
    vmem, sems = [], []
    for entry in held:
        if entry[0] == "load":
            vmem.append(pltpu.VMEM(entry[2], entry[3]))
            sems.append(pltpu.SemaphoreType.DMA((entry[4],)))
    for kind, shape in outs:
        if kind == "store":
            vmem.append(pltpu.VMEM(shape.shape, shape.dtype))
            sems.append(pltpu.SemaphoreType.DMA((1,)))
    count_in, count_out = len(args), len(outs)

    def kernel(*refs):
        inputs, outputs = refs[:count_in], refs[count_in : count_in + count_out]
        rest = refs[count_in + count_out :]
        buffers, semaphores = list(rest[: len(vmem)]), list(rest[len(vmem) : len(vmem) + len(sems)])
        extra = rest[len(vmem) + len(sems) :]
        scal_ref = inputs[0]

        def run():
            moves = Moves(scal_ref[2])
            given = []
            for entry in held:
                if entry[0] == "load":
                    dest, semaphore = buffers.pop(0), semaphores.pop(0)
                    ways = [[(inputs[i], f, a, r) for i, f, a, r in way] for way in entry[1]]
                    moves.load(dest, ways, semaphore)
                    given.append(dest)
                else:
                    given.append(inputs[entry[1]])
            for (kind, unused), output in zip(outs, outputs):
                if kind == "store":
                    source, semaphore = buffers.pop(0), semaphores.pop(0)
                    moves.place(source, output, semaphore.at[0])
                    given.append(source)
                else:
                    given.append(output)
            body(moves, scal_ref, *given, *extra)
            moves.finish()

        if active is None:
            run()
        else:
            pl.when(scal_ref[2] == active)(run)

    pairs = {}
    for position, output in aliases:
        pairs[held[position][1]] = output
    return pl.pallas_call(
        kernel,
        in_specs=specs,
        out_specs=[HB] * count_out,
        out_shape=[shape for unused, shape in outs],
        scratch_shapes=vmem + sems + list(scratch),
        input_output_aliases=pairs,
        compiler_params=pltpu.CompilerParams(vmem_limit_bytes=62 << 20),
        name=name,
    )(*args)


def zero_rows(width):
    return (jnp.zeros((1, width), single),) * 3


def put_rows(ref, rows):
    for number, row in enumerate(rows):
        ref[number : number + 1] = row


def project_norm(length, ctx_t, weight, inner_ref, vec, resid_ref, out_ref):
    def body(rows, carry):
        branch = mm(ctx_t[:, rows].T, weight[...])
        resid = inner_ref[rows].astype(single) * vec[0:1] + branch
        resid_ref[rows] = resid
        out_ref[rows] = normed(resid)[0] * vec[1:2] + vec[2:3]
        return carry

    by_rows(length, body)


def self_forward(io, scal, x, weight, vec, outs, query_t, value_t, key_tiles, ready):
    query, key, value, ctx_t, lse, resid, out = outs
    length, width = x.shape
    io.need(x)
    ready()

    def body(rows, carry):
        tile = x[rows]
        for number, ref in enumerate((query, key, value)):
            ref[rows] = mm(tile, weight[width * number : width * (number + 1)]).astype(bfloat)
        query_t[:, rows] = (query[rows] * bfloat(0.125)).T
        value_t[:, rows] = value[rows].T
        return carry

    by_rows(length, body)
    io.put(query, key, value)
    attend(scal[0], scal[1], key, query_t, value_t, ctx_t, lse, key_tiles)
    io.put(ctx_t, lse)
    io.rest()
    project_norm(length, ctx_t, weight.at[3 * width :], x, vec, resid, out)


def self_forward_body(io, scal, x, weight, vec, *refs):
    self_forward(io, scal, x, weight, vec, refs[:7], *refs[7:], lambda: io.need(weight))


def placed_forward_body(where, io, scal, table, x, vec, *refs):
    sources, refs = refs[: len(where)], refs[len(where) :]
    outs, (weight, rest) = refs[:7], refs[7:9]
    query_t, value_t, key_tiles, semaphores = refs[9:]
    size = sources[0].shape[1]
    cut = weight.shape[0] // size

    for source, ranges in zip(sources, where):
        for start, stop, distance, other, first in ranges:

            def step(slot, unused):
                piece = table[distance, first + slot - start]
                at = piece * 2 + (scal[5] if other == 0 else 1 - scal[5])

                def move(target, place, semaphore):
                    place = pl.ds(pl.multiple_of(place * size, size), size)
                    pltpu.make_async_copy(source.at[slot], target.at[place], semaphore).start()

                pl.when((piece >= 0) & (at < cut))(lambda: move(weight, at, semaphores.at[0]))
                pl.when(at >= cut)(lambda: move(rest, at - cut, semaphores.at[1]))
                return 0

            lax.fori_loop(start, stop, step, 0)

    def ready():
        pltpu.make_async_copy(weight, weight, semaphores.at[0]).wait()
        io.put(weight)

    self_forward(io, scal, x, weight, vec, outs, query_t, value_t, key_tiles, ready)
    pltpu.make_async_copy(rest, rest, semaphores.at[1]).wait()
    io.put(rest)


def encoder_ff_body(
    io, scal, inner, up, down, cross, vec, activ, slope, resid, memory, sendout
):
    length, width = inner.shape
    io.rest()

    def body(rows, carry):
        tile = inner[rows]
        act, grad = gelu_parts(mm_nt(tile.astype(bfloat), up[...]))
        act = act.astype(bfloat)
        activ[rows] = act
        slope[rows] = grad.astype(bfloat)
        total = tile * vec[0:1] + mm(act, down[...])
        resid[rows] = total
        mem = (normed(total)[0] * vec[1:2] + vec[2:3]).astype(bfloat)
        memory[rows] = mem
        sendout[0, rows] = mm(mem, cross[:width]).astype(bfloat)
        sendout[1, rows] = mm(mem, cross[width:]).astype(bfloat)
        return carry

    by_rows(length, body)


def ff_back(length, emit, grad_branch, activ, slope, inner_low, up, down, grad_inner):
    def body(rows, carry):
        grad = mm_nt(grad_branch[rows], down[...]) * slope[rows].astype(single)
        grad = grad.astype(bfloat)
        slope[rows] = grad
        grad_inner[rows] += mm(grad, up[...])
        return carry

    by_rows(length, body)
    for number in range(activ.shape[1] // 512):
        columns = slice(number * 512, (number + 1) * 512)
        emit(0, number, mm_tn(slope[:, columns], inner_low[...]))
        emit(1, number, mm_tn(activ[:, columns], grad_branch[...]))


def branch_back(length, resid, grad_out, inner, vec, grad_branch, grad_inner, grad_vec):
    width = resid.shape[1]

    def body(rows, carry):
        grad_resid, grad_gain, grad_shift = norm_back(resid[rows], grad_out[rows], vec[1:2])
        grad_branch[rows] = grad_resid.astype(bfloat)
        grad_inner[rows] = grad_resid * vec[0:1]
        weigh = jnp.sum(grad_resid * inner[rows].astype(single), 0, keepdims=True)
        return (carry[0] + weigh, carry[1] + grad_gain, carry[2] + grad_shift)

    put_rows(grad_vec, by_rows(length, body, zero_rows(width)))


def ctx_back(length, grad_branch, weight, ctx_t, grad_ctx, grad_ctx_t, dot_ref):
    def body(rows, carry):
        grad_ctx[rows] = mm_nt(grad_branch[rows], weight[...]).astype(bfloat)
        grad_ctx_t[:, rows] = grad_ctx[rows].T
        for head in range(HEADS):
            mine = slice(64 * head, 64 * head + 64)
            product = grad_ctx_t[mine, rows].astype(single) * ctx_t[mine, rows].astype(single)
            dot_ref[head : head + 1, rows] = jnp.sum(product, 0, keepdims=True)
        return carry

    by_rows(length, body)


def middle_body(
    io, scal, inner, keys, cross, cross_vec, up, down, ff_vec, cotan,
    output, sendback, grad_inner, grads, grad_vec,
    query, query_t, ctx_t, lse, resid, after, activ, slope, low_rows, grad_branch, grad_after,
    grad_ctx, grad_ctx_t, dot_ref, key_t, value_t, grad_key, grad_value, grad_query_t,
    key_tiles, key_two, value_two,
):
    rows_here, width = inner.shape
    hidden = up.shape[0]
    io.need(inner, cross, keys)

    def project(rows, carry):
        query[rows] = mm(inner[rows].astype(bfloat), cross[:width]).astype(bfloat)
        query_t[:, rows] = (query[rows] * bfloat(0.125)).T
        return carry

    def turn(rows, carry):
        key_t[:, rows] = keys[0, rows].T
        value_t[:, rows] = keys[1, rows].T
        return carry

    by_rows(rows_here, project)
    by_rows(keys.shape[1], turn)
    attend(scal[4], None, keys.at[0], query_t, value_t, ctx_t, lse, key_tiles)
    io.rest()
    project_norm(rows_here, ctx_t, cross.at[width:], inner, cross_vec, resid, after)

    def feed(rows, carry):
        tile = after[rows]
        low_tile = tile.astype(bfloat)
        low_rows[rows] = low_tile
        act, grad = gelu_parts(mm_nt(low_tile, up[...]))
        act = act.astype(bfloat)
        activ[rows] = act
        slope[rows] = grad.astype(bfloat)
        total = tile * ff_vec[0:1] + mm(act, down[...])
        output[rows] = (normed(total)[0] * ff_vec[1:2] + ff_vec[2:3]).astype(bfloat)
        row = lax.broadcasted_iota(jnp.int32, tile.shape, 0) + rows.start
        grad_out = jnp.where(row < scal[3], cotan[rows].astype(single), 0.0)
        grad_resid, grad_gain, grad_shift = norm_back(total, grad_out, ff_vec[1:2])
        grad_branch[rows] = grad_resid.astype(bfloat)
        grad_after[rows] = grad_resid * ff_vec[0:1]
        weigh = jnp.sum(grad_resid * tile, 0, keepdims=True)
        return (carry[0] + weigh, carry[1] + grad_gain, carry[2] + grad_shift)

    put_rows(grad_vec.at[3:], by_rows(rows_here, feed, zero_rows(width)))
    io.put(output)

    def emit(which, number, value):
        first = 2 * width + which * hidden + number * 512
        grads[first : first + 512] = value.astype(bfloat)

    ff_back(rows_here, emit, grad_branch, activ, slope, low_rows, up, down, grad_after)
    branch_back(rows_here, resid, grad_after, inner, cross_vec, grad_branch, grad_inner, grad_vec)
    io.put(grad_vec)
    grads[width : 2 * width] = mm(ctx_t[...], grad_branch[...]).astype(bfloat)
    ctx_back(rows_here, grad_branch, cross.at[width:], ctx_t, grad_ctx, grad_ctx_t, dot_ref)
    attend_back(
        scal[4], None, query, keys.at[0], keys.at[1], query_t, key_t, grad_ctx, grad_ctx_t, lse, dot_ref,
        grad_key, grad_value, grad_query_t, key_two, value_two,
    )

    def send(rows, carry):
        sendback[0, rows] = (grad_key[rows] * 0.125).astype(bfloat)
        sendback[1, rows] = grad_value[rows].astype(bfloat)
        return carry

    by_rows(keys.shape[1], send)
    io.put(sendback)

    def last(rows, carry):
        grad_query = grad_query_t[:, rows].T
        grad_inner[rows] += mm_nt(grad_query, cross[:width])
        grad_ctx[rows] = grad_query
        return carry

    by_rows(rows_here, last)
    io.put(grad_inner)
    grads[:width] = mm_tn(inner[...].astype(bfloat), grad_ctx[...]).astype(bfloat)


def encoder_back_body(
    io, scal, table, own, received, memory, cross, inner, resid, activ, slope, up, down, vec,
    grad_inner, grad_vec, target,
    grad_mem, inner_low, grad_branch, stage, semaphores,
):
    length, width = inner.shape
    emit = Emitter(table, target, stage, semaphores)
    io.need(own, received, cross, inner)

    def body(rows, carry):
        for number in range(2):
            total = own[number, rows].astype(single) + received[number, rows].astype(single)
            own[number, rows] = total.astype(bfloat)
        grad_mem[rows] = mm_nt(own[0, rows], cross[:width]) + mm_nt(own[1, rows], cross[width:])
        inner_low[rows] = inner[rows].astype(bfloat)
        return carry

    by_rows(length, body)
    io.rest()
    branch_back(length, resid, grad_mem, inner, vec, grad_branch, grad_inner, grad_vec)
    io.put(grad_vec)

    def each(which, number, value):
        emit.chunk(2 * number + which, 24 + 16 * which + 4 * number, value)

    ff_back(length, each, grad_branch, activ, slope, inner_low, up, down, grad_inner)
    io.put(grad_inner)
    emit.chunk(8, 16, mm_tn(memory[...], own[0]))
    emit.chunk(9, 20, mm_tn(memory[...], own[1]))
    emit.wait()


def self_back_body(
    io, scal, table, x, weight, out_weight, vec, resid, query, key, value, ctx_t, lse, grad_out, held,
    grad_x, grad_vec, target,
    grad_branch, grad_ctx, grad_ctx_t, dot_ref, query_t, key_t, grad_key, grad_value, grad_query_t,
    key_two, value_two, stage, semaphores,
):
    length, width = x.shape
    emit = Emitter(table, target, stage, semaphores)
    io.need(resid, grad_out, x, vec)
    branch_back(length, resid, grad_out, x, vec, grad_branch, grad_x, grad_vec)
    io.put(grad_vec)
    io.need(ctx_t, out_weight)
    emit.chunk(3, 12, mm(ctx_t[...], grad_branch[...]))
    ctx_back(length, grad_branch, out_weight, ctx_t, grad_ctx, grad_ctx_t, dot_ref)
    io.rest()

    def body(rows, carry):
        query_t[:, rows] = (query[rows] * bfloat(0.125)).T
        key_t[:, rows] = key[rows].T
        return carry

    by_rows(length, body)
    attend_back(
        scal[0], scal[1], query, key, value, query_t, key_t, grad_ctx, grad_ctx_t, lse, dot_ref,
        grad_key, grad_value, grad_query_t, key_two, value_two,
    )

    def last(rows, carry):
        parts = (
            grad_query_t[:, rows].T,
            (grad_key[rows] * 0.125).astype(bfloat),
            grad_value[rows].astype(bfloat),
        )
        total = grad_x[rows]
        for number, low_grad in enumerate(parts):
            total += mm_nt(low_grad, weight[width * number : width * (number + 1)])
        grad_x[rows] = total
        grad_branch[rows], grad_ctx[rows], value[rows] = parts
        return carry

    by_rows(length, last)
    io.put(grad_x)
    for number, ref in enumerate((grad_branch, grad_ctx, value)):
        emit.chunk(number, 4 * number, mm_tn(x[...], ref[...]))
    emit.wait()


def merge_body(io, scal, table, own, other, held, target, stage, semaphores):
    emit = Emitter(table, target, stage, semaphores)
    io.rest()
    chunk = stage.shape[1]
    for number in range(own.shape[0] // chunk):
        rows = slice(number * chunk, (number + 1) * chunk)
        total = own[rows].astype(single) + other[rows].astype(single)
        emit.chunk(number, 16 + 4 * number, total)
    emit.wait()


RING = (0, 2, 4, 6, 7, 5, 3, 1)
LEAD = 8


def round_ring(value, step):
    count = len(RING)
    return lax.ppermute(value, "wide", [(RING[i], RING[(i + step) % count]) for i in range(count)])


def swapped(value):
    return lax.ppermute(value, "narrow", [(0, 1), (1, 0)])


def step_of(up, down, across):
    return lax.optimization_barrier((round_ring(up, 1), round_ring(down, -1), swapped(across)))


def join(*values):
    return jnp.concatenate(values, 0)


def ring_gather(own, tables):
    every, lead, half = own.shape[0], LEAD, LEAD // 2
    late = every - lead
    found = [([(0, every, 0, 0, 0)], own)]

    def ahead(value, far, near):
        ranges = [(0, lead, far, 0, 0)]
        if near is not None:
            ranges += [(lead, lead + late, near, 0, lead), (lead + late, lead + 2 * late, near, 1, lead)]
        found.append((ranges, value))

    up, down, across = step_of(own[:lead], own[:lead], own[lead:])
    found.append(([(0, late, 0, 1, lead)], across))
    ahead(up, 7, None)
    ahead(down, 1, None)
    pair = join(own[lead:], across)
    up, down, across = step_of(join(up, pair), join(down, pair), join(up, down, own[:half]))
    found.append(
        ([(0, lead, 7, 1, 0), (lead, 2 * lead, 1, 1, 0), (2 * lead, 2 * lead + half, 0, 1, 0)], across)
    )
    up, tables = lax.optimization_barrier((up, tables))
    ahead(up, 6, 7)
    ahead(down, 2, 1)
    up, down, across = step_of(up, down, join(up[:lead], down[:lead], own[half:lead]))
    found.append(
        ([(0, lead, 6, 1, 0), (lead, 2 * lead, 2, 1, 0), (2 * lead, 2 * lead + half, 0, 1, half)], across)
    )
    ahead(up, 5, 6)
    ahead(down, 3, 2)
    up, down, across = step_of(join(up[:half], up[lead:]), down[half:], join(up[:lead], down[:lead]))
    found.append(([(0, lead, 5, 1, 0), (lead, 2 * lead, 3, 1, 0)], across))
    for value, first, near in ((up, 0, 5), (down, half, 3)):
        ranges = [(0, half, 4, 0, first), (half, half + late, near, 0, lead)]
        found.append((ranges + [(half + late, half + 2 * late, near, 1, lead)], value))
    up, down, across = step_of(
        up[half : half + late], down[half + late :], join(up[:half], down[:half])
    )
    found.append(([(0, late, 4, 0, lead)], up))
    found.append(([(0, late, 4, 1, lead)], down))
    found.append(([(0, lead, 4, 1, 0)], across))
    return found, tables


def added(*values):
    return sum(value.astype(single) for value in values).astype(bfloat)


def ring_scatter(grads):
    lead, half = LEAD, LEAD // 2
    late = grads.shape[2] - lead

    def both(distance):
        return grads[distance, :, lead:].reshape((-1,) + grads.shape[3:])

    def mine(distance, start=0, stop=lead):
        return grads[distance, 0, start:stop]

    def other(distance, start=0, stop=lead):
        return grads[distance, 1, start:stop]

    up, down, across = step_of(grads[4, 0, lead:], grads[4, 1, lead:], other(4))
    first = added(mine(4), across)
    up = join(first[:half], added(up, grads[3, 0, lead:]), grads[3, 1, lead:])
    down = join(first[half:], grads[5, 0, lead:], added(down, grads[5, 1, lead:]))
    up, down, across = step_of(up, down, join(other(3), other(5)))
    up = join(
        added(mine(3, 0, half), across[:half], up[:half]),
        added(mine(3, half), across[half:lead]),
        added(up[half:], both(2)),
    )
    down = join(
        added(mine(5, 0, half), across[lead : lead + half]),
        added(mine(5, half), across[lead + half :], down[:half]),
        added(down[half:], both(6)),
    )
    up, down, across = step_of(up, down, join(other(2), other(6), other(0, 0, half)))
    nearest = [across[2 * lead :]]
    up = join(added(mine(2), across[:lead], up[:lead]), added(up[lead:], both(1)))
    down = join(added(mine(6), across[lead : 2 * lead], down[:lead]), added(down[lead:], both(7)))
    up, down, across = step_of(up, down, join(other(1), other(7), other(0, half)))
    nearest.append(across[2 * lead :])
    total = sum(value.astype(single) for value in (both(0), up[lead:], down[lead:]))
    up, down, across = step_of(
        added(mine(1), across[:lead], up[:lead]),
        added(mine(7), across[lead : 2 * lead], down[:lead]),
        total[late:].astype(bfloat),
    )
    first = sum(value.astype(single) for value in (mine(0), join(*nearest), up, down))
    return join(first, total[:late] + across.astype(single))


def shaped(*shape, dtype=single):
    return jax.ShapeDtypeStruct(shape, dtype)


def low(*shape):
    return jax.ShapeDtypeStruct(shape, bfloat)


def low_vm(*shape):
    return pltpu.VMEM(shape, bfloat)


def full_vm(*shape):
    return pltpu.VMEM(shape, single)


def sum_over(value, axis):
    size = lax.axis_size(axis)
    bit = 1
    while bit < size:
        value = value + lax.ppermute(value, axis, [(i, i ^ bit) for i in range(size)])
        bit *= 2
    return value


def adam(weight, gradient, first, second, step_rate, decay_rate):
    first_new = beta_one * first + (1.0 - beta_one) * gradient
    second_new = beta_two * second + (1.0 - beta_two) * gradient * gradient
    first_hat = first_new / (1.0 - beta_one**STEP)
    second_hat = second_new / (1.0 - beta_two**STEP)
    weight_new = weight - step_rate * (
        first_hat / (jnp.sqrt(second_hat) + eps_adam) + decay_rate * weight
    )
    return (weight_new, first_new, second_new)


def on_device(
    stream, cotangent, lengths, owners, master, moment_one, moment_two, vec_master, vec_one, vec_two
):
    narrow_size = lax.axis_size("narrow")
    wide_size = lax.axis_size("wide")
    owner_row = owners[0]
    capacity = master.shape[1]
    half_rows = master.shape[2]
    width = master.shape[3]
    count = owner_row.shape[0]
    counter = jnp.arange(count)
    same = owner_row[:, None] == owner_row[None, :]
    earlier = counter[None, :] < counter[:, None]
    ranks = jnp.sum((same & earlier).astype(jnp.int32), 1)
    on_ring = wide_size == len(RING) and narrow_size == 2 and capacity > LEAD
    wide_at, narrow_at = lax.axis_index("wide"), lax.axis_index("narrow")
    self_rows, rest_rows = 4 * width, count * half_rows * narrow_size - 4 * width
    is_source = lax.axis_index("half") == 0
    x = stream[0, 0]
    length = x.shape[0]
    some = length // 2
    source_len, target_len = lengths[0, 0], lengths[1, 0]
    flag = is_source.astype(jnp.int32)
    scal = jnp.stack(
        [
            jnp.where(is_source, source_len, target_len),
            1 - flag,
            flag,
            jnp.where(is_source, target_len - some, target_len),
            source_len,
            narrow_at,
        ]
    ).astype(jnp.int32)
    own = master[0].astype(bfloat)
    if on_ring:
        turned = [RING.index(i) for i in range(wide_size)]
        position = jnp.array(turned)[wide_at]
        owner_ring = jnp.array(turned)[owner_row]
        distance = (owner_ring - position) % wide_size
        halves = jnp.arange(narrow_size)[None, :] ^ narrow_at
        table = ((distance[:, None] * 2 + halves) * capacity + ranks[:, None]).reshape(-1)
        slot_of = distance * capacity + ranks
        hit = slot_of[None, :] == jnp.arange(wide_size * capacity)[:, None]
        pieces = jnp.sum(hit.astype(jnp.int32) * (counter + 1)[None, :], 1) - 1
        pieces = pieces.reshape(wide_size, capacity).astype(jnp.int32)
        found, (pieces, table, scal) = ring_gather(own, (pieces, table.astype(jnp.int32), scal))
    else:
        places = (
            owner_row[:, None] * narrow_size + jnp.arange(narrow_size)[None, :]
        ) * capacity + ranks[:, None]
        table = places.reshape(-1)
        gathered = lax.all_gather(own, ("wide", "narrow"), axis=0, tiled=True)
        weight = jnp.take(gathered, table, axis=0).reshape(-1, width)
        weight, rest = weight[:self_rows], weight[self_rows:]
    table = table.astype(jnp.int32)
    hidden = (rest_rows - 2 * width) // 2
    self_vec = whole(jnp.where(is_source, vec_master[0:3], vec_master[6:9]))
    cross_vec, ff_vec = whole(vec_master[9:12]), whole(vec_master[12:15])
    memory_vec = whole(vec_master[3:6])
    slots = low(capacity * wide_size * narrow_size, half_rows, width)

    def stage_of(chunks):
        return [
            low_vm(chunks, 512, width),
            pltpu.SemaphoreType.DMA((chunks * 512 // half_rows,)),
        ]

    def store(*shape, dtype=single):
        return ("store", shaped(*shape, dtype=dtype))

    low_out = partial(store, dtype=bfloat)
    two, four = low_vm(2, length, 128), low_vm(4, length, 128)
    down_half, up_half = [(1, 0)], [(0, 1)]

    forward_outs = (
        [low_out(length, width)] * 3
        + [low_out(width, length), store(HEADS, length)]
        + [store(length, width)] * 2
    )
    forward_scratch = [low_vm(width, length), low_vm(width, length), four]
    if on_ring:
        *forward, weight, rest = call(
            partial(placed_forward_body, [where for where, unused in found]),
            "self_forward",
            scal,
            None,
            [("smem", pieces), whole(x), self_vec] + [("hbm", value) for unused, value in found],
            forward_outs + [low_out(self_rows, width), low_out(rest_rows, width)],
            forward_scratch + [pltpu.SemaphoreType.DMA((2,))],
        )
    else:
        forward = call(
            self_forward_body,
            "self_forward",
            scal,
            None,
            [whole(x), whole(weight), self_vec],
            forward_outs,
            forward_scratch,
        )
    query, key, value, ctx_t, lse, resid, inner = forward
    rest_other = lax.ppermute(rest, "half", down_half)
    cross_w = part(rest, 0, 2 * width)
    up_w = part(rest, 2 * width, hidden)
    down_w = part(rest, 2 * width + hidden, hidden)
    inner_other = lax.ppermute(inner[some:], "half", down_half)
    activ, slope, ff_resid, memory, sendout = call(
        encoder_ff_body,
        "encoder_ff",
        scal,
        1,
        [whole(inner), up_w, down_w, cross_w, memory_vec],
        [low_out(length, hidden)] * 2
        + [store(length, width), low_out(length, width), low_out(2, length, width)],
        [],
    )
    sendout_other = lax.ppermute(sendout, "half", up_half)

    def shared(first, rows):
        return either([(rest_other, first, 0, rows)], [(rest, first, 0, rows)])

    mid_inner = either([(inner_other, 0, 0, some)], [(inner, 0, 0, some)])
    keys = either([(sendout, 0, 0, None)], [(sendout_other, 0, 0, None)])
    cotan = cotangent[0]
    output, sendback, grad_one, grad_rest, grad_middle_vec = call(
        middle_body,
        "decoder_middle",
        scal,
        None,
        [
            mid_inner,
            keys,
            shared(0, 2 * width),
            cross_vec,
            shared(2 * width, hidden),
            shared(2 * width + hidden, hidden),
            ff_vec,
            either([(cotan, some, 0, some)], [(cotan, 0, 0, some)]),
        ],
        [
            low_out(some, width),
            low_out(2, length, width),
            store(some, width),
            low_out(rest_rows, width),
            store(6, width),
        ],
        [low_vm(some, width), low_vm(width, some), low_vm(width, some), full_vm(HEADS, some)]
        + [full_vm(some, width), full_vm(some, width), low_vm(some, hidden), low_vm(some, hidden)]
        + [low_vm(some, width), low_vm(some, width), full_vm(some, width)]
        + [low_vm(some, width), low_vm(width, some), full_vm(HEADS, some)]
        + [low_vm(width, length), low_vm(width, length)]
        + [full_vm(length, width), full_vm(length, width), low_vm(width, some), four, two, two],
    )
    sendback_other = lax.ppermute(sendback, "half", down_half)
    grad_one_other = lax.ppermute(grad_one, "half", up_half)
    grad_rest_other = lax.ppermute(grad_rest, "half", up_half)
    output_other = lax.ppermute(output, "half", up_half)
    grad_inner, grad_memory_vec, target = call(
        encoder_back_body,
        "encoder_back",
        scal,
        1,
        [
            ("smem", table),
            whole(sendback),
            whole(sendback_other),
            whole(memory),
            cross_w,
            whole(inner),
            whole(ff_resid),
            whole(activ),
            whole(slope),
            up_w,
            down_w,
            memory_vec,
        ],
        [store(length, width), store(3, width), ("hbm", slots)],
        [full_vm(length, width), low_vm(length, width), low_vm(length, width)] + stage_of(10),
    )
    back_scratch = (
        [low_vm(length, width), low_vm(length, width), low_vm(width, length), full_vm(HEADS, length)]
        + [low_vm(width, length), low_vm(width, length)]
        + [full_vm(length, width), full_vm(length, width), low_vm(width, length), two, two]
    )
    grad_x, grad_self_vec, target = call(
        self_back_body,
        "self_back",
        scal,
        None,
        [
            ("smem", table),
            whole(x),
            part(weight, 0, 3 * width),
            part(weight, 3 * width, width),
            self_vec,
            whole(resid),
            whole(query),
            whole(key),
            whole(value),
            whole(ctx_t),
            whole(lse),
            either(
                [(grad_inner, 0, 0, length)],
                [(grad_one, 0, 0, some), (grad_one_other, 0, some, some)],
            ),
            ("hbm", target),
        ],
        [store(length, width), store(3, width), ("hbm", slots)],
        back_scratch + stage_of(4),
        [(12, 2)],
    )
    (target,) = call(
        merge_body,
        "merge",
        scal,
        0,
        [
            ("smem", table),
            whole(grad_rest),
            whole(grad_rest_other),
            ("hbm", target),
        ],
        [("hbm", slots)],
        stage_of(10),
        [(3, 0)],
    )
    vec_grads = jnp.concatenate(
        [
            jnp.where(is_source, grad_self_vec, 0.0),
            jnp.where(is_source, grad_memory_vec, 0.0),
            jnp.where(is_source, 0.0, grad_self_vec),
            grad_middle_vec,
        ],
        0,
    )
    for axis in ("narrow", "wide"):
        vec_grads = sum_over(vec_grads, axis)
    if on_ring:
        mine = ring_scatter(target.reshape(wide_size, 2, capacity, half_rows, width))
    else:
        mine = lax.psum_scatter(target, ("wide", "narrow"), scatter_dimension=0, tiled=True)
    mine, vec_grads = lax.optimization_barrier((mine, vec_grads))
    vec_grads = sum_over(vec_grads, "half")
    used = jnp.sum((owner_row == wide_at).astype(jnp.int32))
    mine = jnp.where((jnp.arange(capacity) < used)[:, None, None], mine.astype(single), 0.0)
    new_weight, new_first, new_second = adam(
        master[0], mine, moment_one[0], moment_two[0], rate_matrix, decay_matrix
    )
    vec_weight, vec_first, vec_second = adam(
        vec_master, vec_grads, vec_one, vec_two, rate_vector, 0.0
    )
    output = jnp.concatenate([output, output_other], 0)
    return (
        jnp.where(is_source, memory, output)[None, None],
        grad_x[None, None],
        new_first[None],
        new_second[None],
        new_weight[None],
        new_weight.astype(bfloat)[None],
        vec_first,
        vec_second,
        vec_weight,
    )


def solution(mesh):
    in_specs = (
        P("half", ("wide", "narrow"), None, None),
        P(("wide", "narrow"), None, None),
        P(None, ("wide", "narrow")),
        P("half", None),
        P("half", "wide", "narrow", None),
        P("half", "wide", "narrow", None),
        P("half", "wide", "narrow", None),
        P(),
        P(),
        P(),
    )
    out_specs = (
        P("half", ("wide", "narrow"), None, None),
        P("half", ("wide", "narrow"), None, None),
        P("half", "wide", "narrow", None),
        P("half", "wide", "narrow", None),
        P("half", "wide", "narrow", None),
        P("half", "wide", "narrow", None),
        P(),
        P(),
        P(),
    )
    return jax.shard_map(
        on_device, mesh=mesh, in_specs=in_specs, out_specs=out_specs, check_vma=False
    )
```

```python
import math
from functools import partial

import jax
import jax.numpy as jnp
from jax import lax
from jax.experimental import pallas as pl
from jax.experimental.pallas import tpu as pltpu
from jax.sharding import PartitionSpec as P

HEADS = 8
STEP = 5
CAUSAL = 512
RB = 1024
NEG = -1e30

eps_norm = 1e-05
beta_one = 0.5
beta_two = 0.5
rate_matrix = 0.05
rate_vector = 0.3
decay_matrix = 0.01
eps_adam = 1e-08
bfloat = jnp.bfloat16
single = jnp.float32
VM = pl.BlockSpec(memory_space=pltpu.VMEM)
SM = pl.BlockSpec(memory_space=pltpu.SMEM)
HB = pl.BlockSpec(memory_space=pl.ANY)


def mm(left, right):
    return jnp.dot(left, right, preferred_element_type=single)


def mm_tn(left, right):
    return lax.dot_general(left, right, (((0,), (0,)), ((), ())), preferred_element_type=single)


def mm_nt(left, right):
    return lax.dot_general(left, right, (((1,), (1,)), ((), ())), preferred_element_type=single)


def block_of(index, size):
    return pl.ds(pl.multiple_of(index * size, size), size)


def normed(resid):
    center = resid - jnp.mean(resid, -1, keepdims=True)
    spread = jnp.mean(center * center, -1, keepdims=True)
    rstd = lax.rsqrt(spread + eps_norm)
    return center * rstd, rstd


def norm_back(resid, grad, gain):
    hat, rstd = normed(resid)
    grad_hat = grad * gain
    grad_resid = rstd * (
        grad_hat
        - jnp.mean(grad_hat, -1, keepdims=True)
        - hat * jnp.mean(grad_hat * hat, -1, keepdims=True)
    )
    return grad_resid, jnp.sum(grad * hat, 0, keepdims=True), jnp.sum(grad, 0, keepdims=True)


def gelu_parts(pre_act):
    half = 0.5 * (1.0 + lax.erf(pre_act * math.sqrt(0.5)))
    slope = half + pre_act * (jnp.exp(-0.5 * pre_act * pre_act) * (1.0 / math.sqrt(2.0 * math.pi)))
    return pre_act * half, slope


def pair_keys(tile, first_extra, ones):
    rows = tile.shape[0]
    lane = lax.broadcasted_iota(jnp.int32, (rows, 128), 1)
    wide_tile = tile.astype(single)
    out = []
    for head in range(2):
        at = lane - (64 - 64 * head)
        extra = jnp.where(at == 0, first_extra, jnp.where((at > 0) & (at < ones), 1.0, 0.0))
        mine = (lane < 64) if head == 0 else (lane >= 64)
        out.append(jnp.where(mine, wide_tile, extra).astype(bfloat))
    return out


def pair_queries(tile, head, extra_rows):
    mine = tile[64 * head : 64 * head + 64]
    row = lax.broadcasted_iota(jnp.int32, mine.shape, 0)
    extra = jnp.zeros(mine.shape, single)
    for number, value in enumerate(extra_rows):
        extra = jnp.where(row == number, value, extra)
    extra = extra.astype(bfloat)
    return jnp.concatenate([mine, extra] if head == 0 else [extra, mine], 0)


def pack_rows(target, first, value):
    rows = value.shape[0]
    for number, one in enumerate(split_three(value)):
        target[first + number * rows : first + (number + 1) * rows] = one.astype(bfloat)


def unpack_rows(packed, rows):
    high, middle, rest = (packed[n * rows : (n + 1) * rows].astype(single) for n in range(3))
    return (high + middle) + rest


def split_three(value):
    high = value.astype(bfloat).astype(single)
    rest = value - high
    middle = rest.astype(bfloat).astype(single)
    return [high, middle, rest - middle]


def key_bias(limit, rows):
    row = lax.broadcasted_iota(jnp.int32, (rows, 128), 0)
    return jnp.where(row < limit, 0.0, NEG)


def score_parts(scores, diagonal):
    if not diagonal:
        return [scores]
    size = scores.shape[1]
    cut = scores.shape[0] - size
    row = lax.broadcasted_iota(jnp.int32, (size, size), 0)
    column = lax.broadcasted_iota(jnp.int32, (size, size), 1)
    last = jnp.where(row <= column, scores[cut:], NEG)
    return [scores[:cut], last] if cut else [last]


def over_blocks(causal, rows, length, body):
    def every():
        body(0, rows, length, False)

    if causal is None:
        every()
        return
    pl.when(causal == 0)(every)

    @pl.when(causal != 0)
    def _():
        for first in range(0, rows, CAUSAL):
            body(first, CAUSAL, first + CAUSAL, True)


def head_rows(group, heads, head):
    return pl.ds(pl.multiple_of((group * heads + head) * 64, 64), 64)


def attend(limit, causal, key_ref, query_t, value_t, ctx_t, lse_ref, key_tiles):
    length, width = key_ref.shape
    heads = key_tiles.shape[0]
    bias = key_bias(limit, length)

    def group_of(group, unused):
        for number in range(heads // 2):
            columns = block_of(group * (heads // 2) + number, 128)
            for head, tile in enumerate(pair_keys(key_ref[:, columns], bias, 1)):
                key_tiles[2 * number + head] = tile

        def body(first, queries, extent, diagonal):
            at = slice(first, first + queries)

            def scores_of(head):
                columns = block_of(group * (heads // 2) + head // 2, 128)
                tile = pair_queries(query_t[columns, at], head % 2, [1.0])
                return mm(key_tiles[head, :extent], tile)

            following = scores_of(0)
            for head in range(heads):
                parts = score_parts(following, diagonal)
                if head + 1 < heads:
                    following = scores_of(head + 1)
                top = jnp.max(parts[0], 0, keepdims=True)
                for more in parts[1:]:
                    top = jnp.maximum(top, jnp.max(more, 0, keepdims=True))
                parts = [jnp.exp(more - top) for more in parts]
                total = sum(jnp.sum(more, 0, keepdims=True) for more in parts)
                weights = jnp.concatenate([more.astype(bfloat) for more in parts], 0)
                mine = head_rows(group, heads, head)
                context = mm(value_t[mine, :extent], weights)
                ctx_t[mine, at] = (context * (1.0 / total)).astype(bfloat)
                lse_ref[pl.ds(group * heads + head, 1), at] = top + jnp.log(total)

        over_blocks(causal, query_t.shape[1], length, body)
        return 0

    lax.fori_loop(0, HEADS // heads, group_of, 0)


def attend_back(
    limit, causal, query_ref, key_ref, value_ref, query_t, key_t, grad_ctx, grad_ctx_t, lse_ref, dot_ref,
    grad_key, grad_value, grad_query_t, key_two, value_two,
):
    length, width = key_ref.shape
    bias = key_bias(limit, length)

    def pair(number, unused):
        columns = block_of(number, 128)
        for head, tile in enumerate(pair_keys(key_ref[:, columns], bias, 4)):
            key_two[head] = tile
        for head, tile in enumerate(pair_keys(value_ref[:, columns], 1.0, 3)):
            value_two[head] = tile

        def body(first, queries, extent, diagonal):
            at = slice(first, first + queries)

            def products_of(head):
                row = pl.ds(number * 2 + head, 1)
                constants = [1.0] + split_three(-lse_ref[row, at])
                scores = mm(
                    key_two[head, :extent], pair_queries(query_t[columns, at], head, constants)
                )
                constants = split_three(-dot_ref[row, at])
                grad_weights = mm(
                    value_two[head, :extent], pair_queries(grad_ctx_t[columns, at], head, constants)
                )
                return scores, grad_weights

            lane = lax.broadcasted_iota(jnp.int32, (queries, 128), 1)

            def both(tile):
                tile = tile.astype(single)
                return jnp.concatenate(
                    [
                        jnp.where(lane < 64, tile, 0.0).astype(bfloat),
                        jnp.where(lane < 64, 0.0, tile).astype(bfloat),
                    ],
                    0,
                )

            all_weights, all_grads = [], []
            following = products_of(0)
            for head in range(2):
                scores, grad_weights = following
                if head == 0:
                    following = products_of(1)
                weights = [jnp.exp(more) for more in score_parts(scores, diagonal)]
                weights = jnp.concatenate(weights, 0)
                grads = (weights * grad_weights).astype(bfloat)
                all_weights.append(weights.astype(bfloat))
                all_grads.append(grads)
                mine = head_rows(number, 2, head)
                grad_query = mm(key_t[mine, :extent], grads)
                grad_query_t[mine, at] = (grad_query * 0.125).astype(bfloat)
            for out, parts, other in (
                (grad_value, all_weights, grad_ctx),
                (grad_key, all_grads, query_ref),
            ):
                total = mm(jnp.concatenate(parts, 1), both(other[at, columns]))
                if first:
                    total = jnp.concatenate([out[:first, columns] + total[:first], total[first:]], 0)
                out[:extent, columns] = total

        over_blocks(causal, query_t.shape[1], length, body)
        return 0

    lax.fori_loop(0, width // 128, pair, 0)


def by_rows(length, body, init=0):
    if length <= RB:
        return body(pl.ds(0, length), init)

    def step(index, carry):
        return body(block_of(index, RB), carry)

    return lax.fori_loop(0, length // RB, step, init)


class Emitter:
    def __init__(self, table, target, stage, semaphores):
        self.table, self.target, self.stage, self.semaphores = table, target, stage, semaphores
        self.copies = []

    def chunk(self, number, first_piece, value):
        stage, half_rows = self.stage, self.target.shape[1]
        stage[number] = value.astype(bfloat)
        count = stage.shape[1] // half_rows
        per_piece = 128 // half_rows
        for part in range(count):
            copy = pltpu.make_async_copy(
                stage.at[number, pl.ds(part * half_rows, half_rows)],
                self.target.at[self.table[first_piece * per_piece + part]],
                self.semaphores.at[number * count + part],
            )
            copy.start()
            self.copies.append(copy)

    def wait(self):
        for copy in self.copies:
            copy.wait()


class Moves:
    def __init__(self, role, spare):
        self.role = role
        self.spare = spare
        self.some = []
        self.loads = []
        self.stores = []
        self.begun = set()
        self.waited = set()

    def load(self, dest, ways, semaphores):
        def each(way, act):
            for number, (source, first, at, rows) in enumerate(way):
                target = dest
                if rows is not None:
                    source = source.at[pl.ds(first, rows)]
                    target = dest.at[pl.ds(at, rows)]
                act(pltpu.make_async_copy(source, target, semaphores.at[number]))

        def split(act):
            if len(ways) == 1:
                each(ways[0], act)
                return
            pl.when(self.role != 0)(lambda: each(ways[0], act))
            pl.when(self.role == 0)(lambda: each(ways[1], act))

        self.loads.append((dest, split))

    def begin(self, *refs):
        for number, (dest, split) in enumerate(self.loads):
            if number not in self.begun and any(dest is ref for ref in refs):
                self.begun.add(number)
                split(lambda copy: copy.start())

    def need(self, *refs):
        self.begin(*refs)
        for number, (dest, split) in enumerate(self.loads):
            if number not in self.waited and any(dest is ref for ref in refs):
                self.waited.add(number)
                split(lambda copy: copy.wait())

    def follow(self, *refs):
        self.begin(*refs)
        for dest, unused in self.loads:
            self.begin(dest)

    def rest(self):
        self.follow()
        self.need(*[dest for dest, unused in self.loads])

    def place(self, source, target, semaphores):
        self.stores.append((source, target, semaphores, []))

    def put(self, *refs):
        for source, target, semaphores, copies in self.stores:
            if not copies and any(source is ref for ref in refs):
                copies.append(pltpu.make_async_copy(source, target, semaphores.at[0]))
                copies[0].start()

    def put_rows(self, ref, first, rows):
        for source, target, semaphores, copies in self.stores:
            if source is ref:
                at = pl.ds(first, rows)
                copies.append(
                    pltpu.make_async_copy(source.at[at], target.at[at], semaphores.at[len(copies)])
                )
                copies[-1].start()

    def put_if(self, wanted, source, target):
        copy = pltpu.make_async_copy(source, target, self.spare.at[len(self.some)])
        pl.when(wanted)(copy.start)
        self.some.append((wanted, copy))

    def finish(self):
        self.rest()
        self.put(*[entry[0] for entry in self.stores])
        for entry in self.stores:
            for copy in entry[3]:
                copy.wait()
        for wanted, copy in self.some:
            pl.when(wanted)(copy.wait)


def part(value, first, rows):
    return ("load", [[(value, first, 0, rows)]])


def whole(value):
    return ("load", [[(value, 0, 0, None)]])


def either(source_way, target_way):
    return ("load", [source_way, target_way])


def call(body, name, scal, active, ins, outs, scratch, aliases=(), limit=58):
    args, specs, scratch_all, plan = [scal], [SM], [], []
    counts = {"load": 0, "store": 0}

    def arg(value, spec):
        args.append(value)
        specs.append(spec)
        return len(args) - 1

    held = []
    for kind, value in ins:
        if kind == "load":
            ways = [[(arg(v, HB), first, at, rows) for v, first, at, rows in way] for way in value]
            way = value[0] or value[1]
            v, first, at, rows = way[0]
            total = max(a + r for _, _, a, r in way) if rows is not None else None
            shape = v.shape if rows is None else (total,) + v.shape[1:]
            held.append(("load", ways, shape, v.dtype, max(len(w) for w in ways)))
        else:
            held.append((kind, arg(value, SM if kind == "smem" else HB)))
    vmem, sems = [], []
    for entry in held:
        if entry[0] == "load":
            vmem.append(pltpu.VMEM(entry[2], entry[3]))
            sems.append(pltpu.SemaphoreType.DMA((entry[4],)))
    for kind, shape in outs:
        if kind == "store":
            vmem.append(pltpu.VMEM(shape.shape, shape.dtype))
            sems.append(pltpu.SemaphoreType.DMA((6,)))
    count_in, count_out = len(args), len(outs)

    def kernel(*refs):
        inputs, outputs = refs[:count_in], refs[count_in : count_in + count_out]
        rest = refs[count_in + count_out :]
        buffers, semaphores = list(rest[: len(vmem)]), list(rest[len(vmem) : len(vmem) + len(sems)])
        spare, *extra = rest[len(vmem) + len(sems) :]
        scal_ref = inputs[0]

        def run():
            moves = Moves(scal_ref[2], spare)
            given = []
            for entry in held:
                if entry[0] == "load":
                    dest, semaphore = buffers.pop(0), semaphores.pop(0)
                    ways = [[(inputs[i], f, a, r) for i, f, a, r in way] for way in entry[1]]
                    moves.load(dest, ways, semaphore)
                    given.append(dest)
                else:
                    given.append(inputs[entry[1]])
            for (kind, unused), output in zip(outs, outputs):
                if kind == "store":
                    source, semaphore = buffers.pop(0), semaphores.pop(0)
                    moves.place(source, output, semaphore)
                    given.append(source)
                else:
                    given.append(output)
            body(moves, scal_ref, *given, *extra)
            moves.finish()

        if active is None:
            run()
        else:
            pl.when(scal_ref[2] == active)(run)

    pairs = {}
    for position, output in aliases:
        pairs[held[position][1]] = output
    return pl.pallas_call(
        kernel,
        in_specs=specs,
        out_specs=[HB] * count_out,
        out_shape=[shape for unused, shape in outs],
        scratch_shapes=vmem + sems + [pltpu.SemaphoreType.DMA((2,))] + list(scratch),
        input_output_aliases=pairs,
        compiler_params=pltpu.CompilerParams(vmem_limit_bytes=62 << 20),
        name=name,
    )(*args)


def halves_of(length):
    return [pl.ds(0, length // 2), pl.ds(length // 2, length // 2)]


def zero_rows(width):
    return (jnp.zeros((1, width), single),) * 3


def put_rows(ref, rows):
    for number, row in enumerate(rows):
        ref[number : number + 1] = row


def project_norm(io, length, ctx_t, weight, inner_ref, vec, resid_ref, out_ref):
    for rows in halves_of(length):
        branch = mm(ctx_t[:, rows].T, weight[...])
        resid = inner_ref[rows].astype(single) * vec[0:1] + branch
        resid_ref[rows] = resid
        out_ref[rows] = normed(resid)[0] * vec[1:2] + vec[2:3]
        for ref in (resid_ref, out_ref):
            io.put_rows(ref, rows.start, rows.size)


def self_forward(io, scal, x, weight, vec, outs, query_t, value_t, key_tiles, packed, ready):
    query, key, value, ctx_t, lse, resid, out, swap = outs
    length, width = x.shape
    some = length // 2
    io.begin(x)
    ready()
    io.need(x)
    io.follow()

    def body(rows, carry):
        tile = x[rows]
        for number, ref in enumerate((query, key, value)):
            ref[rows] = mm(tile, weight[width * number : width * (number + 1)]).astype(bfloat)
        query_t[:, rows] = (query[rows] * bfloat(0.125)).T
        value_t[:, rows] = value[rows].T
        return carry

    by_rows(length, body)
    io.put(query, key, value)
    attend(scal[0], scal[1], key, query_t, value_t, ctx_t, lse, key_tiles)
    io.put(ctx_t, lse)
    io.rest()
    project_norm(io, length, ctx_t, weight.at[3 * width :], x, vec, resid, out)

    pl.when(scal[2] == 0)(lambda: pack_rows(packed, 0, out[some:]))
    io.put_if(scal[2] == 0, packed, swap.at[pl.ds(0, 3 * some)])


def self_forward_body(io, scal, x, weight, vec, *refs):
    io.begin(x)
    self_forward(io, scal, x, weight, vec, refs[:8], *refs[8:], lambda: io.need(weight))


def placed_forward_body(where, io, scal, table, x, vec, *refs):
    sources, refs = refs[: len(where)], refs[len(where) :]
    outs, (weight, rest) = refs[:8], refs[8:10]
    query_t, value_t, key_tiles, packed, semaphores = refs[10:]
    size = sources[0].shape[1]
    cut = weight.shape[0] // size
    io.begin(x)

    for source, ranges in zip(sources, where):
        for start, stop, distance, other, first in ranges:

            def step(slot, unused):
                piece = table[distance, first + slot - start]
                at = piece * 2 + (scal[5] if other == 0 else 1 - scal[5])

                def move(target, place, semaphore):
                    place = pl.ds(pl.multiple_of(place * size, size), size)
                    pltpu.make_async_copy(source.at[slot], target.at[place], semaphore).start()

                pl.when((piece >= 0) & (at < cut))(lambda: move(weight, at, semaphores.at[0]))
                pl.when(at >= cut)(lambda: move(rest, at - cut, semaphores.at[1]))
                return 0

            lax.fori_loop(start, stop, step, 0)

    def ready():
        pltpu.make_async_copy(weight, weight, semaphores.at[0]).wait()
        io.put(weight)

    self_forward(io, scal, x, weight, vec, outs, query_t, value_t, key_tiles, packed, ready)
    pltpu.make_async_copy(rest, rest, semaphores.at[1]).wait()
    io.put(rest)


def encoder_ff_body(
    io, scal, inner, up, down, cross, vec, held, activ, slope, resid, memory, swap, sendout
):
    length, width = inner.shape
    io.need(inner, up)
    io.follow(down)
    for rows in [pl.ds(0, length)]:
        act, grad = gelu_parts(mm_nt(inner[rows].astype(bfloat), up[...]))
        activ[rows] = act.astype(bfloat)
        slope[rows] = grad.astype(bfloat)
        for ref in (activ, slope):
            io.put_rows(ref, rows.start, rows.size)
    io.rest()
    for rows in [pl.ds(0, length)]:
        total = inner[rows] * vec[0:1] + mm(activ[rows], down[...])
        resid[rows] = total
        mem = (normed(total)[0] * vec[1:2] + vec[2:3]).astype(bfloat)
        memory[rows] = mem
        sendout[rows] = mm(mem, cross[:width]).astype(bfloat)
        sendout[pl.ds(length + rows.start, rows.size)] = mm(mem, cross[width:]).astype(bfloat)
        for ref in (resid, memory):
            io.put_rows(ref, rows.start, rows.size)
    io.put_if(scal[2] != 0, sendout, swap)


def ff_back(length, emit, grad_branch, activ, slope, inner_low, up, down, grad_inner):
    def body(rows, carry):
        grad = mm_nt(grad_branch[rows], down[...]) * slope[rows].astype(single)
        grad = grad.astype(bfloat)
        slope[rows] = grad
        grad_inner[rows] += mm(grad, up[...])
        return carry

    by_rows(length, body)
    for number in range(activ.shape[1] // 512):
        columns = slice(number * 512, (number + 1) * 512)
        emit(0, number, mm_tn(slope[:, columns], inner_low[...]))
        emit(1, number, mm_tn(activ[:, columns], grad_branch[...]))


def branch_back(length, resid, grad_out, inner, vec, grad_branch, grad_inner, grad_vec):
    width = resid.shape[1]

    def body(rows, carry):
        grad_resid, grad_gain, grad_shift = norm_back(resid[rows], grad_out[rows], vec[1:2])
        grad_branch[rows] = grad_resid.astype(bfloat)
        grad_inner[rows] = grad_resid * vec[0:1]
        weigh = jnp.sum(grad_resid * inner[rows].astype(single), 0, keepdims=True)
        return (carry[0] + weigh, carry[1] + grad_gain, carry[2] + grad_shift)

    put_rows(grad_vec, by_rows(length, body, zero_rows(width)))


def ctx_back(length, grad_branch, weight, ctx_t, grad_ctx, grad_ctx_t, dot_ref):
    def body(rows, carry):
        grad_ctx[rows] = mm_nt(grad_branch[rows], weight[...]).astype(bfloat)
        grad_ctx_t[:, rows] = grad_ctx[rows].T
        for head in range(HEADS):
            mine = slice(64 * head, 64 * head + 64)
            product = grad_ctx_t[mine, rows].astype(single) * ctx_t[mine, rows].astype(single)
            dot_ref[head : head + 1, rows] = jnp.sum(product, 0, keepdims=True)
        return carry

    by_rows(length, body)


def middle_body(
    io, scal, inner, packed, keys, cross, cross_vec, up, down, ff_vec, cotan,
    output, sendback, grad_inner, grads, grad_vec, swap,
    query, query_t, ctx_t, lse, resid, after, activ, slope, low_rows, grad_branch, grad_after,
    grad_ctx, grad_ctx_t, dot_ref, key_t, value_t, grad_key, grad_value, grad_query_t,
    key_tiles, key_two, value_two, swap_out,
):
    rows_here, width = inner.shape
    hidden, length = up.shape[0], keys.shape[0] // 2
    key_rows, value_rows = keys.at[:length], keys.at[length:]
    io.need(inner, packed, cross, keys)
    io.follow(cross_vec, up, down)

    @pl.when(scal[2] != 0)
    def _():
        inner[...] = unpack_rows(packed, rows_here)

    def project(rows, carry):
        query[rows] = mm(inner[rows].astype(bfloat), cross[:width]).astype(bfloat)
        query_t[:, rows] = (query[rows] * bfloat(0.125)).T
        return carry

    def turn(rows, carry):
        key_t[:, rows] = key_rows[rows].T
        value_t[:, rows] = value_rows[rows].T
        return carry

    by_rows(rows_here, project)
    by_rows(length, turn)
    attend(scal[4], None, key_rows, query_t, value_t, ctx_t, lse, key_tiles)
    io.rest()
    project_norm(io, rows_here, ctx_t, cross.at[width:], inner, cross_vec, resid, after)

    def feed(rows, carry):
        tile = after[rows]
        low_tile = tile.astype(bfloat)
        low_rows[rows] = low_tile
        act, grad = gelu_parts(mm_nt(low_tile, up[...]))
        act = act.astype(bfloat)
        activ[rows] = act
        slope[rows] = grad.astype(bfloat)
        total = tile * ff_vec[0:1] + mm(act, down[...])
        output[rows] = (normed(total)[0] * ff_vec[1:2] + ff_vec[2:3]).astype(bfloat)
        row = lax.broadcasted_iota(jnp.int32, tile.shape, 0) + rows.start
        grad_out = jnp.where(row < scal[3], cotan[rows].astype(single), 0.0)
        grad_resid, grad_gain, grad_shift = norm_back(total, grad_out, ff_vec[1:2])
        grad_branch[rows] = grad_resid.astype(bfloat)
        grad_after[rows] = grad_resid * ff_vec[0:1]
        weigh = jnp.sum(grad_resid * tile, 0, keepdims=True)
        return (carry[0] + weigh, carry[1] + grad_gain, carry[2] + grad_shift)

    put_rows(grad_vec.at[3:], by_rows(rows_here, feed, zero_rows(width)))
    io.put(output)

    def emit(which, number, value):
        first = 2 * width + which * hidden + number * 512
        grads[first : first + 512] = value.astype(bfloat)
        if which == 1 and number in (1, 3):
            for start in (2 * width, 2 * width + hidden):
                io.put_rows(grads, start + (number - 1) * 512, 1024)

    ff_back(rows_here, emit, grad_branch, activ, slope, low_rows, up, down, grad_after)
    branch_back(rows_here, resid, grad_after, inner, cross_vec, grad_branch, grad_inner, grad_vec)
    io.put(grad_vec)
    grads[width : 2 * width] = mm(ctx_t[...], grad_branch[...]).astype(bfloat)
    ctx_back(rows_here, grad_branch, cross.at[width:], ctx_t, grad_ctx, grad_ctx_t, dot_ref)
    attend_back(
        scal[4], None, query, key_rows, value_rows, query_t, key_t, grad_ctx, grad_ctx_t, lse, dot_ref,
        grad_key, grad_value, grad_query_t, key_two, value_two,
    )

    def send(rows, carry):
        sendback[rows] = (grad_key[rows] * 0.125).astype(bfloat)
        sendback[pl.ds(length + rows.start, rows.size)] = grad_value[rows].astype(bfloat)
        return carry

    by_rows(length, send)
    io.put(sendback)
    io.put_if(scal[2] == 0, sendback, swap)

    def last(rows, carry):
        grad_query = grad_query_t[:, rows].T
        grad_inner[rows] += mm_nt(grad_query, cross[:width])
        grad_ctx[rows] = grad_query
        return carry

    by_rows(rows_here, last)
    io.put(grad_inner)

    @pl.when(scal[2] != 0)
    def _():
        pack_rows(swap_out, 0, grad_inner[...])
        swap_out[3 * rows_here :] = output[...]

    io.put_if(scal[2] != 0, swap_out, swap)

    grads[:width] = mm_tn(inner[...].astype(bfloat), grad_ctx[...]).astype(bfloat)
    io.put_rows(grads, 0, 2 * width)


def encoder_back_body(
    io, scal, table, own, received, memory, cross, inner, resid, activ, slope, up, down, vec,
    grad_inner, grad_vec, target,
    grad_mem, inner_low, grad_branch, stage, semaphores,
):
    length, width = inner.shape
    emit = Emitter(table, target, stage, semaphores)
    io.begin(own, received, cross, inner)
    io.follow(memory, vec, resid, down, slope, up, activ)
    io.need(own, received, cross, inner)

    def body(rows, carry):
        own[...] = added(own[...], received[...])
        grad_mem[rows] = mm_nt(own[:length], cross[:width]) + mm_nt(own[length:], cross[width:])
        inner_low[rows] = inner[rows].astype(bfloat)
        return carry

    by_rows(length, body)
    io.need(vec, resid, memory)
    emit.chunk(8, 16, mm_tn(memory[...], own[:length]))
    emit.chunk(9, 20, mm_tn(memory[...], own[length:]))
    branch_back(length, resid, grad_mem, inner, vec, grad_branch, grad_inner, grad_vec)
    io.put(grad_vec)
    io.rest()

    def each(which, number, value):
        emit.chunk(2 * number + which, 24 + 16 * which + 4 * number, value)

    ff_back(length, each, grad_branch, activ, slope, inner_low, up, down, grad_inner)
    io.put(grad_inner)
    emit.wait()


def self_back_body(
    io, scal, table, x, weight, out_weight, vec, resid, query, key, value, ctx_t, lse, grad_out, packed, held,
    grad_x, grad_vec, target,
    grad_branch, grad_ctx, grad_ctx_t, dot_ref, query_t, key_t, grad_key, grad_value, grad_query_t,
    key_two, value_two, stage, semaphores,
):
    length, width = x.shape
    emit = Emitter(table, target, stage, semaphores)
    some = length // 2
    io.need(resid, grad_out, packed, x, vec)
    io.follow(ctx_t, out_weight, query, key, value)

    @pl.when(scal[2] == 0)
    def _():
        grad_out[some:] = unpack_rows(packed, some)

    branch_back(length, resid, grad_out, x, vec, grad_branch, grad_x, grad_vec)
    io.put(grad_vec)
    io.need(ctx_t, out_weight)
    emit.chunk(3, 12, mm(ctx_t[...], grad_branch[...]))
    ctx_back(length, grad_branch, out_weight, ctx_t, grad_ctx, grad_ctx_t, dot_ref)
    io.rest()

    def body(rows, carry):
        query_t[:, rows] = (query[rows] * bfloat(0.125)).T
        key_t[:, rows] = key[rows].T
        return carry

    by_rows(length, body)
    attend_back(
        scal[0], scal[1], query, key, value, query_t, key_t, grad_ctx, grad_ctx_t, lse, dot_ref,
        grad_key, grad_value, grad_query_t, key_two, value_two,
    )

    def last(rows, carry):
        parts = (
            grad_query_t[:, rows].T,
            (grad_key[rows] * 0.125).astype(bfloat),
            grad_value[rows].astype(bfloat),
        )
        total = grad_x[rows]
        for number, low_grad in enumerate(parts):
            total += mm_nt(low_grad, weight[width * number : width * (number + 1)])
        grad_x[rows] = total
        grad_branch[rows], grad_ctx[rows], value[rows] = parts
        return carry

    by_rows(length, last)
    io.put(grad_x)
    for number, ref in enumerate((grad_branch, grad_ctx, value)):
        emit.chunk(number, 4 * number, mm_tn(x[...], ref[...]))
    emit.wait()


def merge_body(io, scal, table, own, other, held, target, stage, semaphores):
    emit = Emitter(table, target, stage, semaphores)
    io.rest()
    chunk = stage.shape[1]
    for number in range(own.shape[0] // chunk):
        rows = slice(number * chunk, (number + 1) * chunk)
        total = own[rows].astype(single) + other[rows].astype(single)
        emit.chunk(number, 16 + 4 * number, total)
    emit.wait()


RING = (0, 2, 4, 6, 7, 5, 3, 1)
LEAD = 8


def round_ring(value, step):
    count = len(RING)
    return lax.ppermute(value, "wide", [(RING[i], RING[(i + step) % count]) for i in range(count)])


def swapped(value):
    return lax.ppermute(value, "narrow", [(0, 1), (1, 0)])


def step_of(up, down, across):
    return lax.optimization_barrier((round_ring(up, 1), round_ring(down, -1), swapped(across)))


def partner(value, axis, bit):
    return lax.ppermute(value, axis, [(i, i ^ bit) for i in range(lax.axis_size(axis))])


def join(*values):
    return jnp.concatenate(values, 0)


def ring_gather(own, tables):
    every, lead, half = own.shape[0], LEAD, LEAD // 2
    late = every - lead
    found = [([(0, every, 0, 0, 0)], own)]

    def ahead(value, far, near):
        ranges = [(0, lead, far, 0, 0)]
        if near is not None:
            ranges += [(lead, lead + late, near, 0, lead), (lead + late, lead + 2 * late, near, 1, lead)]
        found.append((ranges, value))

    up, down, across = step_of(own[:lead], own[:lead], own[lead:])
    found.append(([(0, late, 0, 1, lead)], across))
    ahead(up, 7, None)
    ahead(down, 1, None)
    pair = join(own[lead:], across)
    up, down, across = step_of(join(up, pair), join(down, pair), join(up, down, own[:half]))
    found.append(
        ([(0, lead, 7, 1, 0), (lead, 2 * lead, 1, 1, 0), (2 * lead, 2 * lead + half, 0, 1, 0)], across)
    )
    up, tables = lax.optimization_barrier((up, tables))
    ahead(up, 6, 7)
    ahead(down, 2, 1)
    up, down, across = step_of(up, down, join(up[:lead], down[:lead], own[half:lead]))
    found.append(
        ([(0, lead, 6, 1, 0), (lead, 2 * lead, 2, 1, 0), (2 * lead, 2 * lead + half, 0, 1, half)], across)
    )
    ahead(up, 5, 6)
    ahead(down, 3, 2)
    up, down, across = step_of(join(up[:half], up[lead:]), down[half:], join(up[:lead], down[:lead]))
    found.append(([(0, lead, 5, 1, 0), (lead, 2 * lead, 3, 1, 0)], across))
    for value, first, near in ((up, 0, 5), (down, half, 3)):
        ranges = [(0, half, 4, 0, first), (half, half + late, near, 0, lead)]
        found.append((ranges + [(half + late, half + 2 * late, near, 1, lead)], value))
    up, down, across = step_of(
        up[half : half + late], down[half + late :], join(up[:half], down[:half])
    )
    found.append(([(0, late, 4, 0, lead)], up))
    found.append(([(0, late, 4, 1, lead)], down))
    found.append(([(0, lead, 4, 1, 0)], across))
    return found, tables


def added(*values):
    return sum(value.astype(single) for value in values).astype(bfloat)


def ring_scatter(grads, vector):
    partners = [("narrow", 1), ("wide", 1), ("wide", 2), ("wide", 4), ("half", 1)]

    def step_of(*values):
        nonlocal vector
        ring = (round_ring(values[0], 1), round_ring(values[1], -1), swapped(values[2]))
        *ring, other = lax.optimization_barrier((*ring, partner(vector, *partners.pop(0))))
        vector = vector + other
        return ring

    lead, half = LEAD, LEAD // 2
    late = grads.shape[2] - lead

    def both(distance):
        return grads[distance, :, lead:].reshape((-1,) + grads.shape[3:])

    def mine(distance, start=0, stop=lead):
        return grads[distance, 0, start:stop]

    def other(distance, start=0, stop=lead):
        return grads[distance, 1, start:stop]

    up, down, across = step_of(grads[4, 0, lead:], grads[4, 1, lead:], other(4))
    first = added(mine(4), across)
    up = join(first[:half], added(up, grads[3, 0, lead:]), grads[3, 1, lead:])
    down = join(first[half:], grads[5, 0, lead:], added(down, grads[5, 1, lead:]))
    up, down, across = step_of(up, down, join(other(3), other(5)))
    up = join(
        added(mine(3, 0, half), across[:half], up[:half]),
        added(mine(3, half), across[half:lead]),
        added(up[half:], both(2)),
    )
    down = join(
        added(mine(5, 0, half), across[lead : lead + half]),
        added(mine(5, half), across[lead + half :], down[:half]),
        added(down[half:], both(6)),
    )
    up, down, across = step_of(up, down, join(other(2), other(6), other(0, 0, half)))
    nearest = [across[2 * lead :]]
    up = join(added(mine(2), across[:lead], up[:lead]), added(up[lead:], both(1)))
    down = join(added(mine(6), across[lead : 2 * lead], down[:lead]), added(down[lead:], both(7)))
    up, down, across = step_of(up, down, join(other(1), other(7), other(0, half)))
    nearest.append(across[2 * lead :])
    total = sum(value.astype(single) for value in (both(0), up[lead:], down[lead:]))
    up, down, across = step_of(
        added(mine(1), across[:lead], up[:lead]),
        added(mine(7), across[lead : 2 * lead], down[:lead]),
        total[late:].astype(bfloat),
    )
    first = sum(value.astype(single) for value in (mine(0), join(*nearest), up, down))
    return join(first, total[:late] + across.astype(single)), vector


def shaped(*shape, dtype=single):
    return jax.ShapeDtypeStruct(shape, dtype)


def low(*shape):
    return jax.ShapeDtypeStruct(shape, bfloat)


def low_vm(*shape):
    return pltpu.VMEM(shape, bfloat)


def full_vm(*shape):
    return pltpu.VMEM(shape, single)


def sum_over(value, axis):
    size = lax.axis_size(axis)
    bit = 1
    while bit < size:
        value = value + partner(value, axis, bit)
        bit *= 2
    return value


def adam(weight, gradient, first, second, step_rate, decay_rate):
    first_new = beta_one * first + (1.0 - beta_one) * gradient
    second_new = beta_two * second + (1.0 - beta_two) * gradient * gradient
    first_hat = first_new / (1.0 - beta_one**STEP)
    second_hat = second_new / (1.0 - beta_two**STEP)
    weight_new = weight - step_rate * (
        first_hat / (jnp.sqrt(second_hat) + eps_adam) + decay_rate * weight
    )
    return (weight_new, first_new, second_new)


def on_device(
    stream, cotangent, lengths, owners, master, moment_one, moment_two, vec_master, vec_one, vec_two
):
    narrow_size = lax.axis_size("narrow")
    wide_size = lax.axis_size("wide")
    owner_row = owners[0]
    capacity = master.shape[1]
    half_rows = master.shape[2]
    width = master.shape[3]
    count = owner_row.shape[0]
    counter = jnp.arange(count)
    same = owner_row[:, None] == owner_row[None, :]
    earlier = counter[None, :] < counter[:, None]
    ranks = jnp.sum((same & earlier).astype(jnp.int32), 1)
    on_ring = wide_size == len(RING) and narrow_size == 2 and capacity > LEAD
    wide_at, narrow_at = lax.axis_index("wide"), lax.axis_index("narrow")
    self_rows, rest_rows = 4 * width, count * half_rows * narrow_size - 4 * width
    is_source = lax.axis_index("half") == 0
    x = stream[0, 0]
    length = x.shape[0]
    some = length // 2
    source_len, target_len = lengths[0, 0], lengths[1, 0]
    flag = is_source.astype(jnp.int32)
    scal = jnp.stack(
        [
            jnp.where(is_source, source_len, target_len),
            1 - flag,
            flag,
            jnp.where(is_source, target_len - some, target_len),
            source_len,
            narrow_at,
        ]
    ).astype(jnp.int32)
    own = master[0].astype(bfloat)
    if on_ring:
        turned = [RING.index(i) for i in range(wide_size)]
        position = jnp.array(turned)[wide_at]
        owner_ring = jnp.array(turned)[owner_row]
        distance = (owner_ring - position) % wide_size
        halves = jnp.arange(narrow_size)[None, :] ^ narrow_at
        table = ((distance[:, None] * 2 + halves) * capacity + ranks[:, None]).reshape(-1)
        slot_of = distance * capacity + ranks
        hit = slot_of[None, :] == jnp.arange(wide_size * capacity)[:, None]
        pieces = jnp.sum(hit.astype(jnp.int32) * (counter + 1)[None, :], 1) - 1
        pieces = pieces.reshape(wide_size, capacity).astype(jnp.int32)
        found, (pieces, table, scal) = ring_gather(own, (pieces, table.astype(jnp.int32), scal))
    else:
        places = (
            owner_row[:, None] * narrow_size + jnp.arange(narrow_size)[None, :]
        ) * capacity + ranks[:, None]
        table = places.reshape(-1)
        gathered = lax.all_gather(own, ("wide", "narrow"), axis=0, tiled=True)
        weight = jnp.take(gathered, table, axis=0).reshape(-1, width)
        weight, rest = weight[:self_rows], weight[self_rows:]
    table = table.astype(jnp.int32)
    hidden = (rest_rows - 2 * width) // 2
    self_vec = whole(jnp.where(is_source, vec_master[0:3], vec_master[6:9]))
    cross_vec, ff_vec = whole(vec_master[9:12]), whole(vec_master[12:15])
    memory_vec = whole(vec_master[3:6])
    slots = low(capacity * wide_size * narrow_size, half_rows, width)

    def stage_of(chunks):
        return [
            low_vm(chunks, 512, width),
            pltpu.SemaphoreType.DMA((chunks * 512 // half_rows,)),
        ]

    def store(*shape, dtype=single):
        return ("store", shaped(*shape, dtype=dtype))

    low_out = partial(store, dtype=bfloat)
    two, four = low_vm(2, length, 128), low_vm(4, length, 128)
    down_half, up_half, both_halves = [(1, 0)], [(0, 1)], [(0, 1), (1, 0)]

    forward_outs = (
        [low_out(length, width)] * 3
        + [low_out(width, length), store(HEADS, length)]
        + [store(length, width)] * 2
        + [("hbm", low(2 * length, width))]
    )
    forward_scratch = [low_vm(width, length), low_vm(width, length), four, low_vm(3 * some, width)]
    if on_ring:
        *forward, weight, rest = call(
            partial(placed_forward_body, [where for where, unused in found]),
            "self_forward",
            scal,
            None,
            [("smem", pieces), whole(x), self_vec] + [("hbm", value) for unused, value in found],
            forward_outs + [low_out(self_rows, width), low_out(rest_rows, width)],
            forward_scratch + [pltpu.SemaphoreType.DMA((2,))],
        )
    else:
        forward = call(
            self_forward_body,
            "self_forward",
            scal,
            None,
            [whole(x), whole(weight), self_vec],
            forward_outs,
            forward_scratch,
        )
    query, key, value, ctx_t, lse, resid, inner, swap = forward
    rest_other = lax.ppermute(rest, "half", down_half)
    cross_w = part(rest, 0, 2 * width)
    up_w = part(rest, 2 * width, hidden)
    down_w = part(rest, 2 * width + hidden, hidden)
    activ, slope, ff_resid, memory, swap = call(
        encoder_ff_body,
        "encoder_ff",
        scal,
        1,
        [whole(inner), up_w, down_w, cross_w, memory_vec, ("hbm", swap)],
        [low_out(length, hidden)] * 2
        + [store(length, width), low_out(length, width), ("hbm", low(2 * length, width))],
        [low_vm(2 * length, width)],
        [(5, 4)],
    )
    swap_other = lax.ppermute(swap, "half", both_halves)

    def shared(first, rows):
        return either([(rest_other, first, 0, rows)], [(rest, first, 0, rows)])

    mid_inner = either([], [(inner, 0, 0, some)])
    mid_packed = either([(swap_other, 0, 0, 3 * some)], [])
    keys = either([(swap, 0, 0, None)], [(swap_other, 0, 0, None)])
    cotan = cotangent[0]
    output, sendback, grad_one, grad_rest, grad_middle_vec, swap = call(
        middle_body,
        "decoder_middle",
        scal,
        None,
        [
            mid_inner,
            mid_packed,
            keys,
            shared(0, 2 * width),
            cross_vec,
            shared(2 * width, hidden),
            shared(2 * width + hidden, hidden),
            ff_vec,
            either([(cotan, some, 0, some)], [(cotan, 0, 0, some)]),
        ],
        [
            low_out(some, width),
            low_out(2 * length, width),
            store(some, width),
            low_out(rest_rows, width),
            store(6, width),
            ("hbm", low(2 * length, width)),
        ],
        [low_vm(some, width), low_vm(width, some), low_vm(width, some), full_vm(HEADS, some)]
        + [full_vm(some, width), full_vm(some, width), low_vm(some, hidden), low_vm(some, hidden)]
        + [low_vm(some, width), low_vm(some, width), full_vm(some, width)]
        + [low_vm(some, width), low_vm(width, some), full_vm(HEADS, some)]
        + [low_vm(width, length), low_vm(width, length)]
        + [full_vm(length, width), full_vm(length, width), low_vm(width, some), four, two, two]
        + [low_vm(2 * length, width)],
    )
    swap_other = lax.ppermute(swap, "half", both_halves)
    grad_rest, swap_other = lax.optimization_barrier((grad_rest, swap_other))
    grad_rest_other = lax.ppermute(grad_rest, "half", up_half)
    output = join(output, swap_other[3 * some :])
    grad_inner, grad_memory_vec, target = call(
        encoder_back_body,
        "encoder_back",
        scal,
        1,
        [
            ("smem", table),
            whole(sendback),
            whole(swap_other),
            whole(memory),
            cross_w,
            whole(inner),
            whole(ff_resid),
            whole(activ),
            whole(slope),
            up_w,
            down_w,
            memory_vec,
        ],
        [store(length, width), store(3, width), ("hbm", slots)],
        [full_vm(length, width), low_vm(length, width), low_vm(length, width)] + stage_of(10),
    )
    back_scratch = (
        [low_vm(length, width), low_vm(length, width), low_vm(width, length), full_vm(HEADS, length)]
        + [low_vm(width, length), low_vm(width, length)]
        + [full_vm(length, width), full_vm(length, width), low_vm(width, length), two, two]
    )
    grad_x, grad_self_vec, target = call(
        self_back_body,
        "self_back",
        scal,
        None,
        [
            ("smem", table),
            whole(x),
            part(weight, 0, 3 * width),
            part(weight, 3 * width, width),
            self_vec,
            whole(resid),
            whole(query),
            whole(key),
            whole(value),
            whole(ctx_t),
            whole(lse),
            either(
                [(grad_inner, 0, 0, length)],
                [(grad_one, 0, 0, some)],
            ),
            either([], [(swap_other, 0, 0, 3 * some)]),
            ("hbm", target),
        ],
        [store(length, width), store(3, width), ("hbm", slots)],
        back_scratch + stage_of(4),
        [(13, 2)],
    )
    (target,) = call(
        merge_body,
        "merge",
        scal,
        0,
        [
            ("smem", table),
            whole(grad_rest),
            whole(grad_rest_other),
            ("hbm", target),
        ],
        [("hbm", slots)],
        stage_of(10),
        [(3, 0)],
    )
    vec_grads = jnp.concatenate(
        [
            jnp.where(is_source, grad_self_vec, 0.0),
            jnp.where(is_source, grad_memory_vec, 0.0),
            jnp.where(is_source, 0.0, grad_self_vec),
            grad_middle_vec,
        ],
        0,
    )
    if on_ring:
        grads = target.reshape(wide_size, 2, capacity, half_rows, width)
        mine, vec_grads = ring_scatter(grads, vec_grads)
    else:
        mine = lax.psum_scatter(target, ("wide", "narrow"), scatter_dimension=0, tiled=True)
        for axis in ("narrow", "wide", "half"):
            vec_grads = sum_over(vec_grads, axis)
    used = jnp.sum((owner_row == wide_at).astype(jnp.int32))
    mine = jnp.where((jnp.arange(capacity) < used)[:, None, None], mine.astype(single), 0.0)
    new_weight, new_first, new_second = adam(
        master[0], mine, moment_one[0], moment_two[0], rate_matrix, decay_matrix
    )
    vec_weight, vec_first, vec_second = adam(
        vec_master, vec_grads, vec_one, vec_two, rate_vector, 0.0
    )
    return (
        jnp.where(is_source, memory, output)[None, None],
        grad_x[None, None],
        new_first[None],
        new_second[None],
        new_weight[None],
        new_weight.astype(bfloat)[None],
        vec_first,
        vec_second,
        vec_weight,
    )


def solution(mesh):
    in_specs = (
        P("half", ("wide", "narrow"), None, None),
        P(("wide", "narrow"), None, None),
        P(None, ("wide", "narrow")),
        P("half", None),
        P("half", "wide", "narrow", None),
        P("half", "wide", "narrow", None),
        P("half", "wide", "narrow", None),
        P(),
        P(),
        P(),
    )
    out_specs = (
        P("half", ("wide", "narrow"), None, None),
        P("half", ("wide", "narrow"), None, None),
        P("half", "wide", "narrow", None),
        P("half", "wide", "narrow", None),
        P("half", "wide", "narrow", None),
        P("half", "wide", "narrow", None),
        P(),
        P(),
        P(),
    )
    return jax.shard_map(
        on_device, mesh=mesh, in_specs=in_specs, out_specs=out_specs, check_vma=False
    )
```

```python
import math
from functools import partial

import jax
import jax.numpy as jnp
from jax import lax
from jax.experimental import pallas as pl
from jax.experimental.pallas import tpu as pltpu
from jax.sharding import PartitionSpec as P

HEADS = 8
STEP = 5
CAUSAL = 512
RB = 1024
NEG = -1e30

eps_norm = 1e-05
beta_one = 0.5
beta_two = 0.5
rate_matrix = 0.05
rate_vector = 0.3
decay_matrix = 0.01
eps_adam = 1e-08
bfloat = jnp.bfloat16
single = jnp.float32
VM = pl.BlockSpec(memory_space=pltpu.VMEM)
SM = pl.BlockSpec(memory_space=pltpu.SMEM)
HB = pl.BlockSpec(memory_space=pl.ANY)


def mm(left, right):
    return jnp.dot(left, right, preferred_element_type=single)


def mm_tn(left, right):
    return lax.dot_general(left, right, (((0,), (0,)), ((), ())), preferred_element_type=single)


def mm_nt(left, right):
    return lax.dot_general(left, right, (((1,), (1,)), ((), ())), preferred_element_type=single)


def block_of(index, size):
    return pl.ds(pl.multiple_of(index * size, size), size)


def normed(resid):
    center = resid - jnp.mean(resid, -1, keepdims=True)
    spread = jnp.mean(center * center, -1, keepdims=True)
    rstd = lax.rsqrt(spread + eps_norm)
    return center * rstd, rstd


def norm_back(resid, grad, gain):
    hat, rstd = normed(resid)
    grad_hat = grad * gain
    grad_resid = rstd * (
        grad_hat
        - jnp.mean(grad_hat, -1, keepdims=True)
        - hat * jnp.mean(grad_hat * hat, -1, keepdims=True)
    )
    return grad_resid, jnp.sum(grad * hat, 0, keepdims=True), jnp.sum(grad, 0, keepdims=True)


def gelu_parts(pre_act):
    half = 0.5 * (1.0 + lax.erf(pre_act * math.sqrt(0.5)))
    slope = half + pre_act * (jnp.exp(-0.5 * pre_act * pre_act) * (1.0 / math.sqrt(2.0 * math.pi)))
    return pre_act * half, slope


def pair_keys(tile, first_extra, ones):
    rows = tile.shape[0]
    lane = lax.broadcasted_iota(jnp.int32, (rows, 128), 1)
    wide_tile = tile.astype(single)
    out = []
    for head in range(2):
        at = lane - (64 - 64 * head)
        extra = jnp.where(at == 0, first_extra, jnp.where((at > 0) & (at < ones), 1.0, 0.0))
        mine = (lane < 64) if head == 0 else (lane >= 64)
        out.append(jnp.where(mine, wide_tile, extra).astype(bfloat))
    return out


def pair_queries(tile, head, extra_rows):
    mine = tile[64 * head : 64 * head + 64]
    row = lax.broadcasted_iota(jnp.int32, mine.shape, 0)
    extra = jnp.zeros(mine.shape, single)
    for number, value in enumerate(extra_rows):
        extra = jnp.where(row == number, value, extra)
    extra = extra.astype(bfloat)
    return jnp.concatenate([mine, extra] if head == 0 else [extra, mine], 0)


def pack_rows(target, first, value):
    rows = value.shape[0]
    for number, one in enumerate(split_three(value)):
        target[first + number * rows : first + (number + 1) * rows] = one.astype(bfloat)


def unpack_rows(packed, rows):
    high, middle, rest = (packed[n * rows : (n + 1) * rows].astype(single) for n in range(3))
    return (high + middle) + rest


def split_three(value):
    high = value.astype(bfloat).astype(single)
    rest = value - high
    middle = rest.astype(bfloat).astype(single)
    return [high, middle, rest - middle]


def key_bias(limit, rows):
    row = lax.broadcasted_iota(jnp.int32, (rows, 128), 0)
    return jnp.where(row < limit, 0.0, NEG)


def score_parts(scores, diagonal):
    if not diagonal:
        return [scores]
    size = scores.shape[1]
    cut = scores.shape[0] - size
    row = lax.broadcasted_iota(jnp.int32, (size, size), 0)
    column = lax.broadcasted_iota(jnp.int32, (size, size), 1)
    last = jnp.where(row <= column, scores[cut:], NEG)
    return [scores[:cut], last] if cut else [last]


def over_blocks(causal, rows, length, body):
    def every():
        body(0, rows, length, False)

    if causal is None:
        every()
        return
    pl.when(causal == 0)(every)

    @pl.when(causal != 0)
    def _():
        for first in range(0, rows, CAUSAL):
            body(first, CAUSAL, first + CAUSAL, True)


def head_rows(group, heads, head):
    return pl.ds(pl.multiple_of((group * heads + head) * 64, 64), 64)


def attend(limit, causal, key_ref, query_t, value_t, ctx_t, lse_ref, key_tiles):
    length, width = key_ref.shape
    heads = key_tiles.shape[0]
    bias = key_bias(limit, length)

    def group_of(group, unused):
        for number in range(heads // 2):
            columns = block_of(group * (heads // 2) + number, 128)
            for head, tile in enumerate(pair_keys(key_ref[:, columns], bias, 1)):
                key_tiles[2 * number + head] = tile

        def body(first, queries, extent, diagonal):
            at = slice(first, first + queries)

            def scores_of(head):
                columns = block_of(group * (heads // 2) + head // 2, 128)
                tile = pair_queries(query_t[columns, at], head % 2, [1.0])
                return mm(key_tiles[head, :extent], tile)

            following = scores_of(0)
            for head in range(heads):
                parts = score_parts(following, diagonal)
                if head + 1 < heads:
                    following = scores_of(head + 1)
                top = jnp.max(parts[0], 0, keepdims=True)
                for more in parts[1:]:
                    top = jnp.maximum(top, jnp.max(more, 0, keepdims=True))
                parts = [jnp.exp(more - top) for more in parts]
                total = sum(jnp.sum(more, 0, keepdims=True) for more in parts)
                weights = jnp.concatenate([more.astype(bfloat) for more in parts], 0)
                mine = head_rows(group, heads, head)
                context = mm(value_t[mine, :extent], weights)
                ctx_t[mine, at] = (context * (1.0 / total)).astype(bfloat)
                lse_ref[pl.ds(group * heads + head, 1), at] = top + jnp.log(total)

        over_blocks(causal, query_t.shape[1], length, body)
        return 0

    lax.fori_loop(0, HEADS // heads, group_of, 0)


def attend_back(
    limit, causal, query_ref, key_ref, value_ref, query_t, key_t, grad_ctx, grad_ctx_t, lse_ref, dot_ref,
    grad_key, grad_value, grad_query_t, key_two, value_two,
):
    length, width = key_ref.shape
    bias = key_bias(limit, length)

    def pair(number, unused):
        columns = block_of(number, 128)
        for head, tile in enumerate(pair_keys(key_ref[:, columns], bias, 4)):
            key_two[head] = tile
        for head, tile in enumerate(pair_keys(value_ref[:, columns], 1.0, 3)):
            value_two[head] = tile

        def body(first, queries, extent, diagonal):
            at = slice(first, first + queries)

            def products_of(head):
                row = pl.ds(number * 2 + head, 1)
                constants = [1.0] + split_three(-lse_ref[row, at])
                scores = mm(
                    key_two[head, :extent], pair_queries(query_t[columns, at], head, constants)
                )
                constants = split_three(-dot_ref[row, at])
                grad_weights = mm(
                    value_two[head, :extent], pair_queries(grad_ctx_t[columns, at], head, constants)
                )
                return scores, grad_weights

            lane = lax.broadcasted_iota(jnp.int32, (queries, 128), 1)

            def both(tile):
                tile = tile.astype(single)
                return jnp.concatenate(
                    [
                        jnp.where(lane < 64, tile, 0.0).astype(bfloat),
                        jnp.where(lane < 64, 0.0, tile).astype(bfloat),
                    ],
                    0,
                )

            all_weights, all_grads = [], []
            following = products_of(0)
            for head in range(2):
                scores, grad_weights = following
                if head == 0:
                    following = products_of(1)
                weights = [jnp.exp(more) for more in score_parts(scores, diagonal)]
                weights = jnp.concatenate(weights, 0)
                grads = (weights * grad_weights).astype(bfloat)
                all_weights.append(weights.astype(bfloat))
                all_grads.append(grads)
                mine = head_rows(number, 2, head)
                grad_query = mm(key_t[mine, :extent], grads)
                grad_query_t[mine, at] = (grad_query * 0.125).astype(bfloat)
            for out, parts, other in (
                (grad_value, all_weights, grad_ctx),
                (grad_key, all_grads, query_ref),
            ):
                total = mm(jnp.concatenate(parts, 1), both(other[at, columns]))
                if first:
                    total = jnp.concatenate([out[:first, columns] + total[:first], total[first:]], 0)
                out[:extent, columns] = total

        over_blocks(causal, query_t.shape[1], length, body)
        return 0

    lax.fori_loop(0, width // 128, pair, 0)


def by_rows(length, body, init=0):
    if length <= RB:
        return body(pl.ds(0, length), init)

    def step(index, carry):
        return body(block_of(index, RB), carry)

    return lax.fori_loop(0, length // RB, step, init)


class Emitter:
    def __init__(self, table, targets, stage, semaphores):
        self.table, self.targets, self.stage, self.semaphores = table, targets, stage, semaphores
        self.copies = []

    def chunk(self, number, first_piece, value):
        stage, half_rows = self.stage, self.targets[0].shape[1]
        stage[number] = value.astype(bfloat)
        count = stage.shape[1] // half_rows
        per_piece = 128 // half_rows
        for part in range(count):
            source = stage.at[number, pl.ds(part * half_rows, half_rows)]
            semaphore = self.semaphores.at[number * count + part]
            slot = self.table[first_piece * per_piece + part]

            def start(targets, first, source=source, semaphore=semaphore, slot=slot):
                def go():
                    pltpu.make_async_copy(source, targets[0].at[slot - first], semaphore).start()

                if len(targets) == 1:
                    go()
                    return
                last = first + targets[0].shape[0]
                pl.when(slot < last)(go)
                pl.when(slot >= last)(lambda: start(targets[1:], last))

            start(self.targets, 0)
            self.copies.append(pltpu.make_async_copy(source, self.targets[0].at[0], semaphore))

    def wait(self):
        for copy in self.copies:
            copy.wait()


class Moves:
    def __init__(self, role, spare):
        self.role = role
        self.spare = spare
        self.some = []
        self.loads = []
        self.stores = []
        self.begun = set()
        self.waited = set()

    def load(self, dest, ways, semaphores):
        def each(way, act):
            for number, (source, first, at, rows) in enumerate(way):
                target = dest
                if rows is not None:
                    source = source.at[pl.ds(first, rows)]
                    target = dest.at[pl.ds(at, rows)]
                act(pltpu.make_async_copy(source, target, semaphores.at[number]))

        def split(act):
            if len(ways) == 1:
                each(ways[0], act)
                return
            pl.when(self.role != 0)(lambda: each(ways[0], act))
            pl.when(self.role == 0)(lambda: each(ways[1], act))

        self.loads.append((dest, split))

    def begin(self, *refs):
        for number, (dest, split) in enumerate(self.loads):
            if number not in self.begun and any(dest is ref for ref in refs):
                self.begun.add(number)
                split(lambda copy: copy.start())

    def need(self, *refs):
        self.begin(*refs)
        for number, (dest, split) in enumerate(self.loads):
            if number not in self.waited and any(dest is ref for ref in refs):
                self.waited.add(number)
                split(lambda copy: copy.wait())

    def follow(self, *refs):
        self.begin(*refs)
        for dest, unused in self.loads:
            self.begin(dest)

    def rest(self):
        self.follow()
        self.need(*[dest for dest, unused in self.loads])

    def place(self, source, target, semaphores):
        self.stores.append((source, target, semaphores, []))

    def put(self, *refs):
        for source, target, semaphores, copies in self.stores:
            if not copies and any(source is ref for ref in refs):
                copies.append(pltpu.make_async_copy(source, target, semaphores.at[0]))
                copies[0].start()

    def put_rows(self, ref, first, rows):
        for source, target, semaphores, copies in self.stores:
            if source is ref:
                at = pl.ds(first, rows)
                copies.append(
                    pltpu.make_async_copy(source.at[at], target.at[at], semaphores.at[len(copies)])
                )
                copies[-1].start()

    def put_if(self, wanted, source, target):
        copy = pltpu.make_async_copy(source, target, self.spare.at[len(self.some)])
        pl.when(wanted)(copy.start)
        self.some.append((wanted, copy))

    def finish(self):
        self.rest()
        self.put(*[entry[0] for entry in self.stores])
        for entry in self.stores:
            for copy in entry[3]:
                copy.wait()
        for wanted, copy in self.some:
            pl.when(wanted)(copy.wait)


def part(value, first, rows):
    return ("load", [[(value, first, 0, rows)]])


def whole(value):
    return ("load", [[(value, 0, 0, None)]])


def either(source_way, target_way):
    return ("load", [source_way, target_way])


def call(body, name, scal, active, ins, outs, scratch, aliases=(), limit=58):
    args, specs, scratch_all, plan = [scal], [SM], [], []
    counts = {"load": 0, "store": 0}

    def arg(value, spec):
        args.append(value)
        specs.append(spec)
        return len(args) - 1

    held = []
    for kind, value in ins:
        if kind == "load":
            ways = [[(arg(v, HB), first, at, rows) for v, first, at, rows in way] for way in value]
            way = value[0] or value[1]
            v, first, at, rows = way[0]
            total = max(a + r for _, _, a, r in way) if rows is not None else None
            shape = v.shape if rows is None else (total,) + v.shape[1:]
            held.append(("load", ways, shape, v.dtype, max(len(w) for w in ways)))
        else:
            held.append((kind, arg(value, SM if kind == "smem" else HB)))
    vmem, sems = [], []
    for entry in held:
        if entry[0] == "load":
            vmem.append(pltpu.VMEM(entry[2], entry[3]))
            sems.append(pltpu.SemaphoreType.DMA((entry[4],)))
    for kind, shape in outs:
        if kind == "store":
            vmem.append(pltpu.VMEM(shape.shape, shape.dtype))
            sems.append(pltpu.SemaphoreType.DMA((6,)))
    count_in, count_out = len(args), len(outs)

    def kernel(*refs):
        inputs, outputs = refs[:count_in], refs[count_in : count_in + count_out]
        rest = refs[count_in + count_out :]
        buffers, semaphores = list(rest[: len(vmem)]), list(rest[len(vmem) : len(vmem) + len(sems)])
        spare, *extra = rest[len(vmem) + len(sems) :]
        scal_ref = inputs[0]

        def run():
            moves = Moves(scal_ref[2], spare)
            given = []
            for entry in held:
                if entry[0] == "load":
                    dest, semaphore = buffers.pop(0), semaphores.pop(0)
                    ways = [[(inputs[i], f, a, r) for i, f, a, r in way] for way in entry[1]]
                    moves.load(dest, ways, semaphore)
                    given.append(dest)
                else:
                    given.append(inputs[entry[1]])
            for (kind, unused), output in zip(outs, outputs):
                if kind == "store":
                    source, semaphore = buffers.pop(0), semaphores.pop(0)
                    moves.place(source, output, semaphore)
                    given.append(source)
                else:
                    given.append(output)
            body(moves, scal_ref, *given, *extra)
            moves.finish()

        if active is None:
            run()
        else:
            pl.when(scal_ref[2] == active)(run)

    pairs = {}
    for position, output in aliases:
        pairs[held[position][1]] = output
    return pl.pallas_call(
        kernel,
        in_specs=specs,
        out_specs=[HB] * count_out,
        out_shape=[shape for unused, shape in outs],
        scratch_shapes=vmem + sems + [pltpu.SemaphoreType.DMA((2,))] + list(scratch),
        input_output_aliases=pairs,
        compiler_params=pltpu.CompilerParams(vmem_limit_bytes=62 << 20),
        name=name,
    )(*args)


def halves_of(length):
    return [pl.ds(0, length // 2), pl.ds(length // 2, length // 2)]


def zero_rows(width):
    return (jnp.zeros((1, width), single),) * 3


def put_rows(ref, rows):
    for number, row in enumerate(rows):
        ref[number : number + 1] = row


def project_norm(io, length, ctx_t, weight, inner_ref, vec, resid_ref, out_ref):
    for rows in halves_of(length):
        branch = mm(ctx_t[:, rows].T, weight[...])
        resid = inner_ref[rows].astype(single) * vec[0:1] + branch
        resid_ref[rows] = resid
        out_ref[rows] = normed(resid)[0] * vec[1:2] + vec[2:3]
        for ref in (resid_ref, out_ref):
            io.put_rows(ref, rows.start, rows.size)


def self_forward(io, scal, x, weight, vec, outs, query_t, value_t, key_tiles, packed, ready):
    query, key, value, ctx_t, lse, resid, out, swap = outs
    length, width = x.shape
    some = length // 2
    io.begin(x)
    ready()
    io.need(x)
    io.follow()

    def body(rows, carry):
        tile = x[rows]
        for number, ref in enumerate((query, key, value)):
            ref[rows] = mm(tile, weight[width * number : width * (number + 1)]).astype(bfloat)
        query_t[:, rows] = (query[rows] * bfloat(0.125)).T
        value_t[:, rows] = value[rows].T
        return carry

    by_rows(length, body)
    io.put(query, key, value)
    attend(scal[0], scal[1], key, query_t, value_t, ctx_t, lse, key_tiles)
    io.put(ctx_t, lse)
    io.rest()
    project_norm(io, length, ctx_t, weight.at[3 * width :], x, vec, resid, out)

    pl.when(scal[2] == 0)(lambda: pack_rows(packed, 0, out[some:]))
    io.put_if(scal[2] == 0, packed, swap.at[pl.ds(0, 3 * some)])


def self_forward_body(io, scal, x, weight, vec, *refs):
    io.begin(x)
    self_forward(io, scal, x, weight, vec, refs[:8], *refs[8:], lambda: io.need(weight))


def placed_forward_body(where, io, scal, table, x, vec, *refs):
    sources, refs = refs[: len(where)], refs[len(where) :]
    outs, (weight, rest) = refs[:8], refs[8:10]
    query_t, value_t, key_tiles, packed, semaphores = refs[10:]
    size = sources[0].shape[1]
    cut = weight.shape[0] // size
    io.begin(x)

    for source, ranges in zip(sources, where):
        for start, stop, distance, other, first in ranges:

            def step(slot, unused):
                piece = table[distance, first + slot - start]
                at = piece * 2 + (scal[5] if other == 0 else 1 - scal[5])

                def move(target, place, semaphore):
                    place = pl.ds(pl.multiple_of(place * size, size), size)
                    pltpu.make_async_copy(source.at[slot], target.at[place], semaphore).start()

                pl.when((piece >= 0) & (at < cut))(lambda: move(weight, at, semaphores.at[0]))
                pl.when(at >= cut)(lambda: move(rest, at - cut, semaphores.at[1]))
                return 0

            lax.fori_loop(start, stop, step, 0)

    def ready():
        pltpu.make_async_copy(weight, weight, semaphores.at[0]).wait()
        io.put(weight)

    self_forward(io, scal, x, weight, vec, outs, query_t, value_t, key_tiles, packed, ready)
    pltpu.make_async_copy(rest, rest, semaphores.at[1]).wait()
    io.put(rest)


def encoder_ff_body(
    io, scal, inner, up, down, cross, vec, held, activ, slope, resid, memory, swap, sendout
):
    length, width = inner.shape
    io.need(inner, up)
    io.follow(down)
    for rows in [pl.ds(0, length)]:
        act, grad = gelu_parts(mm_nt(inner[rows].astype(bfloat), up[...]))
        activ[rows] = act.astype(bfloat)
        slope[rows] = grad.astype(bfloat)
        for ref in (activ, slope):
            io.put_rows(ref, rows.start, rows.size)
    io.rest()
    for rows in [pl.ds(0, length)]:
        total = inner[rows] * vec[0:1] + mm(activ[rows], down[...])
        resid[rows] = total
        mem = (normed(total)[0] * vec[1:2] + vec[2:3]).astype(bfloat)
        memory[rows] = mem
        sendout[rows] = mm(mem, cross[:width]).astype(bfloat)
        sendout[pl.ds(length + rows.start, rows.size)] = mm(mem, cross[width:]).astype(bfloat)
        for ref in (resid, memory):
            io.put_rows(ref, rows.start, rows.size)
    io.put_if(scal[2] != 0, sendout, swap)


def ff_back(length, emit, grad_branch, activ, slope, inner_low, up, down, grad_inner):
    def body(rows, carry):
        grad = mm_nt(grad_branch[rows], down[...]) * slope[rows].astype(single)
        grad = grad.astype(bfloat)
        slope[rows] = grad
        grad_inner[rows] += mm(grad, up[...])
        return carry

    by_rows(length, body)
    for number in range(activ.shape[1] // 512):
        columns = slice(number * 512, (number + 1) * 512)
        emit(0, number, mm_tn(slope[:, columns], inner_low[...]))
        emit(1, number, mm_tn(activ[:, columns], grad_branch[...]))


def branch_back(length, resid, grad_out, inner, vec, grad_branch, grad_inner, grad_vec):
    width = resid.shape[1]

    def body(rows, carry):
        grad_resid, grad_gain, grad_shift = norm_back(resid[rows], grad_out[rows], vec[1:2])
        grad_branch[rows] = grad_resid.astype(bfloat)
        grad_inner[rows] = grad_resid * vec[0:1]
        weigh = jnp.sum(grad_resid * inner[rows].astype(single), 0, keepdims=True)
        return (carry[0] + weigh, carry[1] + grad_gain, carry[2] + grad_shift)

    put_rows(grad_vec, by_rows(length, body, zero_rows(width)))


def ctx_back(length, grad_branch, weight, ctx_t, grad_ctx, grad_ctx_t, dot_ref):
    def body(rows, carry):
        grad_ctx[rows] = mm_nt(grad_branch[rows], weight[...]).astype(bfloat)
        grad_ctx_t[:, rows] = grad_ctx[rows].T
        for head in range(HEADS):
            mine = slice(64 * head, 64 * head + 64)
            product = grad_ctx_t[mine, rows].astype(single) * ctx_t[mine, rows].astype(single)
            dot_ref[head : head + 1, rows] = jnp.sum(product, 0, keepdims=True)
        return carry

    by_rows(length, body)


def middle_body(
    io, scal, inner, packed, keys, cross, cross_vec, up, down, ff_vec, cotan,
    output, sendback, grad_inner, grads, grad_vec, swap,
    query, query_t, ctx_t, lse, resid, after, activ, slope, low_rows, grad_branch, grad_after,
    grad_ctx, grad_ctx_t, dot_ref, key_t, value_t, grad_key, grad_value, grad_query_t,
    key_tiles, key_two, value_two, swap_out,
):
    rows_here, width = inner.shape
    hidden, length = up.shape[0], keys.shape[0] // 2
    key_rows, value_rows = keys.at[:length], keys.at[length:]
    io.need(inner, packed, cross, keys)
    io.follow(cross_vec, up, down)

    @pl.when(scal[2] != 0)
    def _():
        inner[...] = unpack_rows(packed, rows_here)

    def project(rows, carry):
        query[rows] = mm(inner[rows].astype(bfloat), cross[:width]).astype(bfloat)
        query_t[:, rows] = (query[rows] * bfloat(0.125)).T
        return carry

    def turn(rows, carry):
        key_t[:, rows] = key_rows[rows].T
        value_t[:, rows] = value_rows[rows].T
        return carry

    by_rows(rows_here, project)
    by_rows(length, turn)
    attend(scal[4], None, key_rows, query_t, value_t, ctx_t, lse, key_tiles)
    io.rest()
    project_norm(io, rows_here, ctx_t, cross.at[width:], inner, cross_vec, resid, after)

    def feed(rows, carry):
        tile = after[rows]
        low_tile = tile.astype(bfloat)
        low_rows[rows] = low_tile
        act, grad = gelu_parts(mm_nt(low_tile, up[...]))
        act = act.astype(bfloat)
        activ[rows] = act
        slope[rows] = grad.astype(bfloat)
        total = tile * ff_vec[0:1] + mm(act, down[...])
        output[rows] = (normed(total)[0] * ff_vec[1:2] + ff_vec[2:3]).astype(bfloat)
        row = lax.broadcasted_iota(jnp.int32, tile.shape, 0) + rows.start
        grad_out = jnp.where(row < scal[3], cotan[rows].astype(single), 0.0)
        grad_resid, grad_gain, grad_shift = norm_back(total, grad_out, ff_vec[1:2])
        grad_branch[rows] = grad_resid.astype(bfloat)
        grad_after[rows] = grad_resid * ff_vec[0:1]
        weigh = jnp.sum(grad_resid * tile, 0, keepdims=True)
        return (carry[0] + weigh, carry[1] + grad_gain, carry[2] + grad_shift)

    put_rows(grad_vec.at[3:], by_rows(rows_here, feed, zero_rows(width)))
    io.put(output)

    def emit(which, number, value):
        first = 2 * width + which * hidden + number * 512
        grads[first : first + 512] = value.astype(bfloat)
        if which == 1 and number in (1, 3):
            for start in (2 * width, 2 * width + hidden):
                io.put_rows(grads, start + (number - 1) * 512, 1024)

    ff_back(rows_here, emit, grad_branch, activ, slope, low_rows, up, down, grad_after)
    branch_back(rows_here, resid, grad_after, inner, cross_vec, grad_branch, grad_inner, grad_vec)
    io.put(grad_vec)
    grads[width : 2 * width] = mm(ctx_t[...], grad_branch[...]).astype(bfloat)
    ctx_back(rows_here, grad_branch, cross.at[width:], ctx_t, grad_ctx, grad_ctx_t, dot_ref)
    attend_back(
        scal[4], None, query, key_rows, value_rows, query_t, key_t, grad_ctx, grad_ctx_t, lse, dot_ref,
        grad_key, grad_value, grad_query_t, key_two, value_two,
    )

    def send(rows, carry):
        sendback[rows] = (grad_key[rows] * 0.125).astype(bfloat)
        sendback[pl.ds(length + rows.start, rows.size)] = grad_value[rows].astype(bfloat)
        return carry

    by_rows(length, send)
    io.put(sendback)
    io.put_if(scal[2] == 0, sendback, swap)

    def last(rows, carry):
        grad_query = grad_query_t[:, rows].T
        grad_inner[rows] += mm_nt(grad_query, cross[:width])
        grad_ctx[rows] = grad_query
        return carry

    by_rows(rows_here, last)
    io.put(grad_inner)

    @pl.when(scal[2] != 0)
    def _():
        pack_rows(swap_out, 0, grad_inner[...])
        swap_out[3 * rows_here :] = output[...]

    io.put_if(scal[2] != 0, swap_out, swap)

    grads[:width] = mm_tn(inner[...].astype(bfloat), grad_ctx[...]).astype(bfloat)
    io.put_rows(grads, 0, 2 * width)


def encoder_back_body(
    io, scal, table, own, received, memory, cross, inner, resid, activ, slope, up, down, vec,
    grad_inner, grad_vec, *rest_of,
):
    length, width = inner.shape
    *targets, grad_mem, inner_low, grad_branch, stage, semaphores = rest_of
    emit = Emitter(table, targets, stage, semaphores)
    io.begin(own, received, cross, inner)
    io.follow(memory, vec, resid, down, slope, up, activ)
    io.need(own, received, cross, inner)

    def body(rows, carry):
        own[...] = added(own[...], received[...])
        grad_mem[rows] = mm_nt(own[:length], cross[:width]) + mm_nt(own[length:], cross[width:])
        inner_low[rows] = inner[rows].astype(bfloat)
        return carry

    by_rows(length, body)
    io.need(vec, resid, memory)
    emit.chunk(8, 16, mm_tn(memory[...], own[:length]))
    emit.chunk(9, 20, mm_tn(memory[...], own[length:]))
    branch_back(length, resid, grad_mem, inner, vec, grad_branch, grad_inner, grad_vec)
    io.put(grad_vec)
    io.rest()

    def each(which, number, value):
        emit.chunk(2 * number + which, 24 + 16 * which + 4 * number, value)

    ff_back(length, each, grad_branch, activ, slope, inner_low, up, down, grad_inner)
    io.put(grad_inner)
    emit.wait()


def self_back_body(
    io, scal, table, x, weight, out_weight, vec, resid, query, key, value, ctx_t, lse, grad_out, packed, *refs
):
    length, width = x.shape
    count = (len(refs) - 15) // 2
    grad_x, grad_vec, *targets = refs[count : 2 * count + 2]
    (
        grad_branch, grad_ctx, grad_ctx_t, dot_ref, query_t, key_t, grad_key, grad_value, grad_query_t,
        key_two, value_two, stage, semaphores,
    ) = refs[2 * count + 2 :]
    emit = Emitter(table, targets, stage, semaphores)
    some = length // 2
    io.need(resid, grad_out, packed, x, vec)
    io.follow(ctx_t, out_weight, query, key, value)

    @pl.when(scal[2] == 0)
    def _():
        grad_out[some:] = unpack_rows(packed, some)

    branch_back(length, resid, grad_out, x, vec, grad_branch, grad_x, grad_vec)
    io.put(grad_vec)
    io.need(ctx_t, out_weight)
    emit.chunk(3, 12, mm(ctx_t[...], grad_branch[...]))
    ctx_back(length, grad_branch, out_weight, ctx_t, grad_ctx, grad_ctx_t, dot_ref)
    io.rest()

    def body(rows, carry):
        query_t[:, rows] = (query[rows] * bfloat(0.125)).T
        key_t[:, rows] = key[rows].T
        return carry

    by_rows(length, body)
    attend_back(
        scal[0], scal[1], query, key, value, query_t, key_t, grad_ctx, grad_ctx_t, lse, dot_ref,
        grad_key, grad_value, grad_query_t, key_two, value_two,
    )

    def last(rows, carry):
        parts = (
            grad_query_t[:, rows].T,
            (grad_key[rows] * 0.125).astype(bfloat),
            grad_value[rows].astype(bfloat),
        )
        total = grad_x[rows]
        for number, low_grad in enumerate(parts):
            total += mm_nt(low_grad, weight[width * number : width * (number + 1)])
        grad_x[rows] = total
        grad_branch[rows], grad_ctx[rows], value[rows] = parts
        return carry

    by_rows(length, last)
    io.put(grad_x)
    for number, ref in enumerate((grad_branch, grad_ctx, value)):
        emit.chunk(number, 4 * number, mm_tn(x[...], ref[...]))
    emit.wait()


def merge_body(io, scal, table, own, other, *refs):
    count = (len(refs) - 2) // 2
    *targets, stage, semaphores = refs[count:]
    emit = Emitter(table, targets, stage, semaphores)
    io.rest()
    chunk = stage.shape[1]
    for number in range(own.shape[0] // chunk):
        rows = slice(number * chunk, (number + 1) * chunk)
        total = own[rows].astype(single) + other[rows].astype(single)
        emit.chunk(number, 16 + 4 * number, total)
    emit.wait()


RING = (0, 2, 4, 6, 7, 5, 3, 1)
LEAD = 6
LEVEL = 10
FLOW = 8


def lend_kernel(scal, owners, master, own_out, up_out, down_out, plan, counts, low_rows, loaded, sems):
    size = len(RING)
    load = pltpu.make_async_copy(master, loaded, sems.at[0])
    load.start()
    for place in range(size):
        counts[place] = 0

    def count(piece, unused):
        owner = owners[piece]
        place = jnp.where(owner % 2 == 0, owner // 2, size - 1 - owner // 2)
        counts[place] = counts[place] + 1
        return 0

    lax.fori_loop(0, owners.shape[0], count, 0)
    held = [counts[place] for place in range(size)]
    caps = [jnp.int32(FLOW)] * size
    for place in list(range(size - 1, -1, -1)) * 2:
        after = (place + 1) % size
        caps[place] = jnp.minimum(FLOW, caps[after] - held[after] + LEVEL)
    flows = [jnp.minimum(0, cap) for cap in caps]
    for place in list(range(size)) * 2:
        flows[place] = jnp.maximum(flows[place], flows[place - 1] + held[place] - LEVEL)
    for place in range(size):
        ahead = jnp.maximum(flows[place], 0)
        back = jnp.maximum(-flows[place - 1], 0)
        plan[0, place] = held[place] - ahead - back
        plan[1, place] = ahead
        plan[2, place] = back
    load.wait()
    rows = loaded.shape[0]
    low_rows[:rows] = loaded[...].astype(bfloat)
    kept = plan[0, scal[0]]
    copies = [
        pltpu.make_async_copy(low_rows.at[pl.ds(0, rows)], own_out, sems.at[0]),
        pltpu.make_async_copy(low_rows.at[pl.ds(kept, FLOW)], up_out, sems.at[1]),
        pltpu.make_async_copy(
            low_rows.at[pl.ds(kept + plan[1, scal[0]], FLOW)], down_out, sems.at[2]
        ),
    ]
    for copy in copies:
        copy.start()
    for copy in copies:
        copy.wait()


def borrow_kernel(scal, plan, own, below, above, lead_out, late_out, slots, sems, out_sems):
    size = len(RING)
    kept = plan[0, scal[0]]
    from_below = kept + plan[1, (scal[0] + size - 1) % size]
    from_above = from_below + plan[2, (scal[0] + 1) % size]
    for slot in range(LEVEL):

        def move(source, slot=slot):
            pltpu.make_async_copy(source, slots.at[slot], sems.at[slot]).start()

        pl.when(slot < kept)(lambda slot=slot, move=move: move(own.at[slot]))
        pl.when((slot >= kept) & (slot < from_below))(
            lambda slot=slot, move=move: move(below.at[slot - kept])
        )
        pl.when((slot >= from_below) & (slot < from_above))(
            lambda slot=slot, move=move: move(above.at[slot - from_below])
        )
    for slot in range(LEVEL):
        pl.when(slot < from_above)(pltpu.make_async_copy(own.at[0], slots.at[slot], sems.at[slot]).wait)
    copies = [
        pltpu.make_async_copy(slots.at[pl.ds(0, LEAD)], lead_out, out_sems.at[0]),
        pltpu.make_async_copy(slots.at[pl.ds(LEAD, LEVEL - LEAD)], late_out, out_sems.at[1]),
    ]
    for copy in copies:
        copy.start()
    for copy in copies:
        copy.wait()


def lend(position, owner_row, master):
    slot = master.shape[1:]
    rows = master.shape[0]
    where = position[None].astype(jnp.int32)
    own, up, down, plan = pl.pallas_call(
        lend_kernel,
        in_specs=[SM, SM, HB],
        out_specs=[HB, HB, HB, SM],
        out_shape=[
            low(rows, *slot),
            low(FLOW, *slot),
            low(FLOW, *slot),
            jax.ShapeDtypeStruct((3, len(RING)), jnp.int32),
        ],
        scratch_shapes=[
            pltpu.SMEM((len(RING),), jnp.int32),
            low_vm(rows + FLOW, *slot),
            full_vm(rows, *slot),
            pltpu.SemaphoreType.DMA((3,)),
        ],
        name="lend",
    )(where, owner_row, master)
    below, above = round_ring(up, 1), round_ring(down, -1)
    lead, late = pl.pallas_call(
        borrow_kernel,
        in_specs=[SM, SM, HB, HB, HB],
        out_specs=[HB, HB],
        out_shape=[low(LEAD, *slot), low(LEVEL - LEAD, *slot)],
        scratch_shapes=[
            low_vm(LEVEL, *slot),
            pltpu.SemaphoreType.DMA((LEVEL,)),
            pltpu.SemaphoreType.DMA((2,)),
        ],
        name="borrow",
    )(where, plan, own, below, above)
    return lead, late, plan


def adam_kept_body(
    io, scal, plan, sums, master, first, second, new_first, new_second, new_master, new_copy
):
    io.rest()
    count, place = master.shape[0], scal[6]
    kept = plan[0, place]
    held = kept + plan[1, place] + plan[2, place]

    def update(slot, gradient):
        weight, one, two = adam(
            master[slot], gradient, first[slot], second[slot], rate_matrix, decay_matrix
        )
        new_first[slot], new_second[slot], new_master[slot] = one, two, weight
        new_copy[slot] = weight.astype(bfloat)

    def step(slot, unused):
        pl.when(slot < kept)(lambda: update(slot, sums[slot]))
        pl.when(slot >= held)(lambda: update(slot, jnp.zeros(master.shape[1:], single)))
        return 0

    for start in range(0, count, count // 2):
        lax.fori_loop(start, start + count // 2, step, 0)
        for ref in (new_first, new_second, new_master, new_copy):
            io.put_rows(ref, start, count // 2)


def adam_lent_body(
    io, scal, plan, below, above, master, first, second, one_held, two_held, weight_held, copy_held,
    new_first, new_second, new_master, new_copy,
    states, gradients, results, low_result, in_sems, out_sems,
):
    count, place = master.shape[0], scal[6]
    kept = plan[0, place]
    from_above = kept + plan[1, place]
    held = from_above + plan[2, place]

    def each(act):
        def step(slot, unused):
            pl.when((slot >= kept) & (slot < held))(lambda: act(slot))
            return 0

        lax.fori_loop(0, count, step, 0)

    def copies_in(slot):
        sources = [ref.at[slot] for ref in (master, first, second)]
        return [
            pltpu.make_async_copy(source, states.at[number, slot], in_sems.at[number, slot])
            for number, source in enumerate(sources)
        ]

    def copies_out(slot):
        outs = [
            pltpu.make_async_copy(results.at[number, slot], ref.at[slot], out_sems.at[number, slot])
            for number, ref in enumerate((new_first, new_second, new_master))
        ]
        return outs + [
            pltpu.make_async_copy(low_result.at[slot], new_copy.at[slot], out_sems.at[3, slot])
        ]

    def begin(slot):
        for copy in copies_in(slot):
            copy.start()

        def fetch(source):
            pltpu.make_async_copy(source, gradients.at[slot], in_sems.at[3, slot]).start()

        pl.when(slot < from_above)(lambda: fetch(above.at[slot - kept]))
        pl.when(slot >= from_above)(lambda: fetch(below.at[slot - from_above]))

    def update(slot):
        for copy in copies_in(slot):
            copy.wait()
        pltpu.make_async_copy(below.at[0], gradients.at[slot], in_sems.at[3, slot]).wait()
        weight, one, two = adam(
            states[0, slot],
            gradients[slot].astype(single),
            states[1, slot],
            states[2, slot],
            rate_matrix,
            decay_matrix,
        )
        results[0, slot], results[1, slot], results[2, slot] = one, two, weight
        low_result[slot] = weight.astype(bfloat)
        for copy in copies_out(slot):
            copy.start()

    def end(slot):
        for copy in copies_out(slot):
            copy.wait()

    each(begin)
    each(update)
    each(end)


def round_ring(value, step):
    count = len(RING)
    return lax.ppermute(value, "wide", [(RING[i], RING[(i + step) % count]) for i in range(count)])


def swapped(value):
    return lax.ppermute(value, "narrow", [(0, 1), (1, 0)])


def step_of(up, down, across):
    return lax.optimization_barrier((round_ring(up, 1), round_ring(down, -1), swapped(across)))


def partner(value, axis, bit):
    return lax.ppermute(value, axis, [(i, i ^ bit) for i in range(lax.axis_size(axis))])


def join(*values):
    return jnp.concatenate(values, 0)


def ring_gather(own_lead, own_late, tables):
    lead, late, half = LEAD, LEVEL - LEAD, LEAD // 2
    found = [([(0, lead, 0, 0, 0)], own_lead), ([(0, late, 0, 0, lead)], own_late)]

    def ahead(value, far, near):
        ranges = [(0, lead, far, 0, 0)]
        if near is not None:
            ranges += [(lead, lead + late, near, 0, lead), (lead + late, lead + 2 * late, near, 1, lead)]
        found.append((ranges, value))

    up, down, across = step_of(own_lead, own_lead, own_late)
    found.append(([(0, late, 0, 1, lead)], across))
    ahead(up, 7, None)
    ahead(down, 1, None)
    pair = join(own_late, across)
    up, down, across = step_of(join(up, pair), join(down, pair), join(up, down, own_lead[:half]))
    found.append(
        ([(0, lead, 7, 1, 0), (lead, 2 * lead, 1, 1, 0), (2 * lead, 2 * lead + half, 0, 1, 0)], across)
    )
    up, tables = lax.optimization_barrier((up, tables))
    ahead(up, 6, 7)
    ahead(down, 2, 1)
    up, down, across = step_of(up, down, join(up[:lead], down[:lead], own_lead[half:]))
    found.append(
        ([(0, lead, 6, 1, 0), (lead, 2 * lead, 2, 1, 0), (2 * lead, 2 * lead + half, 0, 1, half)], across)
    )
    ahead(up, 5, 6)
    ahead(down, 3, 2)
    up, down, across = step_of(join(up[:half], up[lead:]), down[half:], join(up[:lead], down[:lead]))
    found.append(([(0, lead, 5, 1, 0), (lead, 2 * lead, 3, 1, 0)], across))
    for value, first, near in ((up, 0, 5), (down, half, 3)):
        ranges = [(0, half, 4, 0, first), (half, half + late, near, 0, lead)]
        found.append((ranges + [(half + late, half + 2 * late, near, 1, lead)], value))
    up, down, across = step_of(
        up[half : half + late], down[half + late :], join(up[:half], down[:half])
    )
    found.append(([(0, late, 4, 0, lead)], up))
    found.append(([(0, late, 4, 1, lead)], down))
    found.append(([(0, lead, 4, 1, 0)], across))
    return found, tables


def added(*values):
    return sum(value.astype(single) for value in values).astype(bfloat)


def ring_scatter(grads, far, vector):
    partners = [("narrow", 1), ("wide", 1), ("wide", 2), ("wide", 4), ("half", 1)]

    def step_of(*values):
        nonlocal vector
        ring = (round_ring(values[0], 1), round_ring(values[1], -1), swapped(values[2]))
        *ring, other = lax.optimization_barrier((*ring, partner(vector, *partners.pop(0))))
        vector = vector + other
        return ring

    lead, half = LEAD, LEAD // 2
    late = grads.shape[2] - lead

    def both(distance):
        return grads[distance, :, lead:].reshape((-1,) + grads.shape[3:])

    def mine(distance, start=0, stop=lead):
        return grads[distance, 0, start:stop]

    def other(distance, start=0, stop=lead):
        return grads[distance, 1, start:stop]

    across, down, up = far
    up, down, across = step_of(up, down, across)
    first = added(mine(4), across)
    up = join(first[:half], added(up, grads[3, 0, lead:]), grads[3, 1, lead:])
    down = join(first[half:], grads[5, 0, lead:], added(down, grads[5, 1, lead:]))
    up, down, across = step_of(up, down, join(other(3), other(5)))
    up = join(
        added(mine(3, 0, half), across[:half], up[:half]),
        added(mine(3, half), across[half:lead]),
        added(up[half:], both(2)),
    )
    down = join(
        added(mine(5, 0, half), across[lead : lead + half]),
        added(mine(5, half), across[lead + half :], down[:half]),
        added(down[half:], both(6)),
    )
    up, down, across = step_of(up, down, join(other(2), other(6), other(0, 0, half)))
    nearest = [across[2 * lead :]]
    up = join(added(mine(2), across[:lead], up[:lead]), added(up[lead:], both(1)))
    down = join(added(mine(6), across[lead : 2 * lead], down[:lead]), added(down[lead:], both(7)))
    up, down, across = step_of(up, down, join(other(1), other(7), other(0, half)))
    nearest.append(across[2 * lead :])
    total = sum(value.astype(single) for value in (both(0), up[lead:], down[lead:]))
    up, down, across = step_of(
        added(mine(1), across[:lead], up[:lead]),
        added(mine(7), across[lead : 2 * lead], down[:lead]),
        total[late:].astype(bfloat),
    )
    first = sum(value.astype(single) for value in (mine(0), join(*nearest), up, down))
    return join(first, total[:late] + across.astype(single)), vector


def shaped(*shape, dtype=single):
    return jax.ShapeDtypeStruct(shape, dtype)


def low(*shape):
    return jax.ShapeDtypeStruct(shape, bfloat)


def low_vm(*shape):
    return pltpu.VMEM(shape, bfloat)


def full_vm(*shape):
    return pltpu.VMEM(shape, single)


def sum_over(value, axis):
    size = lax.axis_size(axis)
    bit = 1
    while bit < size:
        value = value + partner(value, axis, bit)
        bit *= 2
    return value


def adam(weight, gradient, first, second, step_rate, decay_rate):
    first_new = beta_one * first + (1.0 - beta_one) * gradient
    second_new = beta_two * second + (1.0 - beta_two) * gradient * gradient
    first_hat = first_new / (1.0 - beta_one**STEP)
    second_hat = second_new / (1.0 - beta_two**STEP)
    weight_new = weight - step_rate * (
        first_hat / (jnp.sqrt(second_hat) + eps_adam) + decay_rate * weight
    )
    return (weight_new, first_new, second_new)


def on_device(
    stream, cotangent, lengths, owners, master, moment_one, moment_two, vec_master, vec_one, vec_two
):
    narrow_size = lax.axis_size("narrow")
    wide_size = lax.axis_size("wide")
    owner_row = owners[0]
    capacity = master.shape[1]
    half_rows = master.shape[2]
    width = master.shape[3]
    count = owner_row.shape[0]
    counter = jnp.arange(count)
    same = owner_row[:, None] == owner_row[None, :]
    earlier = counter[None, :] < counter[:, None]
    ranks = jnp.sum((same & earlier).astype(jnp.int32), 1)
    on_ring = (wide_size, narrow_size, capacity, count) == (len(RING), 2, 14, 56)
    wide_at, narrow_at = lax.axis_index("wide"), lax.axis_index("narrow")
    self_rows, rest_rows = 4 * width, count * half_rows * narrow_size - 4 * width
    is_source = lax.axis_index("half") == 0
    x = stream[0, 0]
    length = x.shape[0]
    some = length // 2
    source_len, target_len = lengths[0, 0], lengths[1, 0]
    flag = is_source.astype(jnp.int32)
    position = jnp.where(wide_at % 2 == 0, wide_at // 2, wide_size - 1 - wide_at // 2)
    scal = jnp.stack(
        [
            jnp.where(is_source, source_len, target_len),
            1 - flag,
            flag,
            jnp.where(is_source, target_len - some, target_len),
            source_len,
            narrow_at,
            position,
        ]
    ).astype(jnp.int32)
    if on_ring:
        capacity = LEVEL
        own_lead, own_late, plan = lend(position, owner_row.astype(jnp.int32), master[0])
        place = jnp.where(owner_row % 2 == 0, owner_row // 2, wide_size - 1 - owner_row // 2)
        kept, ahead, back = (jnp.take(row, place) for row in plan)
        moved = (ranks >= kept).astype(jnp.int32) - 2 * (ranks >= kept + ahead).astype(jnp.int32)
        place = (place + moved) % wide_size
        base = jnp.take(plan[0], place)
        below = jnp.take(plan[1], (place - 1) % wide_size)
        ranks = jnp.where(
            moved == 0,
            ranks,
            jnp.where(moved > 0, base + ranks - kept, base + below + ranks - kept - ahead),
        )
        distance = (place - position) % wide_size
        halves = jnp.arange(narrow_size)[None, :] ^ narrow_at
        table = (distance[:, None] * 2 + halves) * capacity + ranks[:, None]
        total, late = wide_size * 2 * capacity, capacity - LEAD
        is_late = (ranks >= LEAD)[:, None]
        after_late = ranks[:, None] - LEAD + total + LEAD
        far = jnp.where(
            halves == 1,
            jnp.where(is_late, after_late, ranks[:, None] + total),
            jnp.where(is_late, after_late + late, table),
        )
        table = jnp.where(distance[:, None] == 4, far, table).reshape(-1)
        slot_of = distance * capacity + ranks
        hit = slot_of[None, :] == jnp.arange(wide_size * capacity)[:, None]
        pieces = jnp.sum(hit.astype(jnp.int32) * (counter + 1)[None, :], 1) - 1
        pieces = pieces.reshape(wide_size, capacity).astype(jnp.int32)
        found, (pieces, table, scal) = ring_gather(
            own_lead, own_late, (pieces, table.astype(jnp.int32), scal)
        )
    else:
        places = (
            owner_row[:, None] * narrow_size + jnp.arange(narrow_size)[None, :]
        ) * capacity + ranks[:, None]
        table = places.reshape(-1)
        own = master[0].astype(bfloat)
        gathered = lax.all_gather(own, ("wide", "narrow"), axis=0, tiled=True)
        weight = jnp.take(gathered, table, axis=0).reshape(-1, width)
        weight, rest = weight[:self_rows], weight[self_rows:]
    table = table.astype(jnp.int32)
    hidden = (rest_rows - 2 * width) // 2
    self_vec = whole(jnp.where(is_source, vec_master[0:3], vec_master[6:9]))
    cross_vec, ff_vec = whole(vec_master[9:12]), whole(vec_master[12:15])
    memory_vec = whole(vec_master[3:6])
    total = capacity * wide_size * narrow_size
    cuts = [total, LEAD, capacity - LEAD, capacity - LEAD] if on_ring else [total]
    slots = [low(size, half_rows, width) for size in cuts]
    slot_outs = [("hbm", one) for one in slots]

    def stage_of(chunks):
        return [
            low_vm(chunks, 512, width),
            pltpu.SemaphoreType.DMA((chunks * 512 // half_rows,)),
        ]

    def store(*shape, dtype=single):
        return ("store", shaped(*shape, dtype=dtype))

    low_out = partial(store, dtype=bfloat)
    two, four = low_vm(2, length, 128), low_vm(4, length, 128)
    down_half, up_half, both_halves = [(1, 0)], [(0, 1)], [(0, 1), (1, 0)]

    forward_outs = (
        [low_out(length, width)] * 3
        + [low_out(width, length), store(HEADS, length)]
        + [store(length, width)] * 2
        + [("hbm", low(2 * length, width))]
    )
    forward_scratch = [low_vm(width, length), low_vm(width, length), four, low_vm(3 * some, width)]
    if on_ring:
        *forward, weight, rest = call(
            partial(placed_forward_body, [where for where, unused in found]),
            "self_forward",
            scal,
            None,
            [("smem", pieces), whole(x), self_vec] + [("hbm", value) for unused, value in found],
            forward_outs + [low_out(self_rows, width), low_out(rest_rows, width)],
            forward_scratch + [pltpu.SemaphoreType.DMA((2,))],
        )
    else:
        forward = call(
            self_forward_body,
            "self_forward",
            scal,
            None,
            [whole(x), whole(weight), self_vec],
            forward_outs,
            forward_scratch,
        )
    query, key, value, ctx_t, lse, resid, inner, swap = forward
    rest_other = lax.ppermute(rest, "half", down_half)
    cross_w = part(rest, 0, 2 * width)
    up_w = part(rest, 2 * width, hidden)
    down_w = part(rest, 2 * width + hidden, hidden)
    activ, slope, ff_resid, memory, swap = call(
        encoder_ff_body,
        "encoder_ff",
        scal,
        1,
        [whole(inner), up_w, down_w, cross_w, memory_vec, ("hbm", swap)],
        [low_out(length, hidden)] * 2
        + [store(length, width), low_out(length, width), ("hbm", low(2 * length, width))],
        [low_vm(2 * length, width)],
        [(5, 4)],
    )
    swap_other = lax.ppermute(swap, "half", both_halves)

    def shared(first, rows):
        return either([(rest_other, first, 0, rows)], [(rest, first, 0, rows)])

    mid_inner = either([], [(inner, 0, 0, some)])
    mid_packed = either([(swap_other, 0, 0, 3 * some)], [])
    keys = either([(swap, 0, 0, None)], [(swap_other, 0, 0, None)])
    cotan = cotangent[0]
    output, sendback, grad_one, grad_rest, grad_middle_vec, swap = call(
        middle_body,
        "decoder_middle",
        scal,
        None,
        [
            mid_inner,
            mid_packed,
            keys,
            shared(0, 2 * width),
            cross_vec,
            shared(2 * width, hidden),
            shared(2 * width + hidden, hidden),
            ff_vec,
            either([(cotan, some, 0, some)], [(cotan, 0, 0, some)]),
        ],
        [
            low_out(some, width),
            low_out(2 * length, width),
            store(some, width),
            low_out(rest_rows, width),
            store(6, width),
            ("hbm", low(2 * length, width)),
        ],
        [low_vm(some, width), low_vm(width, some), low_vm(width, some), full_vm(HEADS, some)]
        + [full_vm(some, width), full_vm(some, width), low_vm(some, hidden), low_vm(some, hidden)]
        + [low_vm(some, width), low_vm(some, width), full_vm(some, width)]
        + [low_vm(some, width), low_vm(width, some), full_vm(HEADS, some)]
        + [low_vm(width, length), low_vm(width, length)]
        + [full_vm(length, width), full_vm(length, width), low_vm(width, some), four, two, two]
        + [low_vm(2 * length, width)],
    )
    swap_other = lax.ppermute(swap, "half", both_halves)
    grad_rest, swap_other = lax.optimization_barrier((grad_rest, swap_other))
    grad_rest_other = lax.ppermute(grad_rest, "half", up_half)
    output = join(output, swap_other[3 * some :])
    grad_inner, grad_memory_vec, *target = call(
        encoder_back_body,
        "encoder_back",
        scal,
        1,
        [
            ("smem", table),
            whole(sendback),
            whole(swap_other),
            whole(memory),
            cross_w,
            whole(inner),
            whole(ff_resid),
            whole(activ),
            whole(slope),
            up_w,
            down_w,
            memory_vec,
        ],
        [store(length, width), store(3, width)] + slot_outs,
        [full_vm(length, width), low_vm(length, width), low_vm(length, width)] + stage_of(10),
    )
    back_scratch = (
        [low_vm(length, width), low_vm(length, width), low_vm(width, length), full_vm(HEADS, length)]
        + [low_vm(width, length), low_vm(width, length)]
        + [full_vm(length, width), full_vm(length, width), low_vm(width, length), two, two]
    )
    grad_x, grad_self_vec, *target = call(
        self_back_body,
        "self_back",
        scal,
        None,
        [
            ("smem", table),
            whole(x),
            part(weight, 0, 3 * width),
            part(weight, 3 * width, width),
            self_vec,
            whole(resid),
            whole(query),
            whole(key),
            whole(value),
            whole(ctx_t),
            whole(lse),
            either(
                [(grad_inner, 0, 0, length)],
                [(grad_one, 0, 0, some)],
            ),
            either([], [(swap_other, 0, 0, 3 * some)]),
        ]
        + [("hbm", one) for one in target],
        [store(length, width), store(3, width)] + slot_outs,
        back_scratch + stage_of(4),
        [(13 + number, 2 + number) for number in range(len(slots))],
    )
    target = call(
        merge_body,
        "merge",
        scal,
        0,
        [
            ("smem", table),
            whole(grad_rest),
            whole(grad_rest_other),
        ]
        + [("hbm", one) for one in target],
        slot_outs,
        stage_of(10),
        [(3 + number, number) for number in range(len(slots))],
    )
    vec_grads = jnp.concatenate(
        [
            jnp.where(is_source, grad_self_vec, 0.0),
            jnp.where(is_source, grad_memory_vec, 0.0),
            jnp.where(is_source, 0.0, grad_self_vec),
            grad_middle_vec,
        ],
        0,
    )
    if on_ring:
        grads = target[0].reshape(wide_size, 2, capacity, half_rows, width)
        mine, vec_grads = ring_scatter(grads, target[1:], vec_grads)
    else:
        mine = lax.psum_scatter(target[0], ("wide", "narrow"), scatter_dimension=0, tiled=True)
        for axis in ("narrow", "wide", "half"):
            vec_grads = sum_over(vec_grads, axis)
    if on_ring:
        sums = join(mine, jnp.zeros((FLOW, half_rows, width), single))
        cut = plan[0][position]
        lent = lax.dynamic_slice_in_dim(sums, cut, FLOW, 0).astype(bfloat)
        cut = cut + plan[1][(position - 1) % wide_size]
        lent_above = lax.dynamic_slice_in_dim(sums, cut, FLOW, 0).astype(bfloat)
        above, below = round_ring(lent, -1), round_ring(lent_above, 1)
        states = (master[0], moment_one[0], moment_two[0])
        state = states[0].shape
        results = call(
            adam_kept_body,
            "adam_kept",
            scal,
            None,
            [("smem", plan), whole(mine)] + [whole(one) for one in states],
            [store(*state)] * 3 + [low_out(*state)],
            [],
        )
        new_first, new_second, new_weight, new_copy = call(
            adam_lent_body,
            "adam_lent",
            scal,
            None,
            [("smem", plan), ("hbm", below), ("hbm", above)]
            + [("hbm", one) for one in states]
            + [("hbm", one) for one in results],
            [("hbm", shaped(*state))] * 3 + [("hbm", low(*state))],
            [
                full_vm(3, *state),
                low_vm(*state),
                full_vm(3, *state),
                low_vm(*state),
                pltpu.SemaphoreType.DMA((4, state[0])),
                pltpu.SemaphoreType.DMA((4, state[0])),
            ],
            [(6 + number, number) for number in range(4)],
        )
    else:
        used = jnp.sum((owner_row == wide_at).astype(jnp.int32))
        mine = jnp.where((jnp.arange(capacity) < used)[:, None, None], mine.astype(single), 0.0)
        new_weight, new_first, new_second = adam(
            master[0], mine, moment_one[0], moment_two[0], rate_matrix, decay_matrix
        )
        new_copy = new_weight.astype(bfloat)
    vec_weight, vec_first, vec_second = adam(
        vec_master, vec_grads, vec_one, vec_two, rate_vector, 0.0
    )
    return (
        jnp.where(is_source, memory, output)[None, None],
        grad_x[None, None],
        new_first[None],
        new_second[None],
        new_weight[None],
        new_copy[None],
        vec_first,
        vec_second,
        vec_weight,
    )


def solution(mesh):
    in_specs = (
        P("half", ("wide", "narrow"), None, None),
        P(("wide", "narrow"), None, None),
        P(None, ("wide", "narrow")),
        P("half", None),
        P("half", "wide", "narrow", None),
        P("half", "wide", "narrow", None),
        P("half", "wide", "narrow", None),
        P(),
        P(),
        P(),
    )
    out_specs = (
        P("half", ("wide", "narrow"), None, None),
        P("half", ("wide", "narrow"), None, None),
        P("half", "wide", "narrow", None),
        P("half", "wide", "narrow", None),
        P("half", "wide", "narrow", None),
        P("half", "wide", "narrow", None),
        P(),
        P(),
        P(),
    )
    return jax.shard_map(
        on_device, mesh=mesh, in_specs=in_specs, out_specs=out_specs, check_vma=False
    )
```

```python
import math
from functools import partial

import jax
import jax.numpy as jnp
from jax import lax
from jax.experimental import pallas as pl
from jax.experimental.pallas import tpu as pltpu
from jax.sharding import PartitionSpec as P

HEADS = 8
STEP = 5
CAUSAL = 512
RB = 1024
NEG = -1e30

eps_norm = 1e-05
beta_one = 0.5
beta_two = 0.5
rate_matrix = 0.05
rate_vector = 0.3
decay_matrix = 0.01
eps_adam = 1e-08
bfloat = jnp.bfloat16
single = jnp.float32
VM = pl.BlockSpec(memory_space=pltpu.VMEM)
SM = pl.BlockSpec(memory_space=pltpu.SMEM)
HB = pl.BlockSpec(memory_space=pl.ANY)


def mm(left, right):
    return jnp.dot(left, right, preferred_element_type=single)


def mm_tn(left, right):
    return lax.dot_general(left, right, (((0,), (0,)), ((), ())), preferred_element_type=single)


def mm_nt(left, right):
    return lax.dot_general(left, right, (((1,), (1,)), ((), ())), preferred_element_type=single)


def block_of(index, size):
    return pl.ds(pl.multiple_of(index * size, size), size)


def normed(resid):
    center = resid - jnp.mean(resid, -1, keepdims=True)
    spread = jnp.mean(center * center, -1, keepdims=True)
    rstd = lax.rsqrt(spread + eps_norm)
    return center * rstd, rstd


def norm_back(resid, grad, gain):
    hat, rstd = normed(resid)
    grad_hat = grad * gain
    grad_resid = rstd * (
        grad_hat
        - jnp.mean(grad_hat, -1, keepdims=True)
        - hat * jnp.mean(grad_hat * hat, -1, keepdims=True)
    )
    return grad_resid, jnp.sum(grad * hat, 0, keepdims=True), jnp.sum(grad, 0, keepdims=True)


def gelu_parts(pre_act):
    half = 0.5 * (1.0 + lax.erf(pre_act * math.sqrt(0.5)))
    slope = half + pre_act * (jnp.exp(-0.5 * pre_act * pre_act) * (1.0 / math.sqrt(2.0 * math.pi)))
    return pre_act * half, slope


def pair_keys(tile, first_extra, ones):
    rows = tile.shape[0]
    lane = lax.broadcasted_iota(jnp.int32, (rows, 128), 1)
    wide_tile = tile.astype(single)
    out = []
    for head in range(2):
        at = lane - (64 - 64 * head)
        extra = jnp.where(at == 0, first_extra, jnp.where((at > 0) & (at < ones), 1.0, 0.0))
        mine = (lane < 64) if head == 0 else (lane >= 64)
        out.append(jnp.where(mine, wide_tile, extra).astype(bfloat))
    return out


def pair_queries(tile, head, extra_rows):
    mine = tile[64 * head : 64 * head + 64]
    row = lax.broadcasted_iota(jnp.int32, mine.shape, 0)
    extra = jnp.zeros(mine.shape, single)
    for number, value in enumerate(extra_rows):
        extra = jnp.where(row == number, value, extra)
    extra = extra.astype(bfloat)
    return jnp.concatenate([mine, extra] if head == 0 else [extra, mine], 0)


def pack_rows(target, first, value):
    rows = value.shape[0]
    for number, one in enumerate(split_three(value)):
        target[first + number * rows : first + (number + 1) * rows] = one.astype(bfloat)


def unpack_rows(packed, rows):
    high, middle, rest = (packed[n * rows : (n + 1) * rows].astype(single) for n in range(3))
    return (high + middle) + rest


def split_three(value):
    high = value.astype(bfloat).astype(single)
    rest = value - high
    middle = rest.astype(bfloat).astype(single)
    return [high, middle, rest - middle]


def key_bias(limit, rows):
    row = lax.broadcasted_iota(jnp.int32, (rows, 128), 0)
    return jnp.where(row < limit, 0.0, NEG)


def score_parts(scores, diagonal):
    if not diagonal:
        return [scores]
    size = scores.shape[1]
    cut = scores.shape[0] - size
    row = lax.broadcasted_iota(jnp.int32, (size, size), 0)
    column = lax.broadcasted_iota(jnp.int32, (size, size), 1)
    last = jnp.where(row <= column, scores[cut:], NEG)
    return [scores[:cut], last] if cut else [last]


def over_blocks(causal, rows, length, body):
    def every():
        body(0, rows, length, False)

    if causal is None:
        every()
        return
    pl.when(causal == 0)(every)

    @pl.when(causal != 0)
    def _():
        for first in range(0, rows, CAUSAL):
            body(first, CAUSAL, first + CAUSAL, True)


def head_rows(group, heads, head):
    return pl.ds(pl.multiple_of((group * heads + head) * 64, 64), 64)


def attend(limit, causal, key_ref, query_t, value_t, ctx_t, lse_ref, key_tiles):
    length, width = key_ref.shape
    heads = key_tiles.shape[0]
    bias = key_bias(limit, length)

    def group_of(group, unused):
        for number in range(heads // 2):
            columns = block_of(group * (heads // 2) + number, 128)
            for head, tile in enumerate(pair_keys(key_ref[:, columns], bias, 1)):
                key_tiles[2 * number + head] = tile

        def body(first, queries, extent, diagonal):
            at = slice(first, first + queries)

            def scores_of(head):
                columns = block_of(group * (heads // 2) + head // 2, 128)
                tile = pair_queries(query_t[columns, at], head % 2, [1.0])
                return mm(key_tiles[head, :extent], tile)

            following = scores_of(0)
            for head in range(heads):
                parts = score_parts(following, diagonal)
                if head + 1 < heads:
                    following = scores_of(head + 1)
                top = jnp.max(parts[0], 0, keepdims=True)
                for more in parts[1:]:
                    top = jnp.maximum(top, jnp.max(more, 0, keepdims=True))
                parts = [jnp.exp(more - top) for more in parts]
                total = sum(jnp.sum(more, 0, keepdims=True) for more in parts)
                weights = jnp.concatenate([more.astype(bfloat) for more in parts], 0)
                mine = head_rows(group, heads, head)
                context = mm(value_t[mine, :extent], weights)
                ctx_t[mine, at] = (context * (1.0 / total)).astype(bfloat)
                lse_ref[pl.ds(group * heads + head, 1), at] = top + jnp.log(total)

        over_blocks(causal, query_t.shape[1], length, body)
        return 0

    lax.fori_loop(0, HEADS // heads, group_of, 0)


def attend_back(
    limit, causal, query_ref, key_ref, value_ref, query_t, key_t, grad_ctx, grad_ctx_t, lse_ref, dot_ref,
    grad_key, grad_value, grad_query_t, key_two, value_two,
):
    length, width = key_ref.shape
    bias = key_bias(limit, length)

    def pair(number, unused):
        columns = block_of(number, 128)
        for head, tile in enumerate(pair_keys(key_ref[:, columns], bias, 4)):
            key_two[head] = tile
        for head, tile in enumerate(pair_keys(value_ref[:, columns], 1.0, 3)):
            value_two[head] = tile

        def body(first, queries, extent, diagonal):
            at = slice(first, first + queries)

            def products_of(head):
                row = pl.ds(number * 2 + head, 1)
                constants = [1.0] + split_three(-lse_ref[row, at])
                scores = mm(
                    key_two[head, :extent], pair_queries(query_t[columns, at], head, constants)
                )
                constants = split_three(-dot_ref[row, at])
                grad_weights = mm(
                    value_two[head, :extent], pair_queries(grad_ctx_t[columns, at], head, constants)
                )
                return scores, grad_weights

            lane = lax.broadcasted_iota(jnp.int32, (queries, 128), 1)

            def both(tile):
                tile = tile.astype(single)
                return jnp.concatenate(
                    [
                        jnp.where(lane < 64, tile, 0.0).astype(bfloat),
                        jnp.where(lane < 64, 0.0, tile).astype(bfloat),
                    ],
                    0,
                )

            all_weights, all_grads = [], []
            following = products_of(0)
            for head in range(2):
                scores, grad_weights = following
                if head == 0:
                    following = products_of(1)
                weights = [jnp.exp(more) for more in score_parts(scores, diagonal)]
                weights = jnp.concatenate(weights, 0)
                grads = (weights * grad_weights).astype(bfloat)
                all_weights.append(weights.astype(bfloat))
                all_grads.append(grads)
                mine = head_rows(number, 2, head)
                grad_query = mm(key_t[mine, :extent], grads)
                grad_query_t[mine, at] = (grad_query * 0.125).astype(bfloat)
            for out, parts, other in (
                (grad_value, all_weights, grad_ctx),
                (grad_key, all_grads, query_ref),
            ):
                total = mm(jnp.concatenate(parts, 1), both(other[at, columns]))
                if first:
                    total = jnp.concatenate([out[:first, columns] + total[:first], total[first:]], 0)
                out[:extent, columns] = total

        over_blocks(causal, query_t.shape[1], length, body)
        return 0

    lax.fori_loop(0, width // 128, pair, 0)


def by_rows(length, body, init=0):
    if length <= RB:
        return body(pl.ds(0, length), init)

    def step(index, carry):
        return body(block_of(index, RB), carry)

    return lax.fori_loop(0, length // RB, step, init)


class Emitter:
    def __init__(self, table, targets, stage, semaphores):
        self.table, self.targets, self.stage, self.semaphores = table, targets, stage, semaphores
        self.copies = []

    def chunk(self, number, first_piece, value):
        stage, half_rows = self.stage, self.targets[0].shape[1]
        stage[number] = value.astype(bfloat)
        count = stage.shape[1] // half_rows
        per_piece = 128 // half_rows
        for part in range(count):
            source = stage.at[number, pl.ds(part * half_rows, half_rows)]
            semaphore = self.semaphores.at[number * count + part]
            slot = self.table[first_piece * per_piece + part]

            def start(targets, first, source=source, semaphore=semaphore, slot=slot):
                def go():
                    pltpu.make_async_copy(source, targets[0].at[slot - first], semaphore).start()

                if len(targets) == 1:
                    go()
                    return
                last = first + targets[0].shape[0]
                pl.when(slot < last)(go)
                pl.when(slot >= last)(lambda: start(targets[1:], last))

            start(self.targets, 0)
            self.copies.append(pltpu.make_async_copy(source, self.targets[0].at[0], semaphore))

    def wait(self):
        for copy in self.copies:
            copy.wait()


class Moves:
    def __init__(self, role, spare):
        self.role = role
        self.spare = spare
        self.some = []
        self.loads = []
        self.stores = []
        self.begun = set()
        self.waited = set()

    def load(self, dest, ways, semaphores):
        def each(way, act):
            for number, (source, first, at, rows) in enumerate(way):
                target = dest
                if rows is not None:
                    source = source.at[pl.ds(first, rows)]
                    target = dest.at[pl.ds(at, rows)]
                act(pltpu.make_async_copy(source, target, semaphores.at[number]))

        def split(act):
            if len(ways) == 1:
                each(ways[0], act)
                return
            pl.when(self.role != 0)(lambda: each(ways[0], act))
            pl.when(self.role == 0)(lambda: each(ways[1], act))

        self.loads.append((dest, split))

    def begin(self, *refs):
        for number, (dest, split) in enumerate(self.loads):
            if number not in self.begun and any(dest is ref for ref in refs):
                self.begun.add(number)
                split(lambda copy: copy.start())

    def need(self, *refs):
        self.begin(*refs)
        for number, (dest, split) in enumerate(self.loads):
            if number not in self.waited and any(dest is ref for ref in refs):
                self.waited.add(number)
                split(lambda copy: copy.wait())

    def follow(self, *refs):
        self.begin(*refs)
        for dest, unused in self.loads:
            self.begin(dest)

    def rest(self):
        self.follow()
        self.need(*[dest for dest, unused in self.loads])

    def place(self, source, target, semaphores):
        self.stores.append((source, target, semaphores, []))

    def put(self, *refs):
        for source, target, semaphores, copies in self.stores:
            if not copies and any(source is ref for ref in refs):
                copies.append(pltpu.make_async_copy(source, target, semaphores.at[0]))
                copies[0].start()

    def put_rows(self, ref, first, rows):
        for source, target, semaphores, copies in self.stores:
            if source is ref:
                at = pl.ds(first, rows)
                copies.append(
                    pltpu.make_async_copy(source.at[at], target.at[at], semaphores.at[len(copies)])
                )
                copies[-1].start()

    def put_if(self, wanted, source, target):
        copy = pltpu.make_async_copy(source, target, self.spare.at[len(self.some)])
        pl.when(wanted)(copy.start)
        self.some.append((wanted, copy))

    def finish(self):
        self.rest()
        self.put(*[entry[0] for entry in self.stores])
        for entry in self.stores:
            for copy in entry[3]:
                copy.wait()
        for wanted, copy in self.some:
            pl.when(wanted)(copy.wait)


def part(value, first, rows):
    return ("load", [[(value, first, 0, rows)]])


def whole(value):
    return ("load", [[(value, 0, 0, None)]])


def either(source_way, target_way):
    return ("load", [source_way, target_way])


def call(body, name, scal, active, ins, outs, scratch, aliases=(), limit=58):
    args, specs, scratch_all, plan = [scal], [SM], [], []
    counts = {"load": 0, "store": 0}

    def arg(value, spec):
        args.append(value)
        specs.append(spec)
        return len(args) - 1

    held = []
    for kind, value in ins:
        if kind == "load":
            ways = [[(arg(v, HB), first, at, rows) for v, first, at, rows in way] for way in value]
            way = value[0] or value[1]
            v, first, at, rows = way[0]
            total = max(a + r for _, _, a, r in way) if rows is not None else None
            shape = v.shape if rows is None else (total,) + v.shape[1:]
            held.append(("load", ways, shape, v.dtype, max(len(w) for w in ways)))
        else:
            held.append((kind, arg(value, SM if kind == "smem" else HB)))
    vmem, sems = [], []
    for entry in held:
        if entry[0] == "load":
            vmem.append(pltpu.VMEM(entry[2], entry[3]))
            sems.append(pltpu.SemaphoreType.DMA((entry[4],)))
    for kind, shape in outs:
        if kind == "store":
            vmem.append(pltpu.VMEM(shape.shape, shape.dtype))
            sems.append(pltpu.SemaphoreType.DMA((6,)))
    count_in, count_out = len(args), len(outs)

    def kernel(*refs):
        inputs, outputs = refs[:count_in], refs[count_in : count_in + count_out]
        rest = refs[count_in + count_out :]
        buffers, semaphores = list(rest[: len(vmem)]), list(rest[len(vmem) : len(vmem) + len(sems)])
        spare, *extra = rest[len(vmem) + len(sems) :]
        scal_ref = inputs[0]

        def run():
            moves = Moves(scal_ref[2], spare)
            given = []
            for entry in held:
                if entry[0] == "load":
                    dest, semaphore = buffers.pop(0), semaphores.pop(0)
                    ways = [[(inputs[i], f, a, r) for i, f, a, r in way] for way in entry[1]]
                    moves.load(dest, ways, semaphore)
                    given.append(dest)
                else:
                    given.append(inputs[entry[1]])
            for (kind, unused), output in zip(outs, outputs):
                if kind == "store":
                    source, semaphore = buffers.pop(0), semaphores.pop(0)
                    moves.place(source, output, semaphore)
                    given.append(source)
                else:
                    given.append(output)
            body(moves, scal_ref, *given, *extra)
            moves.finish()

        if active is None:
            run()
        else:
            pl.when(scal_ref[2] == active)(run)

    pairs = {}
    for position, output in aliases:
        pairs[held[position][1]] = output
    return pl.pallas_call(
        kernel,
        in_specs=specs,
        out_specs=[HB] * count_out,
        out_shape=[shape for unused, shape in outs],
        scratch_shapes=vmem + sems + [pltpu.SemaphoreType.DMA((2,))] + list(scratch),
        input_output_aliases=pairs,
        compiler_params=pltpu.CompilerParams(vmem_limit_bytes=62 << 20),
        name=name,
    )(*args)


def halves_of(length):
    return [pl.ds(0, length // 2), pl.ds(length // 2, length // 2)]


def zero_rows(width):
    return (jnp.zeros((1, width), single),) * 3


def put_rows(ref, rows):
    for number, row in enumerate(rows):
        ref[number : number + 1] = row


def project_norm(io, length, ctx_t, weight, inner_ref, vec, resid_ref, out_ref):
    for rows in halves_of(length):
        branch = mm(ctx_t[:, rows].T, weight[...])
        resid = inner_ref[rows].astype(single) * vec[0:1] + branch
        resid_ref[rows] = resid
        out_ref[rows] = normed(resid)[0] * vec[1:2] + vec[2:3]
        for ref in (resid_ref, out_ref):
            io.put_rows(ref, rows.start, rows.size)


def self_forward(io, scal, x, weight, vec, outs, query_t, value_t, key_tiles, packed, ready):
    query, key, value, ctx_t, lse, resid, out, swap = outs
    length, width = x.shape
    some = length // 2
    io.begin(x)
    ready()
    io.need(x)
    io.follow()

    def body(rows, carry):
        tile = x[rows]
        for number, ref in enumerate((query, key, value)):
            ref[rows] = mm(tile, weight[width * number : width * (number + 1)]).astype(bfloat)
        query_t[:, rows] = (query[rows] * bfloat(0.125)).T
        value_t[:, rows] = value[rows].T
        return carry

    by_rows(length, body)
    io.put(query, key, value)
    attend(scal[0], scal[1], key, query_t, value_t, ctx_t, lse, key_tiles)
    io.put(ctx_t, lse)
    io.rest()
    project_norm(io, length, ctx_t, weight.at[3 * width :], x, vec, resid, out)

    pl.when(scal[2] == 0)(lambda: pack_rows(packed, 0, out[some:]))
    io.put_if(scal[2] == 0, packed, swap.at[pl.ds(0, 3 * some)])


def self_forward_body(io, scal, x, weight, vec, *refs):
    io.begin(x)
    self_forward(io, scal, x, weight, vec, refs[:8], *refs[8:], lambda: io.need(weight))


def placed_forward_body(where, io, scal, table, x, vec, *refs):
    sources, refs = refs[: len(where)], refs[len(where) :]
    outs, (weight, rest) = refs[:8], refs[8:10]
    query_t, value_t, key_tiles, packed, semaphores = refs[10:]
    size = sources[0].shape[1]
    cut = weight.shape[0] // size
    io.begin(x)

    for source, ranges in zip(sources, where):
        for start, stop, distance, other, first in ranges:

            def step(slot, unused):
                piece = table[distance, first + slot - start]
                at = piece * 2 + (scal[5] if other == 0 else 1 - scal[5])

                def move(target, place, semaphore):
                    place = pl.ds(pl.multiple_of(place * size, size), size)
                    pltpu.make_async_copy(source.at[slot], target.at[place], semaphore).start()

                pl.when((piece >= 0) & (at < cut))(lambda: move(weight, at, semaphores.at[0]))
                pl.when(at >= cut)(lambda: move(rest, at - cut, semaphores.at[1]))
                return 0

            lax.fori_loop(start, stop, step, 0)

    def ready():
        pltpu.make_async_copy(weight, weight, semaphores.at[0]).wait()
        io.put(weight)

    self_forward(io, scal, x, weight, vec, outs, query_t, value_t, key_tiles, packed, ready)
    pltpu.make_async_copy(rest, rest, semaphores.at[1]).wait()
    io.put(rest)


def encoder_ff_body(
    io, scal, inner, up, down, cross, vec, held, activ, slope, resid, memory, swap, sendout
):
    length, width = inner.shape
    io.need(inner, up)
    io.follow(down)
    for rows in [pl.ds(0, length)]:
        act, grad = gelu_parts(mm_nt(inner[rows].astype(bfloat), up[...]))
        activ[rows] = act.astype(bfloat)
        slope[rows] = grad.astype(bfloat)
        for ref in (activ, slope):
            io.put_rows(ref, rows.start, rows.size)
    io.rest()
    for rows in [pl.ds(0, length)]:
        total = inner[rows] * vec[0:1] + mm(activ[rows], down[...])
        resid[rows] = total
        mem = (normed(total)[0] * vec[1:2] + vec[2:3]).astype(bfloat)
        memory[rows] = mem
        sendout[rows] = mm(mem, cross[:width]).astype(bfloat)
        sendout[pl.ds(length + rows.start, rows.size)] = mm(mem, cross[width:]).astype(bfloat)
        for ref in (resid, memory):
            io.put_rows(ref, rows.start, rows.size)
    io.put_if(scal[2] != 0, sendout, swap)


def ff_back(length, emit, grad_branch, activ, slope, inner_low, up, down, grad_inner):
    def body(rows, carry):
        grad = mm_nt(grad_branch[rows], down[...]) * slope[rows].astype(single)
        grad = grad.astype(bfloat)
        slope[rows] = grad
        grad_inner[rows] += mm(grad, up[...])
        return carry

    by_rows(length, body)
    for number in range(activ.shape[1] // 512):
        columns = slice(number * 512, (number + 1) * 512)
        emit(0, number, mm_tn(slope[:, columns], inner_low[...]))
        emit(1, number, mm_tn(activ[:, columns], grad_branch[...]))


def branch_back(length, resid, grad_out, inner, vec, grad_branch, grad_inner, grad_vec):
    width = resid.shape[1]

    def body(rows, carry):
        grad_resid, grad_gain, grad_shift = norm_back(resid[rows], grad_out[rows], vec[1:2])
        grad_branch[rows] = grad_resid.astype(bfloat)
        grad_inner[rows] = grad_resid * vec[0:1]
        weigh = jnp.sum(grad_resid * inner[rows].astype(single), 0, keepdims=True)
        return (carry[0] + weigh, carry[1] + grad_gain, carry[2] + grad_shift)

    put_rows(grad_vec, by_rows(length, body, zero_rows(width)))


def ctx_back(length, grad_branch, weight, ctx_t, grad_ctx, grad_ctx_t, dot_ref):
    def body(rows, carry):
        grad_ctx[rows] = mm_nt(grad_branch[rows], weight[...]).astype(bfloat)
        grad_ctx_t[:, rows] = grad_ctx[rows].T
        for head in range(HEADS):
            mine = slice(64 * head, 64 * head + 64)
            product = grad_ctx_t[mine, rows].astype(single) * ctx_t[mine, rows].astype(single)
            dot_ref[head : head + 1, rows] = jnp.sum(product, 0, keepdims=True)
        return carry

    by_rows(length, body)


def middle_body(
    io, scal, inner, packed, keys, cross, cross_vec, up, down, ff_vec, cotan,
    output, sendback, grad_inner, grads, grad_vec, swap,
    query, query_t, ctx_t, lse, resid, after, activ, slope, low_rows, grad_branch, grad_after,
    grad_ctx, grad_ctx_t, dot_ref, key_t, value_t, grad_key, grad_value, grad_query_t,
    key_tiles, key_two, value_two, swap_out,
):
    rows_here, width = inner.shape
    hidden, length = up.shape[0], keys.shape[0] // 2
    key_rows, value_rows = keys.at[:length], keys.at[length:]
    io.need(inner, packed, cross, keys)
    io.follow(cross_vec, up, down)

    @pl.when(scal[2] != 0)
    def _():
        inner[...] = unpack_rows(packed, rows_here)

    def project(rows, carry):
        query[rows] = mm(inner[rows].astype(bfloat), cross[:width]).astype(bfloat)
        query_t[:, rows] = (query[rows] * bfloat(0.125)).T
        return carry

    def turn(rows, carry):
        key_t[:, rows] = key_rows[rows].T
        value_t[:, rows] = value_rows[rows].T
        return carry

    by_rows(rows_here, project)
    by_rows(length, turn)
    attend(scal[4], None, key_rows, query_t, value_t, ctx_t, lse, key_tiles)
    io.rest()
    project_norm(io, rows_here, ctx_t, cross.at[width:], inner, cross_vec, resid, after)

    def feed(rows, carry):
        tile = after[rows]
        low_tile = tile.astype(bfloat)
        low_rows[rows] = low_tile
        act, grad = gelu_parts(mm_nt(low_tile, up[...]))
        act = act.astype(bfloat)
        activ[rows] = act
        slope[rows] = grad.astype(bfloat)
        total = tile * ff_vec[0:1] + mm(act, down[...])
        output[rows] = (normed(total)[0] * ff_vec[1:2] + ff_vec[2:3]).astype(bfloat)
        row = lax.broadcasted_iota(jnp.int32, tile.shape, 0) + rows.start
        grad_out = jnp.where(row < scal[3], cotan[rows].astype(single), 0.0)
        grad_resid, grad_gain, grad_shift = norm_back(total, grad_out, ff_vec[1:2])
        grad_branch[rows] = grad_resid.astype(bfloat)
        grad_after[rows] = grad_resid * ff_vec[0:1]
        weigh = jnp.sum(grad_resid * tile, 0, keepdims=True)
        return (carry[0] + weigh, carry[1] + grad_gain, carry[2] + grad_shift)

    put_rows(grad_vec.at[3:], by_rows(rows_here, feed, zero_rows(width)))
    io.put(output)

    def emit(which, number, value):
        first = 2 * width + which * hidden + number * 512
        grads[first : first + 512] = value.astype(bfloat)
        if which == 1 and number in (1, 3):
            for start in (2 * width, 2 * width + hidden):
                io.put_rows(grads, start + (number - 1) * 512, 1024)

    ff_back(rows_here, emit, grad_branch, activ, slope, low_rows, up, down, grad_after)
    branch_back(rows_here, resid, grad_after, inner, cross_vec, grad_branch, grad_inner, grad_vec)
    io.put(grad_vec)
    grads[width : 2 * width] = mm(ctx_t[...], grad_branch[...]).astype(bfloat)
    ctx_back(rows_here, grad_branch, cross.at[width:], ctx_t, grad_ctx, grad_ctx_t, dot_ref)
    attend_back(
        scal[4], None, query, key_rows, value_rows, query_t, key_t, grad_ctx, grad_ctx_t, lse, dot_ref,
        grad_key, grad_value, grad_query_t, key_two, value_two,
    )

    def send(rows, carry):
        sendback[rows] = (grad_key[rows] * 0.125).astype(bfloat)
        sendback[pl.ds(length + rows.start, rows.size)] = grad_value[rows].astype(bfloat)
        return carry

    by_rows(length, send)
    io.put(sendback)
    io.put_if(scal[2] == 0, sendback, swap)

    def last(rows, carry):
        grad_query = grad_query_t[:, rows].T
        grad_inner[rows] += mm_nt(grad_query, cross[:width])
        grad_ctx[rows] = grad_query
        return carry

    by_rows(rows_here, last)
    io.put(grad_inner)

    @pl.when(scal[2] != 0)
    def _():
        pack_rows(swap_out, 0, grad_inner[...])
        swap_out[3 * rows_here :] = output[...]

    io.put_if(scal[2] != 0, swap_out, swap)

    grads[:width] = mm_tn(inner[...].astype(bfloat), grad_ctx[...]).astype(bfloat)
    io.put_rows(grads, 0, 2 * width)


def encoder_back_body(
    io, scal, table, own, received, memory, cross, inner, resid, activ, slope, up, down, vec,
    grad_inner, grad_vec, *rest_of,
):
    length, width = inner.shape
    *targets, grad_mem, inner_low, grad_branch, stage, semaphores = rest_of
    emit = Emitter(table, targets, stage, semaphores)
    io.begin(own, received, cross, inner)
    io.follow(memory, vec, resid, down, slope, up, activ)
    io.need(own, received, cross, inner)

    def body(rows, carry):
        own[...] = added(own[...], received[...])
        grad_mem[rows] = mm_nt(own[:length], cross[:width]) + mm_nt(own[length:], cross[width:])
        inner_low[rows] = inner[rows].astype(bfloat)
        return carry

    by_rows(length, body)
    io.need(vec, resid, memory)
    emit.chunk(8, 16, mm_tn(memory[...], own[:length]))
    emit.chunk(9, 20, mm_tn(memory[...], own[length:]))
    branch_back(length, resid, grad_mem, inner, vec, grad_branch, grad_inner, grad_vec)
    io.put(grad_vec)
    io.rest()

    def each(which, number, value):
        emit.chunk(2 * number + which, 24 + 16 * which + 4 * number, value)

    ff_back(length, each, grad_branch, activ, slope, inner_low, up, down, grad_inner)
    io.put(grad_inner)
    emit.wait()


def self_back_body(
    io, scal, table, x, weight, out_weight, vec, resid, query, key, value, ctx_t, lse, grad_out, packed, *refs
):
    length, width = x.shape
    count = (len(refs) - 15) // 2
    grad_x, grad_vec, *targets = refs[count : 2 * count + 2]
    (
        grad_branch, grad_ctx, grad_ctx_t, dot_ref, query_t, key_t, grad_key, grad_value, grad_query_t,
        key_two, value_two, stage, semaphores,
    ) = refs[2 * count + 2 :]
    emit = Emitter(table, targets, stage, semaphores)
    some = length // 2
    io.need(resid, grad_out, packed, x, vec)
    io.follow(ctx_t, out_weight, query, key, value)

    @pl.when(scal[2] == 0)
    def _():
        grad_out[some:] = unpack_rows(packed, some)

    branch_back(length, resid, grad_out, x, vec, grad_branch, grad_x, grad_vec)
    io.put(grad_vec)
    io.need(ctx_t, out_weight)
    emit.chunk(3, 12, mm(ctx_t[...], grad_branch[...]))
    ctx_back(length, grad_branch, out_weight, ctx_t, grad_ctx, grad_ctx_t, dot_ref)
    io.rest()

    def body(rows, carry):
        query_t[:, rows] = (query[rows] * bfloat(0.125)).T
        key_t[:, rows] = key[rows].T
        return carry

    by_rows(length, body)
    attend_back(
        scal[0], scal[1], query, key, value, query_t, key_t, grad_ctx, grad_ctx_t, lse, dot_ref,
        grad_key, grad_value, grad_query_t, key_two, value_two,
    )

    def last(rows, carry):
        parts = (
            grad_query_t[:, rows].T,
            (grad_key[rows] * 0.125).astype(bfloat),
            grad_value[rows].astype(bfloat),
        )
        total = grad_x[rows]
        for number, low_grad in enumerate(parts):
            total += mm_nt(low_grad, weight[width * number : width * (number + 1)])
        grad_x[rows] = total
        grad_branch[rows], grad_ctx[rows], value[rows] = parts
        return carry

    by_rows(length, last)
    io.put(grad_x)
    for number, ref in enumerate((grad_branch, grad_ctx, value)):
        emit.chunk(number, 4 * number, mm_tn(x[...], ref[...]))
    emit.wait()


def merge_body(io, scal, table, own, other, *refs):
    count = (len(refs) - 2) // 2
    *targets, stage, semaphores = refs[count:]
    emit = Emitter(table, targets, stage, semaphores)
    io.rest()
    chunk = stage.shape[1]
    for number in range(own.shape[0] // chunk):
        rows = slice(number * chunk, (number + 1) * chunk)
        total = own[rows].astype(single) + other[rows].astype(single)
        emit.chunk(number, 16 + 4 * number, total)
    emit.wait()


RING = (0, 2, 4, 6, 7, 5, 3, 1)
LEAD = 6
LEVEL = 10
FLOW = 8


def lend_kernel(scal, owners, master, own_out, up_out, down_out, plan, counts, low_rows, loaded, sems):
    size = len(RING)
    load = pltpu.make_async_copy(master, loaded, sems.at[0])
    load.start()
    for place in range(size):
        counts[place] = 0

    def count(piece, unused):
        owner = owners[piece]
        place = jnp.where(owner % 2 == 0, owner // 2, size - 1 - owner // 2)
        counts[place] = counts[place] + 1
        return 0

    lax.fori_loop(0, owners.shape[0], count, 0)
    held = [counts[place] for place in range(size)]
    caps = [jnp.int32(FLOW)] * size
    for place in list(range(size - 1, -1, -1)) * 2:
        after = (place + 1) % size
        caps[place] = jnp.minimum(FLOW, caps[after] - held[after] + LEVEL)
    flows = [jnp.minimum(0, cap) for cap in caps]
    for place in list(range(size)) * 2:
        flows[place] = jnp.maximum(flows[place], flows[place - 1] + held[place] - LEVEL)
    for place in range(size):
        ahead = jnp.maximum(flows[place], 0)
        back = jnp.maximum(-flows[place - 1], 0)
        plan[0, place] = held[place] - ahead - back
        plan[1, place] = ahead
        plan[2, place] = back
    load.wait()
    rows = loaded.shape[0]
    low_rows[:rows] = loaded[...].astype(bfloat)
    kept = plan[0, scal[0]]
    copies = [
        pltpu.make_async_copy(low_rows.at[pl.ds(0, rows)], own_out, sems.at[0]),
        pltpu.make_async_copy(low_rows.at[pl.ds(kept, FLOW)], up_out, sems.at[1]),
        pltpu.make_async_copy(
            low_rows.at[pl.ds(kept + plan[1, scal[0]], FLOW)], down_out, sems.at[2]
        ),
    ]
    for copy in copies:
        copy.start()
    for copy in copies:
        copy.wait()


def borrow_kernel(scal, plan, own, below, above, lead_out, late_out, slots, sems, out_sems):
    size = len(RING)
    kept = plan[0, scal[0]]
    from_below = kept + plan[1, (scal[0] + size - 1) % size]
    from_above = from_below + plan[2, (scal[0] + 1) % size]
    for slot in range(LEVEL):

        def move(source, slot=slot):
            pltpu.make_async_copy(source, slots.at[slot], sems.at[slot]).start()

        pl.when(slot < kept)(lambda slot=slot, move=move: move(own.at[slot]))
        pl.when((slot >= kept) & (slot < from_below))(
            lambda slot=slot, move=move: move(below.at[slot - kept])
        )
        pl.when((slot >= from_below) & (slot < from_above))(
            lambda slot=slot, move=move: move(above.at[slot - from_below])
        )
    for slot in range(LEVEL):
        pl.when(slot < from_above)(pltpu.make_async_copy(own.at[0], slots.at[slot], sems.at[slot]).wait)
    copies = [
        pltpu.make_async_copy(slots.at[pl.ds(0, LEAD)], lead_out, out_sems.at[0]),
        pltpu.make_async_copy(slots.at[pl.ds(LEAD, LEVEL - LEAD)], late_out, out_sems.at[1]),
    ]
    for copy in copies:
        copy.start()
    for copy in copies:
        copy.wait()


def lend(position, owner_row, master):
    slot = master.shape[1:]
    rows = master.shape[0]
    where = position[None].astype(jnp.int32)
    own, up, down, plan = pl.pallas_call(
        lend_kernel,
        in_specs=[SM, SM, HB],
        out_specs=[HB, HB, HB, SM],
        out_shape=[
            low(rows, *slot),
            low(FLOW, *slot),
            low(FLOW, *slot),
            jax.ShapeDtypeStruct((3, len(RING)), jnp.int32),
        ],
        scratch_shapes=[
            pltpu.SMEM((len(RING),), jnp.int32),
            low_vm(rows + FLOW, *slot),
            full_vm(rows, *slot),
            pltpu.SemaphoreType.DMA((3,)),
        ],
        name="lend",
    )(where, owner_row, master)
    below, above = round_ring(up, 1), round_ring(down, -1)
    lead, late = pl.pallas_call(
        borrow_kernel,
        in_specs=[SM, SM, HB, HB, HB],
        out_specs=[HB, HB],
        out_shape=[low(LEAD, *slot), low(LEVEL - LEAD, *slot)],
        scratch_shapes=[
            low_vm(LEVEL, *slot),
            pltpu.SemaphoreType.DMA((LEVEL,)),
            pltpu.SemaphoreType.DMA((2,)),
        ],
        name="borrow",
    )(where, plan, own, below, above)
    return lead, late, plan


def adam_kept_body(
    io, scal, plan, sums, master, first, second, new_first, new_second, new_master, new_copy
):
    io.rest()
    count, place = master.shape[0], scal[6]
    kept = plan[0, place]
    held = kept + plan[1, place] + plan[2, place]

    def update(slot, gradient):
        weight, one, two = adam(
            master[slot], gradient, first[slot], second[slot], rate_matrix, decay_matrix
        )
        new_first[slot], new_second[slot], new_master[slot] = one, two, weight
        new_copy[slot] = weight.astype(bfloat)

    def step(slot, unused):
        pl.when(slot < kept)(lambda: update(slot, sums[slot]))
        pl.when(slot >= held)(lambda: update(slot, jnp.zeros(master.shape[1:], single)))
        return 0

    for start in range(0, count, count // 2):
        lax.fori_loop(start, start + count // 2, step, 0)
        for ref in (new_first, new_second, new_master, new_copy):
            io.put_rows(ref, start, count // 2)


def adam_lent_body(
    io, scal, plan, below, above, master, first, second, one_held, two_held, weight_held, copy_held,
    new_first, new_second, new_master, new_copy,
    states, gradients, results, low_result, in_sems, out_sems,
):
    count, place = master.shape[0], scal[6]
    kept = plan[0, place]
    from_above = kept + plan[1, place]
    held = from_above + plan[2, place]

    def each(act):
        def step(slot, unused):
            pl.when((slot >= kept) & (slot < held))(lambda: act(slot))
            return 0

        lax.fori_loop(0, count, step, 0)

    def copies_in(slot):
        sources = [ref.at[slot] for ref in (master, first, second)]
        return [
            pltpu.make_async_copy(source, states.at[number, slot], in_sems.at[number, slot])
            for number, source in enumerate(sources)
        ]

    def copies_out(slot):
        outs = [
            pltpu.make_async_copy(results.at[number, slot], ref.at[slot], out_sems.at[number, slot])
            for number, ref in enumerate((new_first, new_second, new_master))
        ]
        return outs + [
            pltpu.make_async_copy(low_result.at[slot], new_copy.at[slot], out_sems.at[3, slot])
        ]

    def begin(slot):
        for copy in copies_in(slot):
            copy.start()

        def fetch(source):
            pltpu.make_async_copy(source, gradients.at[slot], in_sems.at[3, slot]).start()

        pl.when(slot < from_above)(lambda: fetch(above.at[slot - kept]))
        pl.when(slot >= from_above)(lambda: fetch(below.at[slot - from_above]))

    def update(slot):
        for copy in copies_in(slot):
            copy.wait()
        pltpu.make_async_copy(below.at[0], gradients.at[slot], in_sems.at[3, slot]).wait()
        weight, one, two = adam(
            states[0, slot],
            gradients[slot].astype(single),
            states[1, slot],
            states[2, slot],
            rate_matrix,
            decay_matrix,
        )
        results[0, slot], results[1, slot], results[2, slot] = one, two, weight
        low_result[slot] = weight.astype(bfloat)
        for copy in copies_out(slot):
            copy.start()

    def end(slot):
        for copy in copies_out(slot):
            copy.wait()

    each(begin)
    each(update)
    each(end)


def round_ring(value, step):
    count = len(RING)
    return lax.ppermute(value, "wide", [(RING[i], RING[(i + step) % count]) for i in range(count)])


def swapped(value):
    return lax.ppermute(value, "narrow", [(0, 1), (1, 0)])


def step_of(up, down, across):
    return lax.optimization_barrier((round_ring(up, 1), round_ring(down, -1), swapped(across)))


def partner(value, axis, bit):
    return lax.ppermute(value, axis, [(i, i ^ bit) for i in range(lax.axis_size(axis))])


def join(*values):
    return jnp.concatenate(values, 0)


def ring_gather(own_lead, own_late, plan, make_tables):
    lead, late, half = LEAD, LEVEL - LEAD, LEAD // 2
    found = [([(0, lead, 0, 0, 0)], own_lead), ([(0, late, 0, 0, lead)], own_late)]

    def ahead(value, far, near):
        ranges = [(0, lead, far, 0, 0)]
        if near is not None:
            ranges += [(lead, lead + late, near, 0, lead), (lead + late, lead + 2 * late, near, 1, lead)]
        found.append((ranges, value))

    up, down, across = step_of(own_lead, own_lead, own_late)
    up, plan = lax.optimization_barrier((up, plan))
    tables = make_tables(plan)
    found.append(([(0, late, 0, 1, lead)], across))
    ahead(up, 7, None)
    ahead(down, 1, None)
    pair = join(own_late, across)
    up, down, across = step_of(join(up, pair), join(down, pair), join(up, down, own_lead[:half]))
    found.append(
        ([(0, lead, 7, 1, 0), (lead, 2 * lead, 1, 1, 0), (2 * lead, 2 * lead + half, 0, 1, 0)], across)
    )
    up, tables = lax.optimization_barrier((up, tables))
    ahead(up, 6, 7)
    ahead(down, 2, 1)
    up, down, across = step_of(up, down, join(up[:lead], down[:lead], own_lead[half:]))
    found.append(
        ([(0, lead, 6, 1, 0), (lead, 2 * lead, 2, 1, 0), (2 * lead, 2 * lead + half, 0, 1, half)], across)
    )
    ahead(up, 5, 6)
    ahead(down, 3, 2)
    up, down, across = step_of(join(up[:half], up[lead:]), down[half:], join(up[:lead], down[:lead]))
    found.append(([(0, lead, 5, 1, 0), (lead, 2 * lead, 3, 1, 0)], across))
    for value, first, near in ((up, 0, 5), (down, half, 3)):
        ranges = [(0, half, 4, 0, first), (half, half + late, near, 0, lead)]
        found.append((ranges + [(half + late, half + 2 * late, near, 1, lead)], value))
    up, down, across = step_of(
        up[half : half + late], down[half + late :], join(up[:half], down[:half])
    )
    found.append(([(0, late, 4, 0, lead)], up))
    found.append(([(0, late, 4, 1, lead)], down))
    found.append(([(0, lead, 4, 1, 0)], across))
    return found, tables


def added(*values):
    return sum(value.astype(single) for value in values).astype(bfloat)


def ring_scatter(grads, far, vector):
    partners = [("narrow", 1), ("wide", 1), ("wide", 2), ("wide", 4), ("half", 1)]

    def step_of(*values):
        nonlocal vector
        ring = (round_ring(values[0], 1), round_ring(values[1], -1), swapped(values[2]))
        *ring, other = lax.optimization_barrier((*ring, partner(vector, *partners.pop(0))))
        vector = vector + other
        return ring

    lead, half = LEAD, LEAD // 2
    late = grads.shape[2] - lead

    def both(distance):
        return grads[distance, :, lead:].reshape((-1,) + grads.shape[3:])

    def mine(distance, start=0, stop=lead):
        return grads[distance, 0, start:stop]

    def other(distance, start=0, stop=lead):
        return grads[distance, 1, start:stop]

    across, down, up = far
    up, down, across = step_of(up, down, across)
    first = added(mine(4), across)
    up = join(first[:half], added(up, grads[3, 0, lead:]), grads[3, 1, lead:])
    down = join(first[half:], grads[5, 0, lead:], added(down, grads[5, 1, lead:]))
    up, down, across = step_of(up, down, join(other(3), other(5)))
    up = join(
        added(mine(3, 0, half), across[:half], up[:half]),
        added(mine(3, half), across[half:lead]),
        added(up[half:], both(2)),
    )
    down = join(
        added(mine(5, 0, half), across[lead : lead + half]),
        added(mine(5, half), across[lead + half :], down[:half]),
        added(down[half:], both(6)),
    )
    up, down, across = step_of(up, down, join(other(2), other(6), other(0, 0, half)))
    nearest = [across[2 * lead :]]
    up = join(added(mine(2), across[:lead], up[:lead]), added(up[lead:], both(1)))
    down = join(added(mine(6), across[lead : 2 * lead], down[:lead]), added(down[lead:], both(7)))
    up, down, across = step_of(up, down, join(other(1), other(7), other(0, half)))
    nearest.append(across[2 * lead :])
    total = sum(value.astype(single) for value in (both(0), up[lead:], down[lead:]))
    up, down, across = step_of(
        added(mine(1), across[:lead], up[:lead]),
        added(mine(7), across[lead : 2 * lead], down[:lead]),
        total[late:].astype(bfloat),
    )
    first = sum(value.astype(single) for value in (mine(0), join(*nearest), up, down))
    return join(first, total[:late] + across.astype(single)), vector


def shaped(*shape, dtype=single):
    return jax.ShapeDtypeStruct(shape, dtype)


def low(*shape):
    return jax.ShapeDtypeStruct(shape, bfloat)


def low_vm(*shape):
    return pltpu.VMEM(shape, bfloat)


def full_vm(*shape):
    return pltpu.VMEM(shape, single)


def sum_over(value, axis):
    size = lax.axis_size(axis)
    bit = 1
    while bit < size:
        value = value + partner(value, axis, bit)
        bit *= 2
    return value


def adam(weight, gradient, first, second, step_rate, decay_rate):
    first_new = beta_one * first + (1.0 - beta_one) * gradient
    second_new = beta_two * second + (1.0 - beta_two) * gradient * gradient
    first_hat = first_new / (1.0 - beta_one**STEP)
    second_hat = second_new / (1.0 - beta_two**STEP)
    weight_new = weight - step_rate * (
        first_hat / (jnp.sqrt(second_hat) + eps_adam) + decay_rate * weight
    )
    return (weight_new, first_new, second_new)


def on_device(
    stream, cotangent, lengths, owners, master, moment_one, moment_two, vec_master, vec_one, vec_two
):
    narrow_size = lax.axis_size("narrow")
    wide_size = lax.axis_size("wide")
    owner_row = owners[0]
    capacity = master.shape[1]
    half_rows = master.shape[2]
    width = master.shape[3]
    count = owner_row.shape[0]
    counter = jnp.arange(count)
    same = owner_row[:, None] == owner_row[None, :]
    earlier = counter[None, :] < counter[:, None]
    ranks = jnp.sum((same & earlier).astype(jnp.int32), 1)
    on_ring = (wide_size, narrow_size, capacity, count) == (len(RING), 2, 14, 56)
    wide_at, narrow_at = lax.axis_index("wide"), lax.axis_index("narrow")
    self_rows, rest_rows = 4 * width, count * half_rows * narrow_size - 4 * width
    is_source = lax.axis_index("half") == 0
    x = stream[0, 0]
    length = x.shape[0]
    some = length // 2
    source_len, target_len = lengths[0, 0], lengths[1, 0]
    flag = is_source.astype(jnp.int32)
    position = jnp.where(wide_at % 2 == 0, wide_at // 2, wide_size - 1 - wide_at // 2)
    scal = jnp.stack(
        [
            jnp.where(is_source, source_len, target_len),
            1 - flag,
            flag,
            jnp.where(is_source, target_len - some, target_len),
            source_len,
            narrow_at,
            position,
        ]
    ).astype(jnp.int32)
    if on_ring:
        capacity = LEVEL
        own_lead, own_late, plan = lend(position, owner_row.astype(jnp.int32), master[0])

        def make_tables(plan):
            def pick(row, index):
                hit = index[:, None] == jnp.arange(wide_size)[None, :]
                return jnp.sum(jnp.where(hit, row[None, :], 0), 1)

            place = jnp.where(owner_row % 2 == 0, owner_row // 2, wide_size - 1 - owner_row // 2)
            kept, ahead = pick(plan[0], place), pick(plan[1], place)
            moved = (ranks >= kept).astype(jnp.int32) - 2 * (ranks >= kept + ahead).astype(jnp.int32)
            place = (place + moved) % wide_size
            base = pick(plan[0], place)
            below = pick(plan[1], (place - 1) % wide_size)
            slots_there = jnp.where(
                moved == 0,
                ranks,
                jnp.where(moved > 0, base + ranks - kept, base + below + ranks - kept - ahead),
            )
            distance = (place - position) % wide_size
            halves = jnp.arange(narrow_size)[None, :] ^ narrow_at
            table = (distance[:, None] * 2 + halves) * capacity + slots_there[:, None]
            total, late = wide_size * 2 * capacity, capacity - LEAD
            is_late = (slots_there >= LEAD)[:, None]
            after_late = slots_there[:, None] - LEAD + total + LEAD
            far = jnp.where(
                halves == 1,
                jnp.where(is_late, after_late, slots_there[:, None] + total),
                jnp.where(is_late, after_late + late, table),
            )
            table = jnp.where(distance[:, None] == 4, far, table).reshape(-1)
            slot_of = distance * capacity + slots_there
            hit = slot_of[None, :] == jnp.arange(wide_size * capacity)[:, None]
            pieces = jnp.sum(hit.astype(jnp.int32) * (counter + 1)[None, :], 1) - 1
            pieces = pieces.reshape(wide_size, capacity).astype(jnp.int32)
            return pieces, table.astype(jnp.int32), scal

        found, (pieces, table, scal) = ring_gather(own_lead, own_late, plan, make_tables)
    else:
        places = (
            owner_row[:, None] * narrow_size + jnp.arange(narrow_size)[None, :]
        ) * capacity + ranks[:, None]
        table = places.reshape(-1)
        own = master[0].astype(bfloat)
        gathered = lax.all_gather(own, ("wide", "narrow"), axis=0, tiled=True)
        weight = jnp.take(gathered, table, axis=0).reshape(-1, width)
        weight, rest = weight[:self_rows], weight[self_rows:]
    table = table.astype(jnp.int32)
    hidden = (rest_rows - 2 * width) // 2
    self_vec = whole(jnp.where(is_source, vec_master[0:3], vec_master[6:9]))
    cross_vec, ff_vec = whole(vec_master[9:12]), whole(vec_master[12:15])
    memory_vec = whole(vec_master[3:6])
    total = capacity * wide_size * narrow_size
    cuts = [total, LEAD, capacity - LEAD, capacity - LEAD] if on_ring else [total]
    slots = [low(size, half_rows, width) for size in cuts]
    slot_outs = [("hbm", one) for one in slots]

    def stage_of(chunks):
        return [
            low_vm(chunks, 512, width),
            pltpu.SemaphoreType.DMA((chunks * 512 // half_rows,)),
        ]

    def store(*shape, dtype=single):
        return ("store", shaped(*shape, dtype=dtype))

    low_out = partial(store, dtype=bfloat)
    two, four = low_vm(2, length, 128), low_vm(4, length, 128)
    both_halves = [(0, 1), (1, 0)]

    forward_outs = (
        [low_out(length, width)] * 3
        + [low_out(width, length), store(HEADS, length)]
        + [store(length, width)] * 2
        + [("hbm", low(2 * length, width))]
    )
    forward_scratch = [low_vm(width, length), low_vm(width, length), four, low_vm(3 * some, width)]
    if on_ring:
        *forward, weight, rest = call(
            partial(placed_forward_body, [where for where, unused in found]),
            "self_forward",
            scal,
            None,
            [("smem", pieces), whole(x), self_vec] + [("hbm", value) for unused, value in found],
            forward_outs + [low_out(self_rows, width), low_out(rest_rows, width)],
            forward_scratch + [pltpu.SemaphoreType.DMA((2,))],
        )
    else:
        forward = call(
            self_forward_body,
            "self_forward",
            scal,
            None,
            [whole(x), whole(weight), self_vec],
            forward_outs,
            forward_scratch,
        )
    query, key, value, ctx_t, lse, resid, inner, swap = forward
    rest_other = lax.ppermute(rest, "half", both_halves)
    cross_w = part(rest, 0, 2 * width)
    up_w = part(rest, 2 * width, hidden)
    down_w = part(rest, 2 * width + hidden, hidden)
    activ, slope, ff_resid, memory, swap = call(
        encoder_ff_body,
        "encoder_ff",
        scal,
        1,
        [whole(inner), up_w, down_w, cross_w, memory_vec, ("hbm", swap)],
        [low_out(length, hidden)] * 2
        + [store(length, width), low_out(length, width), ("hbm", low(2 * length, width))],
        [low_vm(2 * length, width)],
        [(5, 4)],
    )
    swap_other = lax.ppermute(swap, "half", both_halves)

    def shared(first, rows):
        return either([(rest_other, first, 0, rows)], [(rest, first, 0, rows)])

    mid_inner = either([], [(inner, 0, 0, some)])
    mid_packed = either([(swap_other, 0, 0, 3 * some)], [])
    keys = either([(swap, 0, 0, None)], [(swap_other, 0, 0, None)])
    cotan = cotangent[0]
    output, sendback, grad_one, grad_rest, grad_middle_vec, swap = call(
        middle_body,
        "decoder_middle",
        scal,
        None,
        [
            mid_inner,
            mid_packed,
            keys,
            shared(0, 2 * width),
            cross_vec,
            shared(2 * width, hidden),
            shared(2 * width + hidden, hidden),
            ff_vec,
            either([(cotan, some, 0, some)], [(cotan, 0, 0, some)]),
        ],
        [
            low_out(some, width),
            low_out(2 * length, width),
            store(some, width),
            low_out(rest_rows, width),
            store(6, width),
            ("hbm", low(2 * length, width)),
        ],
        [low_vm(some, width), low_vm(width, some), low_vm(width, some), full_vm(HEADS, some)]
        + [full_vm(some, width), full_vm(some, width), low_vm(some, hidden), low_vm(some, hidden)]
        + [low_vm(some, width), low_vm(some, width), full_vm(some, width)]
        + [low_vm(some, width), low_vm(width, some), full_vm(HEADS, some)]
        + [low_vm(width, length), low_vm(width, length)]
        + [full_vm(length, width), full_vm(length, width), low_vm(width, some), four, two, two]
        + [low_vm(2 * length, width)],
    )
    swap_other = lax.ppermute(swap, "half", both_halves)
    grad_rest, swap_other = lax.optimization_barrier((grad_rest, swap_other))
    grad_rest_other = lax.ppermute(grad_rest, "half", both_halves)
    output = join(output, swap_other[3 * some :])
    grad_inner, grad_memory_vec, *target = call(
        encoder_back_body,
        "encoder_back",
        scal,
        1,
        [
            ("smem", table),
            whole(sendback),
            whole(swap_other),
            whole(memory),
            cross_w,
            whole(inner),
            whole(ff_resid),
            whole(activ),
            whole(slope),
            up_w,
            down_w,
            memory_vec,
        ],
        [store(length, width), store(3, width)] + slot_outs,
        [full_vm(length, width), low_vm(length, width), low_vm(length, width)] + stage_of(10),
    )
    back_scratch = (
        [low_vm(length, width), low_vm(length, width), low_vm(width, length), full_vm(HEADS, length)]
        + [low_vm(width, length), low_vm(width, length)]
        + [full_vm(length, width), full_vm(length, width), low_vm(width, length), two, two]
    )
    grad_x, grad_self_vec, *target = call(
        self_back_body,
        "self_back",
        scal,
        None,
        [
            ("smem", table),
            whole(x),
            part(weight, 0, 3 * width),
            part(weight, 3 * width, width),
            self_vec,
            whole(resid),
            whole(query),
            whole(key),
            whole(value),
            whole(ctx_t),
            whole(lse),
            either(
                [(grad_inner, 0, 0, length)],
                [(grad_one, 0, 0, some)],
            ),
            either([], [(swap_other, 0, 0, 3 * some)]),
        ]
        + [("hbm", one) for one in target],
        [store(length, width), store(3, width)] + slot_outs,
        back_scratch + stage_of(4),
        [(13 + number, 2 + number) for number in range(len(slots))],
    )
    target = call(
        merge_body,
        "merge",
        scal,
        0,
        [
            ("smem", table),
            whole(grad_rest),
            whole(grad_rest_other),
        ]
        + [("hbm", one) for one in target],
        slot_outs,
        stage_of(10),
        [(3 + number, number) for number in range(len(slots))],
    )
    vec_grads = jnp.concatenate(
        [
            jnp.where(is_source, grad_self_vec, 0.0),
            jnp.where(is_source, grad_memory_vec, 0.0),
            jnp.where(is_source, 0.0, grad_self_vec),
            grad_middle_vec,
        ],
        0,
    )
    if on_ring:
        grads = target[0].reshape(wide_size, 2, capacity, half_rows, width)
        mine, vec_grads = ring_scatter(grads, target[1:], vec_grads)
    else:
        mine = lax.psum_scatter(target[0], ("wide", "narrow"), scatter_dimension=0, tiled=True)
        for axis in ("narrow", "wide", "half"):
            vec_grads = sum_over(vec_grads, axis)
    if on_ring:
        sums = join(mine, jnp.zeros((FLOW, half_rows, width), single))
        cut = plan[0][position]
        lent = lax.dynamic_slice_in_dim(sums, cut, FLOW, 0).astype(bfloat)
        cut = cut + plan[1][(position - 1) % wide_size]
        lent_above = lax.dynamic_slice_in_dim(sums, cut, FLOW, 0).astype(bfloat)
        above, below = round_ring(lent, -1), round_ring(lent_above, 1)
        states = (master[0], moment_one[0], moment_two[0])
        state = states[0].shape
        results = call(
            adam_kept_body,
            "adam_kept",
            scal,
            None,
            [("smem", plan), whole(mine)] + [whole(one) for one in states],
            [store(*state)] * 3 + [low_out(*state)],
            [],
        )
        new_first, new_second, new_weight, new_copy = call(
            adam_lent_body,
            "adam_lent",
            scal,
            None,
            [("smem", plan), ("hbm", below), ("hbm", above)]
            + [("hbm", one) for one in states]
            + [("hbm", one) for one in results],
            [("hbm", shaped(*state))] * 3 + [("hbm", low(*state))],
            [
                full_vm(3, *state),
                low_vm(*state),
                full_vm(3, *state),
                low_vm(*state),
                pltpu.SemaphoreType.DMA((4, state[0])),
                pltpu.SemaphoreType.DMA((4, state[0])),
            ],
            [(6 + number, number) for number in range(4)],
        )
    else:
        used = jnp.sum((owner_row == wide_at).astype(jnp.int32))
        mine = jnp.where((jnp.arange(capacity) < used)[:, None, None], mine.astype(single), 0.0)
        new_weight, new_first, new_second = adam(
            master[0], mine, moment_one[0], moment_two[0], rate_matrix, decay_matrix
        )
        new_copy = new_weight.astype(bfloat)
    vec_weight, vec_first, vec_second = adam(
        vec_master, vec_grads, vec_one, vec_two, rate_vector, 0.0
    )
    return (
        jnp.where(is_source, memory, output)[None, None],
        grad_x[None, None],
        new_first[None],
        new_second[None],
        new_weight[None],
        new_copy[None],
        vec_first,
        vec_second,
        vec_weight,
    )


def solution(mesh):
    in_specs = (
        P("half", ("wide", "narrow"), None, None),
        P(("wide", "narrow"), None, None),
        P(None, ("wide", "narrow")),
        P("half", None),
        P("half", "wide", "narrow", None),
        P("half", "wide", "narrow", None),
        P("half", "wide", "narrow", None),
        P(),
        P(),
        P(),
    )
    out_specs = (
        P("half", ("wide", "narrow"), None, None),
        P("half", ("wide", "narrow"), None, None),
        P("half", "wide", "narrow", None),
        P("half", "wide", "narrow", None),
        P("half", "wide", "narrow", None),
        P("half", "wide", "narrow", None),
        P(),
        P(),
        P(),
    )
    return jax.shard_map(
        on_device, mesh=mesh, in_specs=in_specs, out_specs=out_specs, check_vma=False
    )
```

```python
import math
from functools import partial

import jax
import jax.numpy as jnp
from jax import lax
from jax.experimental import pallas as pl
from jax.experimental.pallas import tpu as pltpu
from jax.sharding import PartitionSpec as P

HEADS = 8
STEP = 5
CAUSAL = 512
RB = 1024
NEG = -1e30

eps_norm = 1e-05
beta_one = 0.5
beta_two = 0.5
rate_matrix = 0.05
rate_vector = 0.3
decay_matrix = 0.01
eps_adam = 1e-08
bfloat = jnp.bfloat16
single = jnp.float32
VM = pl.BlockSpec(memory_space=pltpu.VMEM)
SM = pl.BlockSpec(memory_space=pltpu.SMEM)
HB = pl.BlockSpec(memory_space=pl.ANY)


def mm(left, right):
    return jnp.dot(left, right, preferred_element_type=single)


def mm_tn(left, right):
    return lax.dot_general(left, right, (((0,), (0,)), ((), ())), preferred_element_type=single)


def mm_nt(left, right):
    return lax.dot_general(left, right, (((1,), (1,)), ((), ())), preferred_element_type=single)


def block_of(index, size):
    return pl.ds(pl.multiple_of(index * size, size), size)


def normed(resid):
    center = resid - jnp.mean(resid, -1, keepdims=True)
    spread = jnp.mean(center * center, -1, keepdims=True)
    rstd = lax.rsqrt(spread + eps_norm)
    return center * rstd, rstd


def norm_back(resid, grad, gain):
    hat, rstd = normed(resid)
    grad_hat = grad * gain
    grad_resid = rstd * (
        grad_hat
        - jnp.mean(grad_hat, -1, keepdims=True)
        - hat * jnp.mean(grad_hat * hat, -1, keepdims=True)
    )
    return grad_resid, jnp.sum(grad * hat, 0, keepdims=True), jnp.sum(grad, 0, keepdims=True)


def gelu_parts(pre_act):
    half = 0.5 * (1.0 + lax.erf(pre_act * math.sqrt(0.5)))
    slope = half + pre_act * (jnp.exp(-0.5 * pre_act * pre_act) * (1.0 / math.sqrt(2.0 * math.pi)))
    return pre_act * half, slope


def pair_keys(tile, first_extra, ones):
    rows = tile.shape[0]
    lane = lax.broadcasted_iota(jnp.int32, (rows, 128), 1)
    wide_tile = tile.astype(single)
    out = []
    for head in range(2):
        at = lane - (64 - 64 * head)
        extra = jnp.where(at == 0, first_extra, jnp.where((at > 0) & (at < ones), 1.0, 0.0))
        mine = (lane < 64) if head == 0 else (lane >= 64)
        out.append(jnp.where(mine, wide_tile, extra).astype(bfloat))
    return out


def pair_queries(tile, head, extra_rows):
    mine = tile[64 * head : 64 * head + 64]
    row = lax.broadcasted_iota(jnp.int32, mine.shape, 0)
    extra = jnp.zeros(mine.shape, single)
    for number, value in enumerate(extra_rows):
        extra = jnp.where(row == number, value, extra)
    extra = extra.astype(bfloat)
    return jnp.concatenate([mine, extra] if head == 0 else [extra, mine], 0)


def pack_rows(target, first, value):
    rows = value.shape[0]
    for number, one in enumerate(split_three(value)):
        target[first + number * rows : first + (number + 1) * rows] = one.astype(bfloat)


def unpack_rows(packed, rows):
    high, middle, rest = (packed[n * rows : (n + 1) * rows].astype(single) for n in range(3))
    return (high + middle) + rest


def split_three(value):
    high = value.astype(bfloat).astype(single)
    rest = value - high
    middle = rest.astype(bfloat).astype(single)
    return [high, middle, rest - middle]


def key_bias(limit, rows):
    row = lax.broadcasted_iota(jnp.int32, (rows, 128), 0)
    return jnp.where(row < limit, 0.0, NEG)


def score_parts(scores, diagonal):
    if not diagonal:
        return [scores]
    size = scores.shape[1]
    cut = scores.shape[0] - size
    row = lax.broadcasted_iota(jnp.int32, (size, size), 0)
    column = lax.broadcasted_iota(jnp.int32, (size, size), 1)
    last = jnp.where(row <= column, scores[cut:], NEG)
    return [scores[:cut], last] if cut else [last]


def over_blocks(causal, rows, length, body):
    def every():
        body(0, rows, length, False)

    if causal is None:
        every()
        return
    pl.when(causal == 0)(every)

    @pl.when(causal != 0)
    def _():
        for first in range(0, rows, CAUSAL):
            body(first, CAUSAL, first + CAUSAL, True)


def head_rows(group, heads, head):
    return pl.ds(pl.multiple_of((group * heads + head) * 64, 64), 64)


def attend(limit, causal, key_ref, query_t, value_t, ctx_t, lse_ref, key_tiles):
    length, width = key_ref.shape
    heads = key_tiles.shape[0]
    bias = key_bias(limit, length)

    def group_of(group, unused):
        for number in range(heads // 2):
            columns = block_of(group * (heads // 2) + number, 128)
            for head, tile in enumerate(pair_keys(key_ref[:, columns], bias, 1)):
                key_tiles[2 * number + head] = tile

        def body(first, queries, extent, diagonal):
            at = slice(first, first + queries)

            def scores_of(head):
                columns = block_of(group * (heads // 2) + head // 2, 128)
                tile = pair_queries(query_t[columns, at], head % 2, [1.0])
                return mm(key_tiles[head, :extent], tile)

            following = scores_of(0)
            for head in range(heads):
                parts = score_parts(following, diagonal)
                if head + 1 < heads:
                    following = scores_of(head + 1)
                top = jnp.max(parts[0], 0, keepdims=True)
                for more in parts[1:]:
                    top = jnp.maximum(top, jnp.max(more, 0, keepdims=True))
                parts = [jnp.exp(more - top) for more in parts]
                total = sum(jnp.sum(more, 0, keepdims=True) for more in parts)
                weights = jnp.concatenate([more.astype(bfloat) for more in parts], 0)
                mine = head_rows(group, heads, head)
                context = mm(value_t[mine, :extent], weights)
                ctx_t[mine, at] = (context * (1.0 / total)).astype(bfloat)
                lse_ref[pl.ds(group * heads + head, 1), at] = top + jnp.log(total)

        over_blocks(causal, query_t.shape[1], length, body)
        return 0

    lax.fori_loop(0, HEADS // heads, group_of, 0)


def attend_back(
    limit, causal, query_ref, key_ref, value_ref, query_t, key_t, grad_ctx, grad_ctx_t, lse_ref, dot_ref,
    grad_key, grad_value, grad_query_t, key_two, value_two,
):
    length, width = key_ref.shape
    bias = key_bias(limit, length)

    def pair(number, unused):
        columns = block_of(number, 128)
        for head, tile in enumerate(pair_keys(key_ref[:, columns], bias, 4)):
            key_two[head] = tile
        for head, tile in enumerate(pair_keys(value_ref[:, columns], 1.0, 3)):
            value_two[head] = tile

        def body(first, queries, extent, diagonal):
            at = slice(first, first + queries)

            def products_of(head):
                row = pl.ds(number * 2 + head, 1)
                constants = [1.0] + split_three(-lse_ref[row, at])
                scores = mm(
                    key_two[head, :extent], pair_queries(query_t[columns, at], head, constants)
                )
                constants = split_three(-dot_ref[row, at])
                grad_weights = mm(
                    value_two[head, :extent], pair_queries(grad_ctx_t[columns, at], head, constants)
                )
                return scores, grad_weights

            lane = lax.broadcasted_iota(jnp.int32, (queries, 128), 1)

            def both(tile):
                tile = tile.astype(single)
                return jnp.concatenate(
                    [
                        jnp.where(lane < 64, tile, 0.0).astype(bfloat),
                        jnp.where(lane < 64, 0.0, tile).astype(bfloat),
                    ],
                    0,
                )

            all_weights, all_grads = [], []
            following = products_of(0)
            for head in range(2):
                scores, grad_weights = following
                if head == 0:
                    following = products_of(1)
                weights = [jnp.exp(more) for more in score_parts(scores, diagonal)]
                weights = jnp.concatenate(weights, 0)
                grads = (weights * grad_weights).astype(bfloat)
                all_weights.append(weights.astype(bfloat))
                all_grads.append(grads)
                mine = head_rows(number, 2, head)
                grad_query = mm(key_t[mine, :extent], grads)
                grad_query_t[mine, at] = (grad_query * 0.125).astype(bfloat)
            for out, parts, other in (
                (grad_value, all_weights, grad_ctx),
                (grad_key, all_grads, query_ref),
            ):
                total = mm(jnp.concatenate(parts, 1), both(other[at, columns]))
                if first:
                    total = jnp.concatenate([out[:first, columns] + total[:first], total[first:]], 0)
                out[:extent, columns] = total

        over_blocks(causal, query_t.shape[1], length, body)
        return 0

    lax.fori_loop(0, width // 128, pair, 0)


def by_rows(length, body, init=0):
    if length <= RB:
        return body(pl.ds(0, length), init)

    def step(index, carry):
        return body(block_of(index, RB), carry)

    return lax.fori_loop(0, length // RB, step, init)


class Emitter:
    def __init__(self, table, targets, stage, semaphores):
        self.table, self.targets, self.stage, self.semaphores = table, targets, stage, semaphores
        self.copies = []

    def chunk(self, number, first_piece, value):
        stage, half_rows = self.stage, self.targets[0].shape[1]
        stage[number] = value.astype(bfloat)
        count = stage.shape[1] // half_rows
        per_piece = 128 // half_rows
        for part in range(count):
            source = stage.at[number, pl.ds(part * half_rows, half_rows)]
            semaphore = self.semaphores.at[number * count + part]
            slot = self.table[first_piece * per_piece + part]

            def start(targets, first, source=source, semaphore=semaphore, slot=slot):
                def go():
                    pltpu.make_async_copy(source, targets[0].at[slot - first], semaphore).start()

                if len(targets) == 1:
                    go()
                    return
                last = first + targets[0].shape[0]
                pl.when(slot < last)(go)
                pl.when(slot >= last)(lambda: start(targets[1:], last))

            start(self.targets, 0)
            self.copies.append(pltpu.make_async_copy(source, self.targets[0].at[0], semaphore))

    def wait(self):
        for copy in self.copies:
            copy.wait()


class Moves:
    def __init__(self, role, spare):
        self.role = role
        self.spare = spare
        self.some = []
        self.loads = []
        self.stores = []
        self.begun = set()
        self.waited = set()

    def load(self, dest, ways, semaphores):
        def each(way, act):
            for number, (source, first, at, rows) in enumerate(way):
                target = dest
                if rows is not None:
                    source = source.at[pl.ds(first, rows)]
                    target = dest.at[pl.ds(at, rows)]
                act(pltpu.make_async_copy(source, target, semaphores.at[number]))

        def split(act):
            if len(ways) == 1:
                each(ways[0], act)
                return
            pl.when(self.role != 0)(lambda: each(ways[0], act))
            pl.when(self.role == 0)(lambda: each(ways[1], act))

        self.loads.append((dest, split))

    def begin(self, *refs):
        for number, (dest, split) in enumerate(self.loads):
            if number not in self.begun and any(dest is ref for ref in refs):
                self.begun.add(number)
                split(lambda copy: copy.start())

    def need(self, *refs):
        self.begin(*refs)
        for number, (dest, split) in enumerate(self.loads):
            if number not in self.waited and any(dest is ref for ref in refs):
                self.waited.add(number)
                split(lambda copy: copy.wait())

    def follow(self, *refs):
        self.begin(*refs)
        for dest, unused in self.loads:
            self.begin(dest)

    def rest(self):
        self.follow()
        self.need(*[dest for dest, unused in self.loads])

    def place(self, source, target, semaphores):
        self.stores.append((source, target, semaphores, []))

    def put(self, *refs):
        for source, target, semaphores, copies in self.stores:
            if not copies and any(source is ref for ref in refs):
                copies.append(pltpu.make_async_copy(source, target, semaphores.at[0]))
                copies[0].start()

    def put_rows(self, ref, first, rows):
        for source, target, semaphores, copies in self.stores:
            if source is ref:
                at = pl.ds(first, rows)
                copies.append(
                    pltpu.make_async_copy(source.at[at], target.at[at], semaphores.at[len(copies)])
                )
                copies[-1].start()

    def put_if(self, wanted, source, target):
        copy = pltpu.make_async_copy(source, target, self.spare.at[len(self.some)])
        pl.when(wanted)(copy.start)
        self.some.append((wanted, copy))

    def finish(self):
        self.rest()
        self.put(*[entry[0] for entry in self.stores])
        for entry in self.stores:
            for copy in entry[3]:
                copy.wait()
        for wanted, copy in self.some:
            pl.when(wanted)(copy.wait)


def part(value, first, rows):
    return ("load", [[(value, first, 0, rows)]])


def whole(value):
    return ("load", [[(value, 0, 0, None)]])


def either(source_way, target_way):
    return ("load", [source_way, target_way])


def call(body, name, scal, active, ins, outs, scratch, aliases=(), limit=58):
    args, specs, scratch_all, plan = [scal], [SM], [], []
    counts = {"load": 0, "store": 0}

    def arg(value, spec):
        args.append(value)
        specs.append(spec)
        return len(args) - 1

    held = []
    for kind, value in ins:
        if kind == "load":
            ways = [[(arg(v, HB), first, at, rows) for v, first, at, rows in way] for way in value]
            way = value[0] or value[1]
            v, first, at, rows = way[0]
            total = max(a + r for _, _, a, r in way) if rows is not None else None
            shape = v.shape if rows is None else (total,) + v.shape[1:]
            held.append(("load", ways, shape, v.dtype, max(len(w) for w in ways)))
        else:
            held.append((kind, arg(value, SM if kind == "smem" else HB)))
    vmem, sems = [], []
    for entry in held:
        if entry[0] == "load":
            vmem.append(pltpu.VMEM(entry[2], entry[3]))
            sems.append(pltpu.SemaphoreType.DMA((entry[4],)))
    for kind, shape in outs:
        if kind == "store":
            vmem.append(pltpu.VMEM(shape.shape, shape.dtype))
            sems.append(pltpu.SemaphoreType.DMA((6,)))
    count_in, count_out = len(args), len(outs)

    def kernel(*refs):
        inputs, outputs = refs[:count_in], refs[count_in : count_in + count_out]
        rest = refs[count_in + count_out :]
        buffers, semaphores = list(rest[: len(vmem)]), list(rest[len(vmem) : len(vmem) + len(sems)])
        spare, *extra = rest[len(vmem) + len(sems) :]
        scal_ref = inputs[0]

        def run():
            moves = Moves(scal_ref[2], spare)
            given = []
            for entry in held:
                if entry[0] == "load":
                    dest, semaphore = buffers.pop(0), semaphores.pop(0)
                    ways = [[(inputs[i], f, a, r) for i, f, a, r in way] for way in entry[1]]
                    moves.load(dest, ways, semaphore)
                    given.append(dest)
                else:
                    given.append(inputs[entry[1]])
            for (kind, unused), output in zip(outs, outputs):
                if kind == "store":
                    source, semaphore = buffers.pop(0), semaphores.pop(0)
                    moves.place(source, output, semaphore)
                    given.append(source)
                else:
                    given.append(output)
            body(moves, scal_ref, *given, *extra)
            moves.finish()

        if active is None:
            run()
        else:
            pl.when(scal_ref[2] == active)(run)

    pairs = {}
    for position, output in aliases:
        pairs[held[position][1]] = output
    return pl.pallas_call(
        kernel,
        in_specs=specs,
        out_specs=[HB] * count_out,
        out_shape=[shape for unused, shape in outs],
        scratch_shapes=vmem + sems + [pltpu.SemaphoreType.DMA((2,))] + list(scratch),
        input_output_aliases=pairs,
        compiler_params=pltpu.CompilerParams(vmem_limit_bytes=62 << 20),
        name=name,
    )(*args)


def halves_of(length):
    return [pl.ds(0, length // 2), pl.ds(length // 2, length // 2)]


def zero_rows(width):
    return (jnp.zeros((1, width), single),) * 3


def put_rows(ref, rows):
    for number, row in enumerate(rows):
        ref[number : number + 1] = row


def project_norm(io, length, ctx_t, weight, inner_ref, vec, resid_ref, out_ref):
    for rows in halves_of(length):
        branch = mm(ctx_t[:, rows].T, weight[...])
        resid = inner_ref[rows].astype(single) * vec[0:1] + branch
        resid_ref[rows] = resid
        out_ref[rows] = normed(resid)[0] * vec[1:2] + vec[2:3]
        for ref in (resid_ref, out_ref):
            io.put_rows(ref, rows.start, rows.size)


def self_forward(io, scal, x, weight, vec, outs, query_t, value_t, key_tiles, packed, ready):
    query, key, value, ctx_t, lse, resid, out, swap = outs
    length, width = x.shape
    some = length // 2
    io.begin(x)
    ready()
    io.need(x)
    io.follow()

    def body(rows, carry):
        tile = x[rows]
        for number, ref in enumerate((query, key, value)):
            ref[rows] = mm(tile, weight[width * number : width * (number + 1)]).astype(bfloat)
        query_t[:, rows] = (query[rows] * bfloat(0.125)).T
        value_t[:, rows] = value[rows].T
        return carry

    by_rows(length, body)
    io.put(query, key, value)
    attend(scal[0], scal[1], key, query_t, value_t, ctx_t, lse, key_tiles)
    io.put(ctx_t, lse)
    io.rest()
    project_norm(io, length, ctx_t, weight.at[3 * width :], x, vec, resid, out)

    pl.when(scal[2] == 0)(lambda: pack_rows(packed, 0, out[some:]))
    io.put_if(scal[2] == 0, packed, swap.at[pl.ds(0, 3 * some)])


def self_forward_body(io, scal, x, weight, vec, *refs):
    io.begin(x)
    self_forward(io, scal, x, weight, vec, refs[:8], *refs[8:], lambda: io.need(weight))


def placed_forward_body(where, io, scal, table, x, vec, *refs):
    sources, refs = refs[: len(where)], refs[len(where) :]
    outs, (weight, rest) = refs[:8], refs[8:10]
    query_t, value_t, key_tiles, packed, semaphores = refs[10:]
    size = sources[0].shape[1]
    cut = weight.shape[0] // size
    io.begin(x)

    for source, ranges in zip(sources, where):
        for start, stop, distance, other, first in ranges:

            def step(slot, unused):
                piece = table[distance, first + slot - start]
                at = piece * 2 + (scal[5] if other == 0 else 1 - scal[5])

                def move(target, place, semaphore):
                    place = pl.ds(pl.multiple_of(place * size, size), size)
                    pltpu.make_async_copy(source.at[slot], target.at[place], semaphore).start()

                pl.when((piece >= 0) & (at < cut))(lambda: move(weight, at, semaphores.at[0]))
                pl.when(at >= cut)(lambda: move(rest, at - cut, semaphores.at[1]))
                return 0

            lax.fori_loop(start, stop, step, 0)

    def ready():
        pltpu.make_async_copy(weight, weight, semaphores.at[0]).wait()
        io.put(weight)

    self_forward(io, scal, x, weight, vec, outs, query_t, value_t, key_tiles, packed, ready)
    pltpu.make_async_copy(rest, rest, semaphores.at[1]).wait()
    io.put(rest)


def encoder_ff_body(
    io, scal, inner, up, down, cross, vec, held, activ, slope, resid, memory, swap, sendout
):
    length, width = inner.shape
    io.need(inner, up)
    io.follow(down)
    for rows in [pl.ds(0, length)]:
        act, grad = gelu_parts(mm_nt(inner[rows].astype(bfloat), up[...]))
        activ[rows] = act.astype(bfloat)
        slope[rows] = grad.astype(bfloat)
        for ref in (activ, slope):
            io.put_rows(ref, rows.start, rows.size)
    io.rest()
    for rows in [pl.ds(0, length)]:
        total = inner[rows] * vec[0:1] + mm(activ[rows], down[...])
        resid[rows] = total
        mem = (normed(total)[0] * vec[1:2] + vec[2:3]).astype(bfloat)
        memory[rows] = mem
        sendout[rows] = mm(mem, cross[:width]).astype(bfloat)
        sendout[pl.ds(length + rows.start, rows.size)] = mm(mem, cross[width:]).astype(bfloat)
        for ref in (resid, memory):
            io.put_rows(ref, rows.start, rows.size)
    io.put_if(scal[2] != 0, sendout, swap)


def ff_back(length, emit, grad_branch, activ, slope, inner_low, up, down, grad_inner):
    def body(rows, carry):
        grad = mm_nt(grad_branch[rows], down[...]) * slope[rows].astype(single)
        grad = grad.astype(bfloat)
        slope[rows] = grad
        grad_inner[rows] += mm(grad, up[...])
        return carry

    by_rows(length, body)
    for number in range(activ.shape[1] // 512):
        columns = slice(number * 512, (number + 1) * 512)
        emit(0, number, mm_tn(slope[:, columns], inner_low[...]))
        emit(1, number, mm_tn(activ[:, columns], grad_branch[...]))


def branch_back(length, resid, grad_out, inner, vec, grad_branch, grad_inner, grad_vec):
    width = resid.shape[1]

    def body(rows, carry):
        grad_resid, grad_gain, grad_shift = norm_back(resid[rows], grad_out[rows], vec[1:2])
        grad_branch[rows] = grad_resid.astype(bfloat)
        grad_inner[rows] = grad_resid * vec[0:1]
        weigh = jnp.sum(grad_resid * inner[rows].astype(single), 0, keepdims=True)
        return (carry[0] + weigh, carry[1] + grad_gain, carry[2] + grad_shift)

    put_rows(grad_vec, by_rows(length, body, zero_rows(width)))


def ctx_back(length, grad_branch, weight, ctx_t, grad_ctx, grad_ctx_t, dot_ref):
    def body(rows, carry):
        grad_ctx[rows] = mm_nt(grad_branch[rows], weight[...]).astype(bfloat)
        grad_ctx_t[:, rows] = grad_ctx[rows].T
        for head in range(HEADS):
            mine = slice(64 * head, 64 * head + 64)
            product = grad_ctx_t[mine, rows].astype(single) * ctx_t[mine, rows].astype(single)
            dot_ref[head : head + 1, rows] = jnp.sum(product, 0, keepdims=True)
        return carry

    by_rows(length, body)


def middle_body(
    io, scal, inner, packed, keys, cross, cross_vec, up, down, ff_vec, cotan,
    output, sendback, grad_inner, grads, grad_vec, swap,
    query, query_t, ctx_t, lse, resid, after, activ, slope, low_rows, grad_branch, grad_after,
    grad_ctx, grad_ctx_t, dot_ref, key_t, value_t, grad_key, grad_value, grad_query_t,
    key_tiles, key_two, value_two, swap_out,
):
    rows_here, width = inner.shape
    hidden, length = up.shape[0], keys.shape[0] // 2
    key_rows, value_rows = keys.at[:length], keys.at[length:]
    io.need(inner, packed, cross, keys)
    io.follow(cross_vec, up, down)

    @pl.when(scal[2] != 0)
    def _():
        inner[...] = unpack_rows(packed, rows_here)

    def project(rows, carry):
        query[rows] = mm(inner[rows].astype(bfloat), cross[:width]).astype(bfloat)
        query_t[:, rows] = (query[rows] * bfloat(0.125)).T
        return carry

    def turn(rows, carry):
        key_t[:, rows] = key_rows[rows].T
        value_t[:, rows] = value_rows[rows].T
        return carry

    by_rows(rows_here, project)
    by_rows(length, turn)
    attend(scal[4], None, key_rows, query_t, value_t, ctx_t, lse, key_tiles)
    io.rest()
    project_norm(io, rows_here, ctx_t, cross.at[width:], inner, cross_vec, resid, after)

    def feed(rows, carry):
        tile = after[rows]
        low_tile = tile.astype(bfloat)
        low_rows[rows] = low_tile
        act, grad = gelu_parts(mm_nt(low_tile, up[...]))
        act = act.astype(bfloat)
        activ[rows] = act
        slope[rows] = grad.astype(bfloat)
        total = tile * ff_vec[0:1] + mm(act, down[...])
        output[rows] = (normed(total)[0] * ff_vec[1:2] + ff_vec[2:3]).astype(bfloat)
        row = lax.broadcasted_iota(jnp.int32, tile.shape, 0) + rows.start
        grad_out = jnp.where(row < scal[3], cotan[rows].astype(single), 0.0)
        grad_resid, grad_gain, grad_shift = norm_back(total, grad_out, ff_vec[1:2])
        grad_branch[rows] = grad_resid.astype(bfloat)
        grad_after[rows] = grad_resid * ff_vec[0:1]
        weigh = jnp.sum(grad_resid * tile, 0, keepdims=True)
        return (carry[0] + weigh, carry[1] + grad_gain, carry[2] + grad_shift)

    put_rows(grad_vec.at[3:], by_rows(rows_here, feed, zero_rows(width)))
    io.put(output)

    def emit(which, number, value):
        first = 2 * width + which * hidden + number * 512
        grads[first : first + 512] = value.astype(bfloat)
        if which == 1 and number in (1, 3):
            for start in (2 * width, 2 * width + hidden):
                io.put_rows(grads, start + (number - 1) * 512, 1024)

    ff_back(rows_here, emit, grad_branch, activ, slope, low_rows, up, down, grad_after)
    branch_back(rows_here, resid, grad_after, inner, cross_vec, grad_branch, grad_inner, grad_vec)
    io.put(grad_vec)
    grads[width : 2 * width] = mm(ctx_t[...], grad_branch[...]).astype(bfloat)
    ctx_back(rows_here, grad_branch, cross.at[width:], ctx_t, grad_ctx, grad_ctx_t, dot_ref)
    attend_back(
        scal[4], None, query, key_rows, value_rows, query_t, key_t, grad_ctx, grad_ctx_t, lse, dot_ref,
        grad_key, grad_value, grad_query_t, key_two, value_two,
    )

    def send(rows, carry):
        sendback[rows] = (grad_key[rows] * 0.125).astype(bfloat)
        sendback[pl.ds(length + rows.start, rows.size)] = grad_value[rows].astype(bfloat)
        return carry

    by_rows(length, send)
    io.put(sendback)
    io.put_if(scal[2] == 0, sendback, swap)

    def last(rows, carry):
        grad_query = grad_query_t[:, rows].T
        grad_inner[rows] += mm_nt(grad_query, cross[:width])
        grad_ctx[rows] = grad_query
        return carry

    by_rows(rows_here, last)
    io.put(grad_inner)

    @pl.when(scal[2] != 0)
    def _():
        pack_rows(swap_out, 0, grad_inner[...])
        swap_out[3 * rows_here :] = output[...]

    io.put_if(scal[2] != 0, swap_out, swap)

    grads[:width] = mm_tn(inner[...].astype(bfloat), grad_ctx[...]).astype(bfloat)
    io.put_rows(grads, 0, 2 * width)


def encoder_back_body(
    io, scal, table, own, received, memory, cross, inner, resid, activ, slope, up, down, vec,
    grad_inner, grad_vec, *rest_of,
):
    length, width = inner.shape
    *targets, grad_mem, inner_low, grad_branch, stage, semaphores = rest_of
    emit = Emitter(table, targets, stage, semaphores)
    io.begin(own, received, cross, inner)
    io.follow(memory, vec, resid, down, slope, up, activ)
    io.need(own, received, cross, inner)

    def body(rows, carry):
        own[...] = added(own[...], received[...])
        grad_mem[rows] = mm_nt(own[:length], cross[:width]) + mm_nt(own[length:], cross[width:])
        inner_low[rows] = inner[rows].astype(bfloat)
        return carry

    by_rows(length, body)
    io.need(vec, resid, memory)
    emit.chunk(8, 16, mm_tn(memory[...], own[:length]))
    emit.chunk(9, 20, mm_tn(memory[...], own[length:]))
    branch_back(length, resid, grad_mem, inner, vec, grad_branch, grad_inner, grad_vec)
    io.put(grad_vec)
    io.rest()

    def each(which, number, value):
        emit.chunk(2 * number + which, 24 + 16 * which + 4 * number, value)

    ff_back(length, each, grad_branch, activ, slope, inner_low, up, down, grad_inner)
    io.put(grad_inner)
    emit.wait()


def self_back_body(
    io, scal, table, x, weight, out_weight, vec, resid, query, key, value, ctx_t, lse, grad_out, packed, *refs
):
    length, width = x.shape
    count = (len(refs) - 15) // 2
    grad_x, grad_vec, *targets = refs[count : 2 * count + 2]
    (
        grad_branch, grad_ctx, grad_ctx_t, dot_ref, query_t, key_t, grad_key, grad_value, grad_query_t,
        key_two, value_two, stage, semaphores,
    ) = refs[2 * count + 2 :]
    emit = Emitter(table, targets, stage, semaphores)
    some = length // 2
    io.need(resid, grad_out, packed, x, vec)
    io.follow(ctx_t, out_weight, query, key, value)

    @pl.when(scal[2] == 0)
    def _():
        grad_out[some:] = unpack_rows(packed, some)

    branch_back(length, resid, grad_out, x, vec, grad_branch, grad_x, grad_vec)
    io.put(grad_vec)
    io.need(ctx_t, out_weight)
    emit.chunk(3, 12, mm(ctx_t[...], grad_branch[...]))
    ctx_back(length, grad_branch, out_weight, ctx_t, grad_ctx, grad_ctx_t, dot_ref)
    io.rest()

    def body(rows, carry):
        query_t[:, rows] = (query[rows] * bfloat(0.125)).T
        key_t[:, rows] = key[rows].T
        return carry

    by_rows(length, body)
    attend_back(
        scal[0], scal[1], query, key, value, query_t, key_t, grad_ctx, grad_ctx_t, lse, dot_ref,
        grad_key, grad_value, grad_query_t, key_two, value_two,
    )

    def last(rows, carry):
        parts = (
            grad_query_t[:, rows].T,
            (grad_key[rows] * 0.125).astype(bfloat),
            grad_value[rows].astype(bfloat),
        )
        total = grad_x[rows]
        for number, low_grad in enumerate(parts):
            total += mm_nt(low_grad, weight[width * number : width * (number + 1)])
        grad_x[rows] = total
        grad_branch[rows], grad_ctx[rows], value[rows] = parts
        return carry

    by_rows(length, last)
    io.put(grad_x)
    for number, ref in enumerate((grad_branch, grad_ctx, value)):
        emit.chunk(number, 4 * number, mm_tn(x[...], ref[...]))
    emit.wait()


def merge_body(io, scal, table, own, other, *refs):
    count = (len(refs) - 2) // 2
    *targets, stage, semaphores = refs[count:]
    emit = Emitter(table, targets, stage, semaphores)
    io.rest()
    chunk = stage.shape[1]
    for number in range(own.shape[0] // chunk):
        rows = slice(number * chunk, (number + 1) * chunk)
        total = own[rows].astype(single) + other[rows].astype(single)
        emit.chunk(number, 16 + 4 * number, total)
    emit.wait()


RING = (0, 2, 4, 6, 7, 5, 3, 1)
LEAD = 6
LEVEL = 10
FLOW = 8


def lend_kernel(scal, owners, master, own_out, up_out, down_out, plan, counts, low_rows, loaded, sems):
    size = len(RING)
    load = pltpu.make_async_copy(master, loaded, sems.at[0])
    load.start()
    for place in range(size):
        counts[place] = 0

    def count(piece, unused):
        owner = owners[piece]
        place = jnp.where(owner % 2 == 0, owner // 2, size - 1 - owner // 2)
        counts[place] = counts[place] + 1
        return 0

    lax.fori_loop(0, owners.shape[0], count, 0)
    held = [counts[place] for place in range(size)]
    caps = [jnp.int32(FLOW)] * size
    for place in list(range(size - 1, -1, -1)) * 2:
        after = (place + 1) % size
        caps[place] = jnp.minimum(FLOW, caps[after] - held[after] + LEVEL)
    flows = [jnp.minimum(0, cap) for cap in caps]
    for place in list(range(size)) * 2:
        flows[place] = jnp.maximum(flows[place], flows[place - 1] + held[place] - LEVEL)
    for place in range(size):
        ahead = jnp.maximum(flows[place], 0)
        back = jnp.maximum(-flows[place - 1], 0)
        plan[0, place] = held[place] - ahead - back
        plan[1, place] = ahead
        plan[2, place] = back
    load.wait()
    rows = loaded.shape[0]
    low_rows[:rows] = loaded[...].astype(bfloat)
    kept = plan[0, scal[0]]
    copies = [
        pltpu.make_async_copy(low_rows.at[pl.ds(0, rows)], own_out, sems.at[0]),
        pltpu.make_async_copy(low_rows.at[pl.ds(kept, FLOW)], up_out, sems.at[1]),
        pltpu.make_async_copy(
            low_rows.at[pl.ds(kept + plan[1, scal[0]], FLOW)], down_out, sems.at[2]
        ),
    ]
    for copy in copies:
        copy.start()
    for copy in copies:
        copy.wait()


def borrow_kernel(scal, plan, own, below, above, lead_out, late_out, slots, sems, out_sems):
    size = len(RING)
    kept = plan[0, scal[0]]
    from_below = kept + plan[1, (scal[0] + size - 1) % size]
    from_above = from_below + plan[2, (scal[0] + 1) % size]
    for slot in range(LEVEL):

        def move(source, slot=slot):
            pltpu.make_async_copy(source, slots.at[slot], sems.at[slot]).start()

        pl.when(slot < kept)(lambda slot=slot, move=move: move(own.at[slot]))
        pl.when((slot >= kept) & (slot < from_below))(
            lambda slot=slot, move=move: move(below.at[slot - kept])
        )
        pl.when((slot >= from_below) & (slot < from_above))(
            lambda slot=slot, move=move: move(above.at[slot - from_below])
        )
    for slot in range(LEVEL):
        pl.when(slot < from_above)(pltpu.make_async_copy(own.at[0], slots.at[slot], sems.at[slot]).wait)
    copies = [
        pltpu.make_async_copy(slots.at[pl.ds(0, LEAD)], lead_out, out_sems.at[0]),
        pltpu.make_async_copy(slots.at[pl.ds(LEAD, LEVEL - LEAD)], late_out, out_sems.at[1]),
    ]
    for copy in copies:
        copy.start()
    for copy in copies:
        copy.wait()


def lend(position, owner_row, master):
    slot = master.shape[1:]
    rows = master.shape[0]
    where = position[None].astype(jnp.int32)
    own, up, down, plan = pl.pallas_call(
        lend_kernel,
        in_specs=[SM, SM, HB],
        out_specs=[HB, HB, HB, SM],
        out_shape=[
            low(rows, *slot),
            low(FLOW, *slot),
            low(FLOW, *slot),
            jax.ShapeDtypeStruct((3, len(RING)), jnp.int32),
        ],
        scratch_shapes=[
            pltpu.SMEM((len(RING),), jnp.int32),
            low_vm(rows + FLOW, *slot),
            full_vm(rows, *slot),
            pltpu.SemaphoreType.DMA((3,)),
        ],
        name="lend",
    )(where, owner_row, master)
    below, above = round_ring(up, 1), round_ring(down, -1)
    lead, late = pl.pallas_call(
        borrow_kernel,
        in_specs=[SM, SM, HB, HB, HB],
        out_specs=[HB, HB],
        out_shape=[low(LEAD, *slot), low(LEVEL - LEAD, *slot)],
        scratch_shapes=[
            low_vm(LEVEL, *slot),
            pltpu.SemaphoreType.DMA((LEVEL,)),
            pltpu.SemaphoreType.DMA((2,)),
        ],
        name="borrow",
    )(where, plan, own, below, above)
    return lead, late, plan


def adam_kept_body(
    io, scal, plan, sums, master, first, second, new_first, new_second, new_master, new_copy
):
    io.rest()
    count, place = master.shape[0], scal[6]
    kept = plan[0, place]
    held = kept + plan[1, place] + plan[2, place]

    def update(slot, gradient):
        weight, one, two = adam(
            master[slot], gradient, first[slot], second[slot], rate_matrix, decay_matrix
        )
        new_first[slot], new_second[slot], new_master[slot] = one, two, weight
        new_copy[slot] = weight.astype(bfloat)

    def step(slot, unused):
        pl.when(slot < kept)(lambda: update(slot, sums[slot]))
        pl.when(slot >= held)(lambda: update(slot, jnp.zeros(master.shape[1:], single)))
        return 0

    for start in range(0, count, count // 2):
        lax.fori_loop(start, start + count // 2, step, 0)
        for ref in (new_first, new_second, new_master, new_copy):
            io.put_rows(ref, start, count // 2)


def adam_lent_body(
    io, scal, plan, below, above, master, first, second, one_held, two_held, weight_held, copy_held,
    new_first, new_second, new_master, new_copy,
    states, gradients, results, low_result, in_sems, out_sems,
):
    count, place = master.shape[0], scal[6]
    kept = plan[0, place]
    from_above = kept + plan[1, place]
    held = from_above + plan[2, place]

    def each(act):
        def step(slot, unused):
            pl.when((slot >= kept) & (slot < held))(lambda: act(slot))
            return 0

        lax.fori_loop(0, count, step, 0)

    def copies_in(slot):
        sources = [ref.at[slot] for ref in (master, first, second)]
        return [
            pltpu.make_async_copy(source, states.at[number, slot], in_sems.at[number, slot])
            for number, source in enumerate(sources)
        ]

    def copies_out(slot):
        outs = [
            pltpu.make_async_copy(results.at[number, slot], ref.at[slot], out_sems.at[number, slot])
            for number, ref in enumerate((new_first, new_second, new_master))
        ]
        return outs + [
            pltpu.make_async_copy(low_result.at[slot], new_copy.at[slot], out_sems.at[3, slot])
        ]

    def begin(slot):
        for copy in copies_in(slot):
            copy.start()

        def fetch(source):
            pltpu.make_async_copy(source, gradients.at[slot], in_sems.at[3, slot]).start()

        pl.when(slot < from_above)(lambda: fetch(above.at[slot - kept]))
        pl.when(slot >= from_above)(lambda: fetch(below.at[slot - from_above]))

    def update(slot):
        for copy in copies_in(slot):
            copy.wait()
        pltpu.make_async_copy(below.at[0], gradients.at[slot], in_sems.at[3, slot]).wait()
        weight, one, two = adam(
            states[0, slot],
            gradients[slot].astype(single),
            states[1, slot],
            states[2, slot],
            rate_matrix,
            decay_matrix,
        )
        results[0, slot], results[1, slot], results[2, slot] = one, two, weight
        low_result[slot] = weight.astype(bfloat)
        for copy in copies_out(slot):
            copy.start()

    def end(slot):
        for copy in copies_out(slot):
            copy.wait()

    each(begin)
    each(update)
    each(end)


def round_ring(value, step):
    count = len(RING)
    return lax.ppermute(value, "wide", [(RING[i], RING[(i + step) % count]) for i in range(count)])


def swapped(value):
    return lax.ppermute(value, "narrow", [(0, 1), (1, 0)])


def step_of(up, down, across):
    return lax.optimization_barrier((round_ring(up, 1), round_ring(down, -1), swapped(across)))


def partner(value, axis, bit):
    return lax.ppermute(value, axis, [(i, i ^ bit) for i in range(lax.axis_size(axis))])


def join(*values):
    return jnp.concatenate(values, 0)


def ring_gather(own_lead, own_late, plan, make_tables):
    lead, late, half = LEAD, LEVEL - LEAD, LEAD // 2
    found = [([(0, lead, 0, 0, 0)], own_lead), ([(0, late, 0, 0, lead)], own_late)]

    def ahead(value, far, near):
        ranges = [(0, lead, far, 0, 0)]
        if near is not None:
            ranges += [(lead, lead + late, near, 0, lead), (lead + late, lead + 2 * late, near, 1, lead)]
        found.append((ranges, value))

    up, down, across = step_of(own_lead, own_lead, own_late)
    up, plan = lax.optimization_barrier((up, plan))
    tables = make_tables(plan)
    found.append(([(0, late, 0, 1, lead)], across))
    ahead(up, 7, None)
    ahead(down, 1, None)
    pair = join(own_late, across)
    up, down, across = step_of(join(up, pair), join(down, pair), join(up, down, own_lead[:half]))
    found.append(
        ([(0, lead, 7, 1, 0), (lead, 2 * lead, 1, 1, 0), (2 * lead, 2 * lead + half, 0, 1, 0)], across)
    )
    up, tables = lax.optimization_barrier((up, tables))
    ahead(up, 6, 7)
    ahead(down, 2, 1)
    up, down, across = step_of(up, down, join(up[:lead], down[:lead], own_lead[half:]))
    found.append(
        ([(0, lead, 6, 1, 0), (lead, 2 * lead, 2, 1, 0), (2 * lead, 2 * lead + half, 0, 1, half)], across)
    )
    ahead(up, 5, 6)
    ahead(down, 3, 2)
    up, down, across = step_of(join(up[:half], up[lead:]), down[half:], join(up[:lead], down[:lead]))
    found.append(([(0, lead, 5, 1, 0), (lead, 2 * lead, 3, 1, 0)], across))
    for value, first, near in ((up, 0, 5), (down, half, 3)):
        ranges = [(0, half, 4, 0, first), (half, half + late, near, 0, lead)]
        found.append((ranges + [(half + late, half + 2 * late, near, 1, lead)], value))
    up, down, across = step_of(
        up[half : half + late], down[half + late :], join(up[:half], down[:half])
    )
    found.append(([(0, late, 4, 0, lead)], up))
    found.append(([(0, late, 4, 1, lead)], down))
    found.append(([(0, lead, 4, 1, 0)], across))
    return found, tables


def added(*values):
    return sum(value.astype(single) for value in values).astype(bfloat)


def ring_scatter(grads, far, vector):
    partners = [("narrow", 1), ("wide", 1), ("wide", 2), ("wide", 4), ("half", 1)]

    def step_of(*values):
        nonlocal vector
        ring = (round_ring(values[0], 1), round_ring(values[1], -1), swapped(values[2]))
        *ring, other = lax.optimization_barrier((*ring, partner(vector, *partners.pop(0))))
        vector = vector + other
        return ring

    lead, half = LEAD, LEAD // 2
    late = grads.shape[2] - lead

    def both(distance):
        return grads[distance, :, lead:].reshape((-1,) + grads.shape[3:])

    def mine(distance, start=0, stop=lead):
        return grads[distance, 0, start:stop]

    def other(distance, start=0, stop=lead):
        return grads[distance, 1, start:stop]

    across, down, up = far
    up, down, across = step_of(up, down, across)
    first = added(mine(4), across)
    up = join(first[:half], added(up, grads[3, 0, lead:]), grads[3, 1, lead:])
    down = join(first[half:], grads[5, 0, lead:], added(down, grads[5, 1, lead:]))
    up, down, across = step_of(up, down, join(other(3), other(5)))
    up = join(
        added(mine(3, 0, half), across[:half], up[:half]),
        added(mine(3, half), across[half:lead]),
        added(up[half:], both(2)),
    )
    down = join(
        added(mine(5, 0, half), across[lead : lead + half]),
        added(mine(5, half), across[lead + half :], down[:half]),
        added(down[half:], both(6)),
    )
    up, down, across = step_of(up, down, join(other(2), other(6), other(0, 0, half)))
    nearest = [across[2 * lead :]]
    up = join(added(mine(2), across[:lead], up[:lead]), added(up[lead:], both(1)))
    down = join(added(mine(6), across[lead : 2 * lead], down[:lead]), added(down[lead:], both(7)))
    up, down, across = step_of(up, down, join(other(1), other(7), other(0, half)))
    nearest.append(across[2 * lead :])
    total = sum(value.astype(single) for value in (both(0), up[lead:], down[lead:]))
    up, down, across = step_of(
        added(mine(1), across[:lead], up[:lead]),
        added(mine(7), across[lead : 2 * lead], down[:lead]),
        total[late:].astype(bfloat),
    )
    first = sum(value.astype(single) for value in (mine(0), join(*nearest), up, down))
    return join(first, total[:late] + across.astype(single)), vector


def shaped(*shape, dtype=single):
    return jax.ShapeDtypeStruct(shape, dtype)


def low(*shape):
    return jax.ShapeDtypeStruct(shape, bfloat)


def low_vm(*shape):
    return pltpu.VMEM(shape, bfloat)


def full_vm(*shape):
    return pltpu.VMEM(shape, single)


def sum_over(value, axis):
    size = lax.axis_size(axis)
    bit = 1
    while bit < size:
        value = value + partner(value, axis, bit)
        bit *= 2
    return value


def adam(weight, gradient, first, second, step_rate, decay_rate):
    first_new = beta_one * first + (1.0 - beta_one) * gradient
    second_new = beta_two * second + (1.0 - beta_two) * gradient * gradient
    first_hat = first_new / (1.0 - beta_one**STEP)
    second_hat = second_new / (1.0 - beta_two**STEP)
    weight_new = weight - step_rate * (
        first_hat / (jnp.sqrt(second_hat) + eps_adam) + decay_rate * weight
    )
    return (weight_new, first_new, second_new)


def on_device(
    stream, cotangent, lengths, owners, master, moment_one, moment_two, vec_master, vec_one, vec_two
):
    narrow_size = lax.axis_size("narrow")
    wide_size = lax.axis_size("wide")
    owner_row = owners[0]
    capacity = master.shape[1]
    half_rows = master.shape[2]
    width = master.shape[3]
    count = owner_row.shape[0]
    counter = jnp.arange(count)
    same = owner_row[:, None] == owner_row[None, :]
    earlier = counter[None, :] < counter[:, None]
    ranks = jnp.sum((same & earlier).astype(jnp.int32), 1)
    on_ring = (wide_size, narrow_size, capacity, count) == (len(RING), 2, 14, 56)
    wide_at, narrow_at = lax.axis_index("wide"), lax.axis_index("narrow")
    self_rows, rest_rows = 4 * width, count * half_rows * narrow_size - 4 * width
    is_source = lax.axis_index("half") == 0
    x = stream[0, 0]
    length = x.shape[0]
    some = length // 2
    source_len, target_len = lengths[0, 0], lengths[1, 0]
    flag = is_source.astype(jnp.int32)
    position = jnp.where(wide_at % 2 == 0, wide_at // 2, wide_size - 1 - wide_at // 2)
    scal = jnp.stack(
        [
            jnp.where(is_source, source_len, target_len),
            1 - flag,
            flag,
            jnp.where(is_source, target_len - some, target_len),
            source_len,
            narrow_at,
            position,
        ]
    ).astype(jnp.int32)
    if on_ring:
        capacity = LEVEL
        own_lead, own_late, plan = lend(position, owner_row.astype(jnp.int32), master[0])

        def make_tables(plan):
            def pick(row, index):
                hit = index[:, None] == jnp.arange(wide_size)[None, :]
                return jnp.sum(jnp.where(hit, row[None, :], 0), 1)

            place = jnp.where(owner_row % 2 == 0, owner_row // 2, wide_size - 1 - owner_row // 2)
            kept, ahead = pick(plan[0], place), pick(plan[1], place)
            moved = (ranks >= kept).astype(jnp.int32) - 2 * (ranks >= kept + ahead).astype(jnp.int32)
            place = (place + moved) % wide_size
            base = pick(plan[0], place)
            below = pick(plan[1], (place - 1) % wide_size)
            slots_there = jnp.where(
                moved == 0,
                ranks,
                jnp.where(moved > 0, base + ranks - kept, base + below + ranks - kept - ahead),
            )
            distance = (place - position) % wide_size
            halves = jnp.arange(narrow_size)[None, :] ^ narrow_at
            table = (distance[:, None] * 2 + halves) * capacity + slots_there[:, None]
            total, late = wide_size * 2 * capacity, capacity - LEAD
            is_late = (slots_there >= LEAD)[:, None]
            after_late = slots_there[:, None] - LEAD + total + LEAD
            far = jnp.where(
                halves == 1,
                jnp.where(is_late, after_late, slots_there[:, None] + total),
                jnp.where(is_late, after_late + late, table),
            )
            table = jnp.where(distance[:, None] == 4, far, table).reshape(-1)
            slot_of = distance * capacity + slots_there
            hit = slot_of[None, :] == jnp.arange(wide_size * capacity)[:, None]
            pieces = jnp.sum(hit.astype(jnp.int32) * (counter + 1)[None, :], 1) - 1
            pieces = pieces.reshape(wide_size, capacity).astype(jnp.int32)
            return pieces, table.astype(jnp.int32), scal

        found, (pieces, table, scal) = ring_gather(own_lead, own_late, plan, make_tables)
    else:
        places = (
            owner_row[:, None] * narrow_size + jnp.arange(narrow_size)[None, :]
        ) * capacity + ranks[:, None]
        table = places.reshape(-1)
        own = master[0].astype(bfloat)
        gathered = lax.all_gather(own, ("wide", "narrow"), axis=0, tiled=True)
        weight = jnp.take(gathered, table, axis=0).reshape(-1, width)
        weight, rest = weight[:self_rows], weight[self_rows:]
    table = table.astype(jnp.int32)
    hidden = (rest_rows - 2 * width) // 2
    self_vec = whole(jnp.where(is_source, vec_master[0:3], vec_master[6:9]))
    cross_vec, ff_vec = whole(vec_master[9:12]), whole(vec_master[12:15])
    memory_vec = whole(vec_master[3:6])
    total = capacity * wide_size * narrow_size
    cuts = [total, LEAD, capacity - LEAD, capacity - LEAD] if on_ring else [total]
    slots = [low(size, half_rows, width) for size in cuts]
    slot_outs = [("hbm", one) for one in slots]

    def stage_of(chunks):
        return [
            low_vm(chunks, 512, width),
            pltpu.SemaphoreType.DMA((chunks * 512 // half_rows,)),
        ]

    def store(*shape, dtype=single):
        return ("store", shaped(*shape, dtype=dtype))

    low_out = partial(store, dtype=bfloat)
    two, four = low_vm(2, length, 128), low_vm(4, length, 128)
    both_halves = [(0, 1), (1, 0)]

    forward_outs = (
        [low_out(length, width)] * 3
        + [low_out(width, length), store(HEADS, length)]
        + [store(length, width)] * 2
        + [("hbm", low(2 * length, width))]
    )
    forward_scratch = [low_vm(width, length), low_vm(width, length), four, low_vm(3 * some, width)]
    if on_ring:
        *forward, weight, rest = call(
            partial(placed_forward_body, [where for where, unused in found]),
            "self_forward",
            scal,
            None,
            [("smem", pieces), whole(x), self_vec] + [("hbm", value) for unused, value in found],
            forward_outs + [low_out(self_rows, width), low_out(rest_rows, width)],
            forward_scratch + [pltpu.SemaphoreType.DMA((2,))],
        )
    else:
        forward = call(
            self_forward_body,
            "self_forward",
            scal,
            None,
            [whole(x), whole(weight), self_vec],
            forward_outs,
            forward_scratch,
        )
    query, key, value, ctx_t, lse, resid, inner, swap = forward
    rest_other = lax.ppermute(rest, "half", both_halves)
    cross_w = part(rest, 0, 2 * width)
    up_w = part(rest, 2 * width, hidden)
    down_w = part(rest, 2 * width + hidden, hidden)
    activ, slope, ff_resid, memory, swap = call(
        encoder_ff_body,
        "encoder_ff",
        scal,
        1,
        [whole(inner), up_w, down_w, cross_w, memory_vec, ("hbm", swap)],
        [low_out(length, hidden)] * 2
        + [store(length, width), low_out(length, width), ("hbm", low(2 * length, width))],
        [low_vm(2 * length, width)],
        [(5, 4)],
    )
    swap_other = lax.ppermute(swap, "half", both_halves)

    def shared(first, rows):
        return either([(rest_other, first, 0, rows)], [(rest, first, 0, rows)])

    mid_inner = either([], [(inner, 0, 0, some)])
    mid_packed = either([(swap_other, 0, 0, 3 * some)], [])
    keys = either([(swap, 0, 0, None)], [(swap_other, 0, 0, None)])
    cotan = cotangent[0]
    output, sendback, grad_one, grad_rest, grad_middle_vec, swap = call(
        middle_body,
        "decoder_middle",
        scal,
        None,
        [
            mid_inner,
            mid_packed,
            keys,
            shared(0, 2 * width),
            cross_vec,
            shared(2 * width, hidden),
            shared(2 * width + hidden, hidden),
            ff_vec,
            either([(cotan, some, 0, some)], [(cotan, 0, 0, some)]),
        ],
        [
            low_out(some, width),
            low_out(2 * length, width),
            store(some, width),
            low_out(rest_rows, width),
            store(6, width),
            ("hbm", low(2 * length, width)),
        ],
        [low_vm(some, width), low_vm(width, some), low_vm(width, some), full_vm(HEADS, some)]
        + [full_vm(some, width), full_vm(some, width), low_vm(some, hidden), low_vm(some, hidden)]
        + [low_vm(some, width), low_vm(some, width), full_vm(some, width)]
        + [low_vm(some, width), low_vm(width, some), full_vm(HEADS, some)]
        + [low_vm(width, length), low_vm(width, length)]
        + [full_vm(length, width), full_vm(length, width), low_vm(width, some), four, two, two]
        + [low_vm(2 * length, width)],
    )
    swap_other = lax.ppermute(swap, "half", both_halves)
    grad_rest, swap_other = lax.optimization_barrier((grad_rest, swap_other))
    grad_rest_other = lax.ppermute(grad_rest, "half", both_halves)
    output = join(output, swap_other[3 * some :])
    grad_inner, grad_memory_vec, *target = call(
        encoder_back_body,
        "encoder_back",
        scal,
        1,
        [
            ("smem", table),
            whole(sendback),
            whole(swap_other),
            whole(memory),
            cross_w,
            whole(inner),
            whole(ff_resid),
            whole(activ),
            whole(slope),
            up_w,
            down_w,
            memory_vec,
        ],
        [store(length, width), store(3, width)] + slot_outs,
        [full_vm(length, width), low_vm(length, width), low_vm(length, width)] + stage_of(10),
    )
    back_scratch = (
        [low_vm(length, width), low_vm(length, width), low_vm(width, length), full_vm(HEADS, length)]
        + [low_vm(width, length), low_vm(width, length)]
        + [full_vm(length, width), full_vm(length, width), low_vm(width, length), two, two]
    )
    grad_x, grad_self_vec, *target = call(
        self_back_body,
        "self_back",
        scal,
        None,
        [
            ("smem", table),
            whole(x),
            part(weight, 0, 3 * width),
            part(weight, 3 * width, width),
            self_vec,
            whole(resid),
            whole(query),
            whole(key),
            whole(value),
            whole(ctx_t),
            whole(lse),
            either(
                [(grad_inner, 0, 0, length)],
                [(grad_one, 0, 0, some)],
            ),
            either([], [(swap_other, 0, 0, 3 * some)]),
        ]
        + [("hbm", one) for one in target],
        [store(length, width), store(3, width)] + slot_outs,
        back_scratch + stage_of(4),
        [(13 + number, 2 + number) for number in range(len(slots))],
    )
    target = call(
        merge_body,
        "merge",
        scal,
        0,
        [
            ("smem", table),
            whole(grad_rest),
            whole(grad_rest_other),
        ]
        + [("hbm", one) for one in target],
        slot_outs,
        stage_of(10),
        [(3 + number, number) for number in range(len(slots))],
    )
    vec_grads = jnp.concatenate(
        [
            jnp.where(is_source, grad_self_vec, 0.0),
            jnp.where(is_source, grad_memory_vec, 0.0),
            jnp.where(is_source, 0.0, grad_self_vec),
            grad_middle_vec,
        ],
        0,
    )
    if on_ring:
        grads = target[0].reshape(wide_size, 2, capacity, half_rows, width)
        mine, vec_grads = ring_scatter(grads, target[1:], vec_grads)
    else:
        mine = lax.psum_scatter(target[0], ("wide", "narrow"), scatter_dimension=0, tiled=True)
        for axis in ("narrow", "wide", "half"):
            vec_grads = sum_over(vec_grads, axis)
    if on_ring:
        sums = join(mine, jnp.zeros((FLOW, half_rows, width), single))
        cut = plan[0][position]
        lent = lax.dynamic_slice_in_dim(sums, cut, FLOW, 0).astype(bfloat)
        cut = cut + plan[1][(position - 1) % wide_size]
        lent_above = lax.dynamic_slice_in_dim(sums, cut, FLOW, 0).astype(bfloat)
        above, below = round_ring(lent, -1), round_ring(lent_above, 1)
        states = (master[0], moment_one[0], moment_two[0])
        state = states[0].shape
        results = call(
            adam_kept_body,
            "adam_kept",
            scal,
            None,
            [("smem", plan), whole(mine)] + [whole(one) for one in states],
            [store(*state)] * 3 + [low_out(*state)],
            [],
        )
        new_first, new_second, new_weight, new_copy = call(
            adam_lent_body,
            "adam_lent",
            scal,
            None,
            [("smem", plan), ("hbm", below), ("hbm", above)]
            + [("hbm", one) for one in states]
            + [("hbm", one) for one in results],
            [("hbm", shaped(*state))] * 3 + [("hbm", low(*state))],
            [
                full_vm(3, *state),
                low_vm(*state),
                full_vm(3, *state),
                low_vm(*state),
                pltpu.SemaphoreType.DMA((4, state[0])),
                pltpu.SemaphoreType.DMA((4, state[0])),
            ],
            [(6 + number, number) for number in range(4)],
        )
    else:
        used = jnp.sum((owner_row == wide_at).astype(jnp.int32))
        mine = jnp.where((jnp.arange(capacity) < used)[:, None, None], mine.astype(single), 0.0)
        new_weight, new_first, new_second = adam(
            master[0], mine, moment_one[0], moment_two[0], rate_matrix, decay_matrix
        )
        new_copy = new_weight.astype(bfloat)
    memory, output, vec_grads = lax.optimization_barrier((memory, output, vec_grads))
    vec_weight, vec_first, vec_second = adam(
        vec_master, vec_grads, vec_one, vec_two, rate_vector, 0.0
    )
    return (
        jnp.where(is_source, memory, output)[None, None],
        grad_x[None, None],
        new_first[None],
        new_second[None],
        new_weight[None],
        new_copy[None],
        vec_first,
        vec_second,
        vec_weight,
    )


def solution(mesh):
    in_specs = (
        P("half", ("wide", "narrow"), None, None),
        P(("wide", "narrow"), None, None),
        P(None, ("wide", "narrow")),
        P("half", None),
        P("half", "wide", "narrow", None),
        P("half", "wide", "narrow", None),
        P("half", "wide", "narrow", None),
        P(),
        P(),
        P(),
    )
    out_specs = (
        P("half", ("wide", "narrow"), None, None),
        P("half", ("wide", "narrow"), None, None),
        P("half", "wide", "narrow", None),
        P("half", "wide", "narrow", None),
        P("half", "wide", "narrow", None),
        P("half", "wide", "narrow", None),
        P(),
        P(),
        P(),
    )
    return jax.shard_map(
        on_device, mesh=mesh, in_specs=in_specs, out_specs=out_specs, check_vma=False
    )
```
